32 devices in a mesh: dp: 8 (over y, x, core), rep: 4 (over z).
Axes of the slice: x: 2, y: 2, z: 4, core: 2. Of those that a mesh axis runs over, the one named last changes fastest.
Arguments:
- features: bfloat16 [6144, 768], P(('dp', 'rep')), may hold values from -6 to 6
- tile_records: float32 [6144, 128], P(('dp', 'rep')), may hold values from -6 to 6
- patch_counts: int32 [8], P('dp'), may hold values from 384 to 768, as said below
- lead_counts: int32 [8], P('dp'), may hold values from 1 to 8
- attn_master: float32 [8, 768, 768], P('rep', 'dp')
- attn_momentum: float32 [8, 768, 768], P('rep', 'dp'), may hold values from -0.001953125 to 0.001953125
- mlp_master: float32 [4, 3072, 768], P('rep', 'dp')
- mlp_momentum: float32 [4, 3072, 768], P('rep', 'dp'), may hold values from -0.001953125 to 0.001953125
- vectors: float32 [32384], replicated
- vec_momentum: float32 [32384], replicated, may hold values from -0.005859375 to 0.005859375
- head_master: float32 [768, 128], replicated, may hold values from -0.21875 to 0.21875
- head_momentum: float32 [768, 128], replicated, may hold values from -0.00390625 to 0.00390625
Outputs:
- prediction: float32 [6144, 32], P(('dp', 'rep'))
- features_grad: float32 [6144, 768], P(('dp', 'rep'))
- penalty: float32 [], replicated
- attn_moment_new: float32 [8, 768, 768], P('rep', 'dp')
- attn_new: float32 [8, 768, 768], P('rep', 'dp')
- mlp_moment_new: float32 [4, 3072, 768], P('rep', 'dp')
- mlp_new: float32 [4, 3072, 768], P('rep', 'dp')
- vec_moment_new: float32 [32384], replicated
- vec_new: float32 [32384], replicated
- head_moment_new: float32 [768, 128], replicated
- head_new: float32 [768, 128], replicated
The draws below stay inside these ranges and needn't reach their ends.
Inputs may be any that keep to these rules, and one draw needn't show every extreme that they name: `patch_counts`: every frame holds either 768 or 384 valid patches, always its first ones; some frame holds 768.
All inputs are finite; a program needn't handle non-finite values.
Results may differ from the reference program's by a relative error of at most 0.0095.
The reference program's roundings to bfloat16 on the way count: a program that leaves them out, or rounds other values in their place, can miss the bound.
Values may be sent and summed in bfloat16 or wider, within the bound.
No kernel may reach another device: no remote copies, remote signals or barrier semaphores. Data moves between devices by JAX's collectives and lax.ppermute only.
A program may use at most 256 MiB of HBM per device.

```python
import jax
import jax.numpy as jnp
from jax import lax

D = 768
HEADS = 12
HDIM = 64
FF = 3072
LAYERS = 2
MODEL_NUMBER = 3
TILE_CELLS = 32
NLEAD = 8
NS_STEPS = 2
TILE_PLACES = 768
FRAMES = 8
TOKENS = 6144
HEAD_OUT = 128
VECTORS = 32384


def draw_patch_counts(key, part):
    key = jax.random.fold_in(key, 11)
    first_key, second_key = jax.random.split(key)
    coins = jax.random.randint(first_key, (FRAMES,), 0, 8)
    chosen = jax.random.randint(second_key, (), 0, FRAMES)
    longer = (coins < 5) | (jnp.arange(FRAMES) == chosen)
    return jnp.where(longer, TILE_PLACES, TILE_PLACES // 2).astype(jnp.int32)


def draw_lead_counts(key, part):
    key = jax.random.fold_in(key, 12)
    index_range = jnp.arange(FRAMES)
    rising = (NLEAD - 1) * index_range // (FRAMES - 1)
    jitter = jax.random.randint(key, (FRAMES,), 0, 2)
    return jnp.minimum(rising + 1 + jitter, NLEAD).astype(jnp.int32)


def draw_attn_master(key, part):
    key = jax.random.fold_in(key, 21)
    noise_draw = jax.random.normal(key, (4 * LAYERS, D, D), jnp.float32)
    kinds = jnp.arange(4 * LAYERS) % 4
    spread = jnp.where(kinds == 3, 4.0, 1.0) * D ** (-0.5)
    return noise_draw * spread[:, None, None]


def draw_mlp_master(key, part):
    key = jax.random.fold_in(key, 22)
    noise_draw = jax.random.normal(key, (2 * LAYERS, FF, D), jnp.float32)
    kinds = jnp.arange(2 * LAYERS) % 2
    spread = jnp.where(kinds == 0, D ** (-0.5), FF ** (-0.5))
    return noise_draw * spread[:, None, None]


def draw_vectors(key, part):
    key = jax.random.fold_in(key, 31)
    noise_draw = jnp.clip(jax.random.normal(key, (VECTORS,), jnp.float32), -3.0, 3.0)
    layout = []
    for layer_index in range(LAYERS):
        layout += [(D, 1.0, 0.2), (D, 0.0, 0.2), (D, 0.0, 0.2), (D, 0.0, 0.2), (D, 0.0, 0.2), (D, 1.0, 0.2), (D, 0.0, 0.2), (D, 0.0, 0.2), (FF, 0.0, 0.2), (NLEAD * D, 0.0, 0.5)]
    layout += [(D, 1.0, 0.2), (D, 0.0, 0.2), (HEAD_OUT, 0.0, 0.3)]
    centre = jnp.concatenate([jnp.full((width,), middle, jnp.float32) for width, middle, spread in layout])
    scales = jnp.concatenate([jnp.full((width,), spread, jnp.float32) for width, middle, spread in layout])
    return centre + scales * noise_draw


def levels(own_key, shape, cuts, low, largest):
    factor_of, own = 1.0, jax.random.fold_in(own_key, 6)
    for axis_at, parts in cuts:
        heights = jnp.exp(jax.random.uniform(jax.random.fold_in(own, axis_at), (parts,), jnp.float32, low / len(cuts), largest / len(cuts)))
        factor_of = factor_of * jnp.repeat(heights, shape[axis_at] // parts).reshape([-1 if axis == axis_at else 1 for axis in range(len(shape))])
    return factor_of


def scatter_about(rng, dims, deviation, reach, cuts=(), dtype=jnp.bfloat16):
    level = levels(rng, dims, cuts, -0.22, 0.18) if cuts else 1.0
    entries = jax.random.normal(rng, dims, jnp.float32) * deviation * level
    return jnp.minimum(jnp.maximum(entries, -reach), reach).astype(dtype)


def setup_inputs(seed: int = 0) -> dict:
    seeds = jax.random.split(jax.random.key(seed), 13)
    return {
        "features": scatter_about(seeds[0], (TOKENS, D), 1.0, 6.0, ((0, 32),)),
        "tile_records": scatter_about(seeds[1], (TOKENS, HEAD_OUT), 1.0, 6.0, ((0, 32),), jnp.float32),
        "patch_counts": draw_patch_counts(jax.random.fold_in(seeds[12], 71), 0),
        "lead_counts": draw_lead_counts(jax.random.fold_in(seeds[12], 71), 0),
        "attn_master": draw_attn_master(jax.random.fold_in(seeds[12], 71), 0),
        "attn_momentum": scatter_about(seeds[5], (4 * LAYERS, D, D), (0.01 * TOKENS ** -0.5), 0.001953125, ((0, 4), (1, 8)), jnp.float32),
        "mlp_master": draw_mlp_master(jax.random.fold_in(seeds[12], 71), 0),
        "mlp_momentum": scatter_about(seeds[7], (2 * LAYERS, FF, D), (0.01 * TOKENS ** -0.5), 0.001953125, ((0, 4), (1, 8)), jnp.float32),
        "vectors": draw_vectors(jax.random.fold_in(seeds[12], 71), 0),
        "vec_momentum": scatter_about(seeds[9], (VECTORS,), (0.03 * TOKENS ** -0.5), 0.005859375, (), jnp.float32),
        "head_master": scatter_about(seeds[10], (D, HEAD_OUT), D ** -0.5, 0.21875, (), jnp.float32),
        "head_momentum": scatter_about(seeds[11], (D, HEAD_OUT), (0.02 * TOKENS ** -0.5), 0.00390625, (), jnp.float32),
    }


EPS = 1e-05
NEG = -1e+30
MOMENTUM = 0.95
COEF_A = 3.4445
COEF_B = -4.775
COEF_C = 2.0315
PENALTY = 0.5
VEC_RATE = 1000.0
HEAD_RATE = 300.0
DECAY = 0.01
ATTN_RATES = (1.0, 1.0, 1.0, 4.0)
MLP_RATES = (2.0, 1.0)
HIGH = lax.Precision.HIGHEST

@jax.custom_vjp
def low(v):
    return lax.optimization_barrier(v.astype(jnp.bfloat16)).astype(jnp.float32)

@jax.custom_vjp
def low_back(v):
    return v

def low_keep(v):
    return (low(v), None)

def low_pass(kept, grad):
    return (grad,)

def back_keep(v):
    return (v, None)

def back_low(kept, grad):
    return (low(grad),)
low.defvjp(low_keep, low_pass)
low_back.defvjp(back_keep, back_low)

def layer_fields(vec_weights, layer_index):
    stride = 8 * D + FF + NLEAD * D
    offset = layer_index * stride
    pieces = [vec_weights[offset + slot * D:offset + (slot + 1) * D] for slot in range(8)]
    up_bias = vec_weights[offset + 8 * D:offset + 8 * D + FF]
    lead_table = vec_weights[offset + 8 * D + FF:offset + stride].reshape(NLEAD, D)
    return pieces + [up_bias, lead_table]

def tail_fields(vec_weights):
    offset = LAYERS * (8 * D + FF + NLEAD * D)
    return (vec_weights[offset:offset + D], vec_weights[offset + D:offset + 2 * D], vec_weights[offset + 2 * D:offset + 2 * D + HEAD_OUT])

def layer_norm(hidden, gain, shift):
    centred = hidden - lax.optimization_barrier(jnp.mean(hidden, -1, keepdims=True))
    variance = lax.optimization_barrier(jnp.mean(centred * centred, -1, keepdims=True))
    return centred * lax.rsqrt(variance + EPS) * gain + shift

def frame_terms(weights, frame_rows, snapshot_grid_entries, frame_count, lead_value, pixel_total):
    attn_w, mlp_w, vec_w, head_w = weights
    valid = (jnp.arange(TILE_PLACES) < frame_count).astype(jnp.float32)
    row_weight = valid * lead_value.astype(jnp.float32)
    hidden = frame_rows
    for layer_index in range(LAYERS):
        gain_one, bias_one, query_bias, value_bias, output_bias, gain_two, bias_two, down_bias, up_bias, lead_table = layer_fields(vec_w, layer_index)
        lead_embed = lead_table[lead_value - 1]
        mixed_in = low(layer_norm(hidden, gain_one, bias_one) + lead_embed)
        queries = low(low_back(jnp.dot(mixed_in, attn_w[4 * layer_index], precision=HIGH) + query_bias))
        keys_all = low(low_back(jnp.dot(mixed_in, attn_w[4 * layer_index + 1], precision=HIGH)))
        values_all = low(low_back(jnp.dot(mixed_in, attn_w[4 * layer_index + 2], precision=HIGH) + value_bias))
        queries = queries.reshape(TILE_PLACES, HEADS, HDIM)
        keys_all = keys_all.reshape(TILE_PLACES, HEADS, HDIM)
        values_all = values_all.reshape(TILE_PLACES, HEADS, HDIM)
        scores = jnp.einsum('qhd,khd->hqk', queries, keys_all, precision=HIGH) * HDIM ** (-0.5)
        scores = low_back(jnp.where(valid[None, None, :] > 0, scores, NEG))
        attn_probs = low(jax.nn.softmax(scores, axis=-1))
        attended = jnp.einsum('hqk,khd->qhd', attn_probs, values_all, precision=HIGH).reshape(TILE_PLACES, D)
        attended = low(low_back(attended))
        hidden_mid = hidden + low_back(jnp.dot(attended, attn_w[4 * layer_index + 3], precision=HIGH) + output_bias)
        mlp_in = low(layer_norm(hidden_mid, gain_two, bias_two))
        pre_act = low_back(jnp.dot(mlp_in, mlp_w[2 * layer_index].T, precision=HIGH) + up_bias)
        activated = low(jax.nn.gelu(pre_act, approximate=True))
        hidden = hidden_mid + low_back(jnp.dot(activated, mlp_w[2 * layer_index + 1], precision=HIGH) + down_bias)
    final_gain, final_bias, head_bias = tail_fields(vec_w)
    final_in = low(layer_norm(hidden, final_gain, final_bias))
    head_out = low_back(jnp.dot(final_in, head_w, precision=HIGH) + head_bias)
    logits = head_out[:, :MODEL_NUMBER * TILE_CELLS].reshape(TILE_PLACES, MODEL_NUMBER, TILE_CELLS)
    magnitude_adjustment = head_out[:, MODEL_NUMBER * TILE_CELLS:]
    log_gate = jax.nn.log_softmax(logits, axis=1)
    mixing_share_lines = jnp.exp(log_gate)
    member_outlooks = snapshot_grid_entries[:, :MODEL_NUMBER * TILE_CELLS].reshape(TILE_PLACES, MODEL_NUMBER, TILE_CELLS)
    observed = snapshot_grid_entries[:, MODEL_NUMBER * TILE_CELLS:]
    estimated_grids = lax.optimization_barrier(jnp.sum(mixing_share_lines * member_outlooks, 1)) + magnitude_adjustment
    pred_error = estimated_grids - observed
    fitted = jnp.sum(row_weight[:, None] * pred_error * pred_error)
    negent = jnp.sum(row_weight[:, None, None] * mixing_share_lines * log_gate)
    frame_value = (0.5 * fitted + PENALTY * negent) / pixel_total
    return (frame_value, estimated_grids * valid[:, None], negent)

def orthogonalize(update):
    gram = jnp.dot(update.T, update, precision=HIGH)
    state = update / (jnp.sqrt(jnp.trace(gram)) + 1e-07)
    for step_index in range(NS_STEPS):
        gram = jnp.dot(state.T, state, precision=HIGH)
        product = jnp.dot(state, gram, precision=HIGH)
        state = COEF_A * state + COEF_B * product + COEF_C * jnp.dot(product, gram, precision=HIGH)
    return state

def muon_update(master, momentum, grad, rates):
    moment = MOMENTUM * momentum + grad
    update = grad + MOMENTUM * moment
    ortho = jnp.stack([orthogonalize(update[index]) for index in range(master.shape[0])])
    rate = jnp.array(rates * (master.shape[0] // len(rates)), jnp.float32)[:, None, None]
    return (moment, master * (1.0 - rate * DECAY) - rate * ortho)

def reference(features, tile_records, patch_counts, lead_counts, attn_master, attn_momentum, mlp_master, mlp_momentum, vectors, vec_momentum, head_master, head_momentum):
    pixel_total = (TILE_CELLS * jnp.sum(patch_counts * lead_counts)).astype(jnp.float32)
    frame_fn = jax.checkpoint(frame_terms)

    def objective_of(weights, inputs):

        def one_frame(running, frame_item):
            rows_in, fields_in, frame_count, lead_value = frame_item
            frame_value, estimated_grids, negent = frame_fn(weights, rows_in, fields_in, frame_count, lead_value, pixel_total)
            return (running + frame_value, (estimated_grids, negent))
        stacked = (inputs.reshape(FRAMES, TILE_PLACES, D), tile_records.reshape(FRAMES, TILE_PLACES, HEAD_OUT), patch_counts, lead_counts)
        running, (estimated_grids, negents) = lax.scan(one_frame, jnp.zeros((), jnp.float32), stacked)
        return (running, (estimated_grids.reshape(TOKENS, TILE_CELLS), jnp.sum(negents)))
    weights = (low(attn_master), low(mlp_master), vectors, low(head_master))
    objective, backward, (prediction, negent) = jax.vjp(objective_of, weights, features.astype(jnp.float32), has_aux=True)
    grads, features_grad = backward(jnp.ones_like(objective))
    attn_grad, mlp_grad, vec_grad, head_grad = grads
    attn_moment, attn_new = muon_update(attn_master, attn_momentum, attn_grad, ATTN_RATES)
    mlp_moment, mlp_new = muon_update(mlp_master, mlp_momentum, mlp_grad, MLP_RATES)
    vec_moment = MOMENTUM * vec_momentum + vec_grad
    vec_new = vectors - VEC_RATE * vec_moment
    head_moment = MOMENTUM * head_momentum + head_grad
    head_new = head_master - HEAD_RATE * head_moment
    penalty = negent / pixel_total
    return (prediction, features_grad, penalty, attn_moment, attn_new, mlp_moment, mlp_new, vec_moment, vec_new, head_moment, head_new)
```

```python
import jax
import jax.numpy as jnp
from jax import lax
from jax.experimental import pallas as pl
from jax.experimental.pallas import tpu as pltpu
from jax.sharding import PartitionSpec as P

D = 768
HEADS = 12
HDIM = 64
FF = 3072
LAYERS = 2
MODEL_NUMBER = 3
TILE_CELLS = 32
NLEAD = 8
NS_STEPS = 2


EPS = 1e-05
NEG = -1e30
MOMENTUM = 0.95
COEF_A = 3.4445
COEF_B = -4.775
COEF_C = 2.0315
PENALTY = 0.5
VEC_RATE = 1000.0
HEAD_RATE = 300.0
DECAY = 0.01
ATTN_RATES = (1.0, 1.0, 1.0, 4.0)
MLP_RATES = (2.0, 1.0)
HIGH = lax.Precision.HIGHEST


def layer_fields(vec_weights, layer_index):
    stride = 8 * D + FF + NLEAD * D
    offset = layer_index * stride
    pieces = [vec_weights[offset + slot * D : offset + (slot + 1) * D] for slot in range(8)]
    up_bias = vec_weights[offset + 8 * D : offset + 8 * D + FF]
    lead_table = vec_weights[offset + 8 * D + FF : offset + stride].reshape(NLEAD, D)
    return pieces + [up_bias, lead_table]


def tail_fields(vec_weights):
    offset = LAYERS * (8 * D + FF + NLEAD * D)
    return (
        vec_weights[offset : offset + D],
        vec_weights[offset + D : offset + 2 * D],
        vec_weights[offset + 2 * D : offset + 2 * D + (MODEL_NUMBER + 1) * TILE_CELLS],
    )


def norm_parts(hidden):
    centred = hidden - jnp.mean(hidden, -1, keepdims=True)
    variance = jnp.mean(centred * centred, -1, keepdims=True)
    inverse = lax.rsqrt(variance + EPS)
    return (centred * inverse, inverse)


def norm_back(grad_out, normed, inverse, gain):
    scaled = grad_out * gain
    mean_one = jnp.mean(scaled, -1, keepdims=True)
    mean_two = jnp.mean(scaled * normed, -1, keepdims=True)
    grad_in = inverse * (scaled - mean_one - normed * mean_two)
    return (grad_in, jnp.sum(grad_out * normed, 0), jnp.sum(grad_out, 0))


def gelu_tanh(values):
    return jax.nn.gelu(values, approximate=True)


def masked_scores(queries, keys_all, key_valid):
    scores = jnp.einsum("qhd,khd->hqk", queries, keys_all, preferred_element_type=jnp.float32)
    scores = scores * queries.shape[-1] ** (-0.5)
    return jnp.where(key_valid[None, None, :], scores, NEG)


def swap_dp(value, bit):
    size = lax.axis_size("dp")
    return lax.ppermute(value, "dp", [(i, i ^ (1 << bit)) for i in range(size)])


def swap_rep(value, mask):
    size = lax.axis_size("rep")
    return lax.ppermute(value, "rep", [(i, i ^ mask) for i in range(size)])


def link_bits():
    count = lax.axis_size("dp").bit_length() - 1
    return (list(range(1, count)), list(range(count - 1, 0, -1)))


def path_ids(order):
    ids = [0]
    for bit in order:
        ids = ids + [i | (1 << bit) for i in ids]
    return ids


def gather_path(value, order, axis):
    for bit in order:
        value = jnp.concatenate([value, swap_dp(value, bit)], axis)
    return value


def scatter_path(value, order, axis):
    for bit in reversed(order):
        half = value.shape[axis] // 2
        keep = lax.slice_in_dim(value, 0, half, axis=axis)
        send = lax.slice_in_dim(value, half, 2 * half, axis=axis)
        value = (keep.astype(jnp.float32) + swap_dp(send, bit).astype(jnp.float32)).astype(
            jnp.bfloat16
        )
    return value


def spread_rep(own):
    rep = lax.axis_index("rep")
    far = swap_rep(own, 2)
    near = swap_rep(jnp.stack([own, far]), 1)
    all_four = jnp.stack([own, near[0], far, near[1]])
    return [
        lax.dynamic_index_in_dim(all_four, rep ^ i, 0, keepdims=False) for i in range(4)
    ]


def own_rep(pair, layer_index):
    rep = lax.axis_index("rep")
    low = rep & 1
    keep = lax.dynamic_index_in_dim(pair, low, 0, keepdims=False)
    send = lax.dynamic_index_in_dim(pair, 1 - low, 0, keepdims=False)
    part = keep.astype(jnp.float32) + swap_rep(send, 1).astype(jnp.float32)
    first = 2 * layer_index
    moves = [(i, i ^ 2) for i in range(4) if i // 2 != layer_index]
    return part + lax.ppermute(part.astype(jnp.bfloat16), "rep", moves).astype(jnp.float32)


def sum_all(flat):
    core = lax.axis_index("dp") & 1
    size = flat.shape[0]
    width = -(-size // 2048) * 1024
    halves = jnp.pad(flat, (0, 2 * width - size)).reshape(2, width // 128, 128)
    mine = lax.dynamic_index_in_dim(halves, core, 0, keepdims=False)
    other = lax.dynamic_index_in_dim(halves, 1 - core, 0, keepdims=False)
    total = mine + swap_dp(other, 0)
    for bit in link_bits()[0]:
        total = total + swap_dp(total, bit)
    total = total + swap_rep(total, 1)
    total = total + swap_rep(total, 2)
    other = swap_dp(total, 0)
    whole = jnp.where(
        core == 0, jnp.stack([total, other]), jnp.stack([other, total])
    )
    return whole.reshape(-1)[:size]


def place_kernel(order_ref, own_ref, other_ref, out_ref):
    step = pl.program_id(1)
    out_ref[...] = lax.cond(
        order_ref[1, step] == 0, lambda: own_ref[...], lambda: other_ref[...]
    )


def place(own, other, order):
    blocks, mats, rows, width = own.shape
    me = lax.axis_index("dp")
    size = 2 * blocks
    ids = path_ids(order)
    slot = [0] * size
    for at, i in enumerate(ids):
        slot[i] = slot[i | 1] = at
    wanted = jnp.arange(size) ^ me
    table = jnp.stack([jnp.asarray(slot, jnp.int32)[wanted], wanted & 1]).astype(jnp.int32)
    spec = pl.BlockSpec((1, 1, rows, width), lambda m, i, t: (t[0, i], m, 0, 0))
    out = pl.pallas_call(
        place_kernel,
        grid_spec=pltpu.PrefetchScalarGridSpec(
            num_scalar_prefetch=1,
            grid=(mats, size),
            in_specs=[spec, spec],
            out_specs=pl.BlockSpec((1, 1, rows, width), lambda m, i, t: (m, i, 0, 0)),
        ),
        out_shape=jax.ShapeDtypeStruct((mats, size, rows, width), own.dtype),
    )(table, own, other)
    return out.reshape(mats, size * rows, width)


def core_columns(value, blocks, which):
    rows, width = value.shape
    split = value.reshape(rows, blocks // 2, 2, width // blocks)
    return lax.dynamic_index_in_dim(split, which, 2, keepdims=False).reshape(rows, width // 2)


def dot32(spec, left, right):
    return jnp.einsum(spec, left, right, preferred_element_type=jnp.float32)


def low_dot(spec, left, right):
    return dot32(spec, left.astype(jnp.bfloat16), right.astype(jnp.bfloat16))


def orthogonal(state, gram):
    factor = 1.0 / (jnp.sqrt(jnp.trace(gram)) + 1e-07)
    state = state * factor
    gram = gram * (factor * factor)
    square = low_dot("ij,jk->ik", gram, gram)
    mix = COEF_B * gram + COEF_C * square
    state = COEF_A * state + low_dot("ri,ij->rj", state, mix)
    cross = low_dot("ij,jk->ik", mix, gram)
    gram = COEF_A * COEF_A * gram + 2.0 * COEF_A * cross + low_dot("ij,jk->ik", mix, cross)
    square = low_dot("ij,jk->ik", gram, gram)
    mix = COEF_B * gram + COEF_C * square
    return COEF_A * state + low_dot("ri,ij->rj", state, mix)


def gather_rows(value):
    half = value.shape[0] // 2
    low = value.astype(jnp.bfloat16)
    paths = link_bits()
    parts = [
        gather_path(low[:half], paths[0], 0),
        gather_path(low[half:], paths[1], 0),
    ]
    return jnp.concatenate(parts + [swap_dp(part, 0) for part in parts], 0)


def local(
    features,
    tile_records,
    patch_counts,
    lead_counts,
    attn_master,
    attn_momentum,
    mlp_master,
    mlp_momentum,
    vectors,
    vec_momentum,
    head_master,
    head_momentum,
):
    rep_size = lax.axis_size("rep")
    dp_size = lax.axis_size("dp")
    me = lax.axis_index("dp")
    core = me & 1
    rep = lax.axis_index("rep")
    rep_low = rep & 1
    rep_high = rep >> 1
    total_row_count = features.shape[0]
    seq_len = total_row_count * rep_size
    attn_rows = attn_master.shape[1]
    mlp_rows = mlp_master.shape[1]
    half_rows = mlp_rows // 2
    links = dp_size // 2
    path_a, path_b = link_bits()

    moves = []
    for d in range(dp_size):
        for r in range(rep_size):
            to = (d - d % 2 + r // 2) * rep_size + (d % 2) * 2 + r % 2
            moves.append((d * rep_size + r, to))

    def exchange_frames(value):
        return lax.ppermute(value, ("dp", "rep"), moves)

    features = exchange_frames(features)
    tile_records = exchange_frames(tile_records)

    counts = jnp.concatenate([patch_counts, lead_counts]).reshape(1, 2)
    counts = jnp.concatenate([counts, swap_dp(counts, 0)], 0)
    frame_count, lead_value = lax.dynamic_index_in_dim(
        counts, core ^ rep_high, 0, keepdims=False
    )
    counts = gather_path(counts, path_a, 0)
    pixel_total = (TILE_CELLS * jnp.sum(counts[:, 0] * counts[:, 1])).astype(jnp.float32)

    attn_by_rep = spread_rep(attn_master.astype(jnp.bfloat16))
    mlp_by_rep = spread_rep(mlp_master[0].astype(jnp.bfloat16))

    def attn_weights(layer_index):
        own_a = gather_path(attn_by_rep[2 * layer_index][None], path_a, 0)
        own_b = gather_path(attn_by_rep[2 * layer_index + 1][None], path_b, 0)
        first = place(own_a, swap_dp(own_a, 0), path_a)
        second = place(own_b, swap_dp(own_b, 0), path_b)
        return first[0], first[1], second[0], second[1]

    def mlp_weights(layer_index):
        pair = jnp.stack([mlp_by_rep[2 * layer_index], mlp_by_rep[2 * layer_index + 1]])[None]
        own_a = gather_path(pair[:, :, :half_rows], path_a, 0)
        own_b = gather_path(pair[:, :, half_rows:], path_b, 0)
        parts = [own_a, own_b, swap_dp(own_a, 0), swap_dp(own_b, 0)]
        return [
            jnp.concatenate([part[:, m].reshape(-1, D) for part in parts], 0) for m in range(2)
        ]

    ids_a, ids_b = path_ids(path_a), path_ids(path_b)
    unit_from = [[(i | c, p) for p, ids in enumerate((ids_a, ids_b)) for i in ids] for c in (0, 1)]
    unit_from = unit_from[0] + unit_from[1]
    from_dp = jnp.asarray([i for i, _ in unit_from], jnp.int32) ^ me
    from_path = jnp.asarray([p for _, p in unit_from], jnp.int32)
    unit_take = 2 * from_dp + from_path
    at = {key: n for n, key in enumerate(unit_from)}
    slot_table = jnp.asarray([[at[(i, p)] for p in (0, 1)] for i in range(dp_size)], jnp.int32)
    unit_back = slot_table[jnp.arange(dp_size) ^ me].reshape(-1)

    head_low = head_master.astype(jnp.bfloat16)
    quarter = 2 * core + rep_low
    row_ids = quarter * total_row_count + jnp.arange(total_row_count)
    row_valid = (row_ids < frame_count).astype(jnp.float32)
    key_quarter = quarter ^ jnp.arange(rep_size)
    key_ids = (key_quarter[:, None] * total_row_count + jnp.arange(total_row_count)).reshape(-1)
    key_valid = key_ids < frame_count
    row_weight = row_valid * lead_value.astype(jnp.float32)
    lead_hot = (jnp.arange(NLEAD) == lead_value - 1).astype(jnp.float32)
    hidden = features.astype(jnp.float32)
    saved = []
    for layer_index in range(LAYERS):
        (
            gain_one,
            bias_one,
            query_bias,
            value_bias,
            output_bias,
            gain_two,
            bias_two,
            down_bias,
            up_bias,
            lead_table,
        ) = layer_fields(vectors, layer_index)
        w_query, w_key, w_value, w_output = attn_weights(layer_index)
        w_up, w_down = mlp_weights(layer_index)
        up_bias = up_bias.reshape(2 * dp_size, half_rows)[unit_take].reshape(FF)
        lead_embed = lax.dynamic_index_in_dim(lead_table, lead_value - 1, 0, keepdims=False)
        normed_one, inverse_one = norm_parts(hidden)
        mixed_in = (normed_one * gain_one + bias_one + lead_embed).astype(jnp.bfloat16)
        queries = (dot32("rd,de->re", mixed_in, w_query) + query_bias).astype(jnp.bfloat16)
        keys_local = dot32("rd,de->re", mixed_in, w_key).astype(jnp.bfloat16)
        values_local = (dot32("rd,de->re", mixed_in, w_value) + value_bias).astype(jnp.bfloat16)
        pair = jnp.concatenate([keys_local, values_local], 1)
        pair = jnp.concatenate([pair, swap_rep(pair, 1)], 0)
        pair = jnp.concatenate([pair, swap_dp(pair, 0)], 0)
        key_heads = pair[:, :D].reshape(seq_len, HEADS, HDIM)
        value_heads = pair[:, D:].reshape(seq_len, HEADS, HDIM)
        query_heads = queries.reshape(total_row_count, HEADS, HDIM)
        scores = masked_scores(query_heads, key_heads, key_valid)
        score_top = jnp.max(scores, -1, keepdims=True)
        expo = jnp.exp(scores - score_top)
        exp_total = jnp.sum(expo, -1, keepdims=True)
        attn_probs = (expo / exp_total).astype(jnp.bfloat16)
        log_total = score_top + jnp.log(exp_total)
        attended = (
            dot32("hqk,khd->qhd", attn_probs, value_heads)
            .reshape(total_row_count, D)
            .astype(jnp.bfloat16)
        )
        hidden_mid = hidden + dot32("rd,de->re", attended, w_output) + output_bias
        normed_two, inverse_two = norm_parts(hidden_mid)
        mlp_in = (normed_two * gain_two + bias_two).astype(jnp.bfloat16)
        pre_act = dot32("rd,fd->rf", mlp_in, w_up) + up_bias
        activated = gelu_tanh(pre_act).astype(jnp.bfloat16)
        saved.append(
            (
                normed_one,
                inverse_one,
                mixed_in,
                query_heads,
                key_heads,
                value_heads,
                log_total,
                attended,
                normed_two,
                inverse_two,
                mlp_in,
                pre_act,
                activated,
                (w_query, w_key, w_value, w_output, w_up, w_down),
            )
        )
        hidden = hidden_mid + dot32("rf,fd->rd", activated, w_down) + down_bias
    final_gain, final_bias, head_bias = tail_fields(vectors)
    normed_final, inverse_final = norm_parts(hidden)
    final_in = (normed_final * final_gain + final_bias).astype(jnp.bfloat16)
    head_out = jnp.dot(final_in, head_low, preferred_element_type=jnp.float32) + head_bias
    logits = [head_out[:, e * TILE_CELLS : (e + 1) * TILE_CELLS] for e in range(MODEL_NUMBER)]
    magnitude_adjustment = head_out[:, MODEL_NUMBER * TILE_CELLS :]
    members = [tile_records[:, e * TILE_CELLS : (e + 1) * TILE_CELLS] for e in range(MODEL_NUMBER)]
    observed = tile_records[:, MODEL_NUMBER * TILE_CELLS :]
    top = jnp.maximum(jnp.maximum(logits[0], logits[1]), logits[2])
    shifted = [value - top for value in logits]
    log_sum = jnp.log(sum(jnp.exp(value) for value in shifted))
    log_gate = [value - log_sum for value in shifted]
    gate = [jnp.exp(value) for value in log_gate]
    mixed_outlook = sum(g * m for g, m in zip(gate, members))
    estimated_grids = mixed_outlook + magnitude_adjustment
    pred_error = estimated_grids - observed
    entropy_rows = sum(g * v for g, v in zip(gate, log_gate))
    negent_local = jnp.sum(row_weight[:, None] * entropy_rows)
    learned_multiplier = row_weight[:, None] * pred_error / pixel_total
    ent_scale = PENALTY * row_weight[:, None] / pixel_total
    grad_logits = [
        g * (learned_multiplier * (m - mixed_outlook) + ent_scale * (v - entropy_rows))
        for g, m, v in zip(gate, members, log_gate)
    ]
    grad_head = jnp.concatenate(grad_logits + [learned_multiplier], 1).astype(jnp.bfloat16)
    prediction = exchange_frames(estimated_grids * row_valid[:, None])
    head_grad = dot32("rd,rc->dc", final_in, grad_head)
    head_bias_grad = jnp.sum(grad_head.astype(jnp.float32), 0)
    grad_final = dot32("rc,dc->rd", grad_head, head_low)
    grad_hidden, final_gain_grad, final_bias_grad = norm_back(
        grad_final, normed_final, inverse_final, final_gain
    )
    attn_shares = [None] * LAYERS
    mlp_shares = [None] * LAYERS
    layer_grads = [None] * LAYERS
    early = None
    for layer_index in reversed(range(LAYERS)):
        (
            normed_one,
            inverse_one,
            mixed_in,
            query_heads,
            key_heads,
            value_heads,
            log_total,
            attended,
            normed_two,
            inverse_two,
            mlp_in,
            pre_act,
            activated,
            (w_query, w_key, w_value, w_output, w_up, w_down),
        ) = saved[layer_index]
        fields = layer_fields(vectors, layer_index)
        gain_one, gain_two = fields[0], fields[5]
        grad_down_out = grad_hidden.astype(jnp.bfloat16)
        down_bias_grad = jnp.sum(grad_down_out.astype(jnp.float32), 0)
        grad_activated = dot32("rd,fd->rf", grad_down_out, w_down)
        _, gelu_back = jax.vjp(gelu_tanh, pre_act)
        grad_pre = gelu_back(grad_activated)[0].astype(jnp.bfloat16)
        up_bias_grad = jnp.sum(grad_pre.astype(jnp.float32), 0)
        up_bias_grad = up_bias_grad.reshape(2 * dp_size, half_rows)[unit_back].reshape(FF)

        mine, theirs = slice(0, FF // 2), slice(FF // 2, FF)
        act_two = jnp.concatenate([activated[:, mine], swap_dp(activated[:, theirs], 0)], 0)
        pre_two = jnp.concatenate([grad_pre[:, mine], swap_dp(grad_pre[:, theirs], 0)], 0)
        out_two = jnp.concatenate([grad_down_out, swap_dp(grad_down_out, 0)], 0)
        in_two = jnp.concatenate([mlp_in, swap_dp(mlp_in, 0)], 0)
        up_grad = dot32("rf,rd->fd", pre_two, in_two).astype(jnp.bfloat16)
        down_grad = dot32("rf,rd->fd", act_two, out_two).astype(jnp.bfloat16)
        both = jnp.stack([up_grad, down_grad]).reshape(2, 2, links, half_rows, D)
        both_a = scatter_path(both[:, 0], path_a, 1)
        both_b = scatter_path(both[:, 1], path_b, 1)
        both = jnp.concatenate([both_a[:, 0], both_b[:, 0]], 1)
        mlp_shares[layer_index] = own_rep(both, layer_index)

        grad_mlp_in = dot32("rf,fd->rd", grad_pre, w_up)
        grad_norm_two, gain_two_grad, bias_two_grad = norm_back(
            grad_mlp_in, normed_two, inverse_two, gain_two
        )
        grad_mid = grad_hidden + grad_norm_two
        grad_branch = grad_mid.astype(jnp.bfloat16)
        output_bias_grad = jnp.sum(grad_branch.astype(jnp.float32), 0)
        grad_attended = dot32("re,de->rd", grad_branch, w_output)
        grad_attended = grad_attended.astype(jnp.bfloat16).reshape(total_row_count, HEADS, HDIM)
        scores = masked_scores(query_heads, key_heads, key_valid)
        probs_full = jnp.exp(scores - log_total)
        probs_low = probs_full.astype(jnp.bfloat16)
        value_part = dot32("hqk,qhd->khd", probs_low, grad_attended)
        grad_probs = dot32("qhd,khd->hqk", grad_attended, value_heads)
        row_dot = jnp.sum(probs_full * grad_probs, -1, keepdims=True)
        grad_scores = (probs_full * (grad_probs - row_dot)).astype(jnp.bfloat16)
        head_scale = HDIM ** (-0.5)
        grad_queries = dot32("hqk,khd->qhd", grad_scores, key_heads) * head_scale
        grad_queries = grad_queries.reshape(total_row_count, D).astype(jnp.bfloat16)
        key_part = dot32("hqk,qhd->khd", grad_scores, query_heads) * head_scale
        parts = jnp.concatenate(
            [key_part.reshape(seq_len, D), value_part.reshape(seq_len, D)], 1
        ).astype(jnp.bfloat16)
        half = seq_len // 2
        parts = parts[:half].astype(jnp.float32) + swap_dp(parts[half:], 0).astype(jnp.float32)
        arrived = swap_rep(parts[total_row_count:].astype(jnp.bfloat16), 1)
        parts = (parts[:total_row_count] + arrived.astype(jnp.float32)).astype(jnp.bfloat16)
        grad_keys, grad_values = parts[:, :D], parts[:, D:]

        mix_two = jnp.concatenate(
            [
                core_columns(mixed_in, dp_size, core),
                swap_dp(core_columns(mixed_in, dp_size, 1 - core), 0),
            ],
            0,
        )
        att_two = jnp.concatenate(
            [
                core_columns(attended, dp_size, core),
                swap_dp(core_columns(attended, dp_size, 1 - core), 0),
            ],
            0,
        )

        def attn_grad(left_two, right):
            right_two = jnp.concatenate([right, swap_dp(right, 0)], 0)
            return dot32("rd,re->de", left_two, right_two).astype(jnp.bfloat16)

        shape = [2] + [2] * len(path_a) + [attn_rows, D]
        tops = [
            jnp.stack([attn_grad(mix_two, grad_queries), attn_grad(mix_two, grad_keys)]),
            jnp.stack([attn_grad(mix_two, grad_values), attn_grad(att_two, grad_branch)]),
        ]
        tops = [value.reshape(shape) for value in tops]
        for which, order in enumerate((path_b, path_a)):
            value = tops[which]
            for bit in order:
                axis = len(path_a) + 1 - bit
                mine_bit = (me >> bit) & 1
                keep = lax.dynamic_slice_in_dim(value, mine_bit, 1, axis)
                send = lax.dynamic_slice_in_dim(value, 1 - mine_bit, 1, axis)
                value = (
                    keep.astype(jnp.float32) + swap_dp(send, bit).astype(jnp.float32)
                ).astype(jnp.bfloat16)
            tops[which] = value.reshape(2, attn_rows, D)
        attn_shares[layer_index] = own_rep(jnp.stack(tops), layer_index)

        grad_mixed = (
            dot32("re,de->rd", grad_queries, w_query)
            + dot32("re,de->rd", grad_keys, w_key)
            + dot32("re,de->rd", grad_values, w_value)
        )
        table_grad = lead_hot[:, None] * jnp.sum(grad_mixed, 0)[None, :]
        grad_norm_one, gain_one_grad, bias_one_grad = norm_back(
            grad_mixed, normed_one, inverse_one, gain_one
        )
        grad_hidden = grad_mid + grad_norm_one
        query_bias_grad = jnp.sum(grad_queries.astype(jnp.float32), 0)
        value_bias_grad = jnp.sum(grad_values.astype(jnp.float32), 0)
        layer_grads[layer_index] = jnp.concatenate(
            [
                gain_one_grad,
                bias_one_grad,
                query_bias_grad,
                value_bias_grad,
                output_bias_grad,
                gain_two_grad,
                bias_two_grad,
                down_bias_grad,
                up_bias_grad,
                table_grad.reshape(NLEAD * D),
            ]
        )
        if layer_index == LAYERS - 1:
            early = sum_all(
                jnp.concatenate(
                    [
                        head_grad.reshape(-1),
                        layer_grads[layer_index],
                        final_gain_grad,
                        final_bias_grad,
                        head_bias_grad,
                        negent_local.reshape(1),
                    ]
                )
            )
    features_grad = exchange_frames(grad_hidden)
    late = sum_all(jnp.concatenate(layer_grads[: LAYERS - 1]))
    head_size = D * head_master.shape[1]
    head_sum = early[:head_size].reshape(D, -1)
    vec_sum = jnp.concatenate([late, early[head_size:-1]])
    penalty = early[-1] / pixel_total

    attn_share = jnp.where(rep_high == 0, attn_shares[0], attn_shares[1])
    mlp_share = jnp.where(rep_high == 0, mlp_shares[0], mlp_shares[1])
    attn_moment = MOMENTUM * attn_momentum + attn_share
    mlp_moment = MOMENTUM * mlp_momentum + mlp_share[None]
    attn_state = attn_share + MOMENTUM * attn_moment
    mlp_state = mlp_share + MOMENTUM * mlp_moment[0]
    mlp_rows_all = gather_rows(mlp_state)
    mlp_state = orthogonal(mlp_state, dot32("rd,re->de", mlp_rows_all, mlp_rows_all))
    attn_states = []
    for index in range(2):
        rows_all = gather_rows(attn_state[index])
        attn_states.append(
            orthogonal(attn_state[index], dot32("rd,re->de", rows_all, rows_all))
        )
    attn_state = jnp.stack(attn_states)
    attn_kinds = (rep * 2 + jnp.arange(2)) % 4
    attn_rate = jnp.asarray(ATTN_RATES, jnp.float32)[attn_kinds][:, None, None]
    mlp_rate = jnp.asarray(MLP_RATES, jnp.float32)[rep % 2]
    attn_new = attn_master * (1.0 - attn_rate * DECAY) - attn_rate * attn_state
    mlp_new = mlp_master * (1.0 - mlp_rate * DECAY) - mlp_rate * mlp_state[None]
    vec_moment = MOMENTUM * vec_momentum + vec_sum
    vec_new = vectors - VEC_RATE * vec_moment
    head_moment = MOMENTUM * head_momentum + head_sum
    head_new = head_master - HEAD_RATE * head_moment
    return (
        prediction,
        features_grad,
        penalty,
        attn_moment,
        attn_new,
        mlp_moment,
        mlp_new,
        vec_moment,
        vec_new,
        head_moment,
        head_new,
    )


def solution(mesh):
    return jax.shard_map(
        local,
        mesh=mesh,
        in_specs=(
            P(("dp", "rep"), None),
            P(("dp", "rep"), None),
            P("dp"),
            P("dp"),
            P("rep", "dp", None),
            P("rep", "dp", None),
            P("rep", "dp", None),
            P("rep", "dp", None),
            P(),
            P(),
            P(),
            P(),
        ),
        out_specs=(
            P(("dp", "rep"), None),
            P(("dp", "rep"), None),
            P(),
            P("rep", "dp", None),
            P("rep", "dp", None),
            P("rep", "dp", None),
            P("rep", "dp", None),
            P(),
            P(),
            P(),
            P(),
        ),
        check_vma=False,
    )
```

```python
import functools

import jax
import jax.numpy as jnp
from jax import lax
from jax.experimental import pallas as pl
from jax.experimental.pallas import tpu as pltpu
from jax.sharding import PartitionSpec as P

D = 768
HEADS = 12
HDIM = 64
FF = 3072
LAYERS = 2
MODEL_NUMBER = 3
TILE_CELLS = 32
NLEAD = 8
NS_STEPS = 2


EPS = 1e-05
NEG = -1e30
MOMENTUM = 0.95
COEF_A = 3.4445
COEF_B = -4.775
COEF_C = 2.0315
PENALTY = 0.5
VEC_RATE = 1000.0
HEAD_RATE = 300.0
DECAY = 0.01
ATTN_RATES = (1.0, 1.0, 1.0, 4.0)
MLP_RATES = (2.0, 1.0)


def norm_parts(hidden):
    centred = hidden - jnp.mean(hidden, -1, keepdims=True)
    variance = jnp.mean(centred * centred, -1, keepdims=True)
    inverse = lax.rsqrt(variance + EPS)
    return (centred * inverse, inverse)


def norm_back(grad_out, normed, inverse, gain):
    scaled = grad_out * gain
    mean_one = jnp.mean(scaled, -1, keepdims=True)
    mean_two = jnp.mean(scaled * normed, -1, keepdims=True)
    grad_in = inverse * (scaled - mean_one - normed * mean_two)
    return (grad_in, jnp.sum(grad_out * normed, 0), jnp.sum(grad_out, 0))


ROOT_TWO_OVER_PI = 0.7978845608028654
CUBE = 0.044715
VEC_ROWS = 20
VMEM = pl.BlockSpec(memory_space=pltpu.VMEM)
SMEM = pl.BlockSpec(memory_space=pltpu.SMEM)
HBM = pl.BlockSpec(memory_space=pl.ANY)
BF16 = jnp.bfloat16
F32 = jnp.float32


def shape_of(*dims, dtype=F32):
    return jax.ShapeDtypeStruct(dims, dtype)


def limits(mib):
    return pltpu.CompilerParams(vmem_limit_bytes=mib * 1024 * 1024)


def dot_nn(left, right):
    return jnp.dot(left, right, preferred_element_type=F32)


def dot_nt(left, right):
    return lax.dot_general(left, right, (((1,), (1,)), ((), ())), preferred_element_type=F32)


def dot_tn(left, right):
    return lax.dot_general(left, right, (((0,), (0,)), ((), ())), preferred_element_type=F32)


def column_sum(value):
    return jnp.sum(value, 0, keepdims=True)


def start_all(copies):
    for copy in copies:
        copy.start()


def wait_all(copies):
    for copy in copies:
        copy.wait()


def attn_copies(refs, ids, rows, me, wanted, store, sems):
    result = []
    count = 0
    for place_at, (path, mat) in enumerate(wanted):
        copies = []
        for ref, ref_ids in zip(refs[path], ids[path]):
            for at, i in enumerate(ref_ids):
                first = pl.multiple_of((me ^ i) * rows, rows)
                copies.append(
                    pltpu.make_async_copy(
                        ref.at[at, mat], store.at[place_at, pl.ds(first, rows)], sems.at[count]
                    )
                )
                count += 1
        result.append(copies)
    return result


def mlp_copies(refs, plan, store, sems):
    result = []
    count = 0
    for chunk, parts in enumerate(plan):
        pair = []
        for mat in range(2):
            copies = []
            first = chunk * CHUNK
            for path, piece, at, start, rows in parts:
                copies.append(
                    pltpu.make_async_copy(
                        refs[path][piece].at[at, mat, pl.ds(start, rows)],
                        store.at[mat, pl.ds(first, rows)],
                        sems.at[count],
                    )
                )
                first += rows
                count += 1
            pair.append(copies)
        result.append(pair)
    return result


CHUNK = 384


def split_refs(refs, sizes):
    out = []
    at = 0
    for size in sizes:
        out.append(refs[at : at + size])
        at += size
    assert at == len(refs)
    return out


def select_matrix(source):
    rows = lax.broadcasted_iota(jnp.int32, (D, D), 0)
    return (rows == source).astype(F32).astype(BF16)


def qkv_kernel(ids, rows, layer, info, hidden, vec, source, *refs):
    sizes = [len(ids[0]), len(ids[1]), 4, 2]
    path_a, path_b, (own, other, queries, pair), (store, sems) = split_refs(refs, sizes)
    copies = attn_copies((path_a, path_b), ids, rows, info[0], ((0, 0), (0, 1), (1, 0)), store, sems)
    for group in copies:
        start_all(group)
    row = VEC_ROWS * layer
    lead_row = row + 12 + info[2] - 1
    normed, _ = norm_parts(hidden[...].astype(F32))
    mixed = (normed * vec[row : row + 1] + vec[row + 1 : row + 2] + vec[pl.ds(lead_row, 1)]).astype(BF16)
    moved = dot_nn(mixed, select_matrix(source[...])).astype(BF16)
    own[...] = moved[:, : D // 2]
    other[...] = moved[:, D // 2 :]
    wait_all(copies[0])
    queries[...] = (dot_nn(mixed, store[0]) + vec[row + 2 : row + 3]).astype(BF16)
    wait_all(copies[1])
    pair[:, :D] = dot_nn(mixed, store[1]).astype(BF16)
    wait_all(copies[2])
    pair[:, D:] = (dot_nn(mixed, store[2]) + vec[row + 3 : row + 4]).astype(BF16)


def valid_row(quarter, count, rows, total):
    at = lax.broadcasted_iota(jnp.int32, (1, total), 1)
    block = jnp.zeros((1, total), jnp.int32)
    for step in range(1, total // rows):
        block = block + (at >= step * rows).astype(jnp.int32)
    return ((quarter ^ block) - block) * rows + at < count


def head_mask(sub, rows):
    lanes = lax.broadcasted_iota(jnp.int32, (rows, 2 * HDIM), 1)
    return (lanes < HDIM) if sub == 0 else (lanes >= HDIM)


def attend_kernel(ids, rows, layer, info, hidden, vec, source, queries, *refs):
    sizes = [4, len(ids[0]), len(ids[1]), 5, 3]
    pairs, path_a, path_b, (own, other, log_total, mid, mlp_in), (store, joined, sems) = split_refs(refs, sizes)
    copies = attn_copies((path_a, path_b), ids, rows, info[0], ((1, 1),), store, sems)
    start_all(copies[0])
    row = VEC_ROWS * layer
    count = queries.shape[0]
    total = count * len(pairs)
    valid = valid_row(info[3], info[1], count, total)
    log_total[...] = jnp.zeros_like(log_total)
    for pair in range(HEADS // 2):
        lanes = slice(2 * HDIM * pair, 2 * HDIM * (pair + 1))
        shifted = slice(D + 2 * HDIM * pair, D + 2 * HDIM * (pair + 1))
        query = queries[:, lanes] * jnp.asarray(HDIM ** (-0.5), BF16)
        keys = jnp.concatenate([ref[:, lanes] for ref in pairs], 0)
        values = jnp.concatenate([ref[:, shifted] for ref in pairs], 0)
        outs = []
        for sub in range(2):
            mask = head_mask(sub, count)
            scores = dot_nt(jnp.where(mask, query, jnp.zeros_like(query)), keys)
            scores = jnp.where(valid, scores, NEG)
            top = jnp.max(scores, -1, keepdims=True)
            expo = jnp.exp(scores - top)
            sums = jnp.sum(expo, -1, keepdims=True)
            probs = (expo * (1.0 / sums)).astype(BF16)
            outs.append(dot_nn(probs, values))
            head = 2 * pair + sub
            log_total[:, head : head + 1] = top + jnp.log(sums)
        joined[:, lanes] = jnp.where(head_mask(0, count), outs[0], outs[1]).astype(BF16)
    attended = joined[...]
    moved = dot_nn(attended, select_matrix(source[...])).astype(BF16)
    own[...] = moved[:, : D // 2]
    other[...] = moved[:, D // 2 :]
    wait_all(copies[0])
    hidden_mid = hidden[...].astype(F32) + dot_nn(attended, store[0]) + vec[row + 4 : row + 5]
    mid[...] = hidden_mid
    normed, _ = norm_parts(hidden_mid)
    mlp_in[...] = (normed * vec[row + 5 : row + 6] + vec[row + 6 : row + 7]).astype(BF16)


def gelu_parts(value):
    inner = ROOT_TWO_OVER_PI * (value + CUBE * (value * value * value))
    return jnp.tanh(inner)


def mlp_kernel(sizes, plan, layer, chunk_ids, info, mid, mlp_in, vec, up_bias, *refs):
    count_a, count_b = sizes
    path_a, path_b, outs, (store, sems) = split_refs(refs, [count_a, count_b, 4, 2])
    hidden, pre_act, act_own, act_other = outs
    copies = mlp_copies((path_a, path_b), plan, store, sems)
    for pair in copies:
        start_all(pair[0])
        start_all(pair[1])
    row = VEC_ROWS * layer
    total = mid[...] + vec[row + 7 : row + 8]
    given = mlp_in[...]
    chunks = len(plan)
    for chunk in range(chunks):
        at = slice(chunk * CHUNK, (chunk + 1) * CHUNK)
        wait_all(copies[chunk][0])
        bias = up_bias[pl.ds(info[0] ^ chunk_ids[chunk], 1)].reshape(1, CHUNK)
        value = dot_nt(given, store[0, at]) + bias
        pre_act[:, at] = value
        active = (value * (0.5 * (1.0 + gelu_parts(value)))).astype(BF16)
        if chunk < chunks // 2:
            act_own[:, at] = active
        else:
            act_other[:, (chunk - chunks // 2) * CHUNK : (chunk - chunks // 2 + 1) * CHUNK] = active
        wait_all(copies[chunk][1])
        total = total + dot_nn(active, store[1, at])
    hidden[...] = total


def head_kernel(info, scale, hidden, tiles, vec, head_bias, head, *outs):
    prediction, head_grad, grad_hidden, sums = outs
    row = VEC_ROWS * LAYERS
    gain = vec[row : row + 1]
    count = hidden.shape[0]
    normed, inverse = norm_parts(hidden[...])
    final_in = (normed * gain + vec[row + 1 : row + 2]).astype(BF16)
    low = head[...].astype(BF16)
    out = dot_nn(final_in, low) + head_bias[...]
    lanes = lax.broadcasted_iota(jnp.int32, out.shape, 1)
    last = lanes >= MODEL_NUMBER * TILE_CELLS

    def over(value, join):
        result = value
        for step in range(1, MODEL_NUMBER + 1):
            result = join(result, pltpu.roll(value, step * TILE_CELLS, 1))
        return result

    def add(left, right):
        return left + right

    record = tiles[...]
    logits = jnp.where(last, NEG, out)
    shifted = logits - over(logits, jnp.maximum)
    log_gate = shifted - jnp.log(over(jnp.exp(shifted), add))
    gate = jnp.where(last, 0.0, jnp.exp(log_gate))
    blend = over(gate * record, add)
    estimate = blend + over(jnp.where(last, out, 0.0), add)
    error = estimate - over(jnp.where(last, record, 0.0), add)
    entropy = over(gate * log_gate, add)
    row_ids = info[3] * count + lax.broadcasted_iota(jnp.int32, (count, 1), 0)
    valid = (row_ids < info[1]).astype(F32)
    weight = valid * info[2].astype(F32)
    share = weight * scale[0]
    factor = share * error
    grads = gate * (factor * (record - blend) + PENALTY * share * (log_gate - entropy))
    grads = jnp.where(last, factor, grads).astype(BF16)
    prediction[...] = (estimate * valid)[:, :TILE_CELLS]
    head_grad[...] = dot_tn(final_in, grads)
    grad_final = dot_nt(grads, low)
    grad_in, gain_grad, bias_grad = norm_back(grad_final, normed, inverse, gain)
    grad_hidden[...] = grad_in
    sums[...] = jnp.zeros_like(sums)
    sums[0:1] = gain_grad[None]
    sums[1:2] = bias_grad[None]
    sums[2:3, :128] = column_sum(grads.astype(F32))
    sums[3:4, :128] = column_sum(jnp.where(lanes < TILE_CELLS, weight * entropy, 0.0))


def mlp_back_kernel(ids, rows, sizes, plan, layer, chunk_ids, info, grad, mid, pre_act, vec, *refs):
    groups = [sizes[0], sizes[1], len(ids[0]), len(ids[1]), 8, 4]
    mlp_a, mlp_b, path_a, path_b, outs, scratch = split_refs(refs, groups)
    grad_low, pre_own, pre_other, grad_mid, grad_branch, grad_attended, up_bias_grad, sums = outs
    store, out_store, sems, out_sems = scratch
    copies = mlp_copies((mlp_a, mlp_b), plan, store, sems)
    for pair in copies:
        start_all(pair[1])
        start_all(pair[0])
    out_copies = attn_copies((path_a, path_b), ids, rows, info[0], ((1, 1),), out_store, out_sems)
    start_all(out_copies[0])
    row = VEC_ROWS * layer
    upper = grad[...]
    low = upper.astype(BF16)
    grad_low[...] = low
    total = jnp.zeros(upper.shape, F32)
    chunks = len(plan)
    for chunk in range(chunks):
        at = slice(chunk * CHUNK, (chunk + 1) * CHUNK)
        wait_all(copies[chunk][1])
        grad_active = dot_nt(low, store[1, at])
        value = pre_act[:, at]
        tanh = gelu_parts(value)
        slope = 0.5 * (1.0 + tanh) + (0.5 * ROOT_TWO_OVER_PI) * value * (1.0 - tanh * tanh) * (
            1.0 + (3.0 * CUBE) * (value * value)
        )
        grad_pre = (grad_active * slope).astype(BF16)
        if chunk < chunks // 2:
            pre_own[:, at] = grad_pre
        else:
            pre_other[:, (chunk - chunks // 2) * CHUNK : (chunk - chunks // 2 + 1) * CHUNK] = grad_pre
        up_bias_grad[pl.ds(info[0] ^ chunk_ids[chunk], 1)] = column_sum(grad_pre.astype(F32)).reshape(1, 1, CHUNK)
        wait_all(copies[chunk][0])
        total = total + dot_nn(grad_pre, store[0, at])
    normed, inverse = norm_parts(mid[...])
    grad_norm, gain_grad, bias_grad = norm_back(total, normed, inverse, vec[row + 5 : row + 6])
    grad_sum = upper + grad_norm
    grad_mid[...] = grad_sum
    branch = grad_sum.astype(BF16)
    grad_branch[...] = branch
    sums[...] = jnp.zeros_like(sums)
    sums[0:1] = column_sum(branch.astype(F32))
    sums[1:2] = gain_grad[None]
    sums[2:3] = bias_grad[None]
    sums[3:4] = column_sum(low.astype(F32))
    wait_all(out_copies[0])
    grad_attended[...] = dot_nt(branch, out_store[0]).astype(BF16)


def attend_back_kernel(info, queries, grad_attended, log_total, *refs):
    pairs, outs = split_refs(refs, [4, 4])
    grad_queries, keep, near, send = outs
    count = queries.shape[0]
    total = count * len(pairs)
    valid = valid_row(info[3], info[1], count, total)
    scale = HDIM ** (-0.5)
    for pair in range(HEADS // 2):
        lanes = slice(2 * HDIM * pair, 2 * HDIM * (pair + 1))
        shifted = slice(D + 2 * HDIM * pair, D + 2 * HDIM * (pair + 1))
        query = queries[:, lanes] * jnp.asarray(scale, BF16)
        grad = grad_attended[:, lanes]
        query_t = query.astype(F32).T.astype(BF16)
        grad_t = grad.astype(F32).T.astype(BF16)
        keys = jnp.concatenate([ref[:, lanes] for ref in pairs], 0)
        values = jnp.concatenate([ref[:, shifted] for ref in pairs], 0)
        outs_q, outs_k, outs_v = [], [], []
        for sub in range(2):
            mask = head_mask(sub, count)
            head = 2 * pair + sub
            rows = slice(HDIM * sub, HDIM * (sub + 1))
            zero = jnp.zeros_like(query)
            scores = dot_nt(jnp.where(mask, query, zero), keys)
            scores = jnp.where(valid, scores, NEG)
            probs = jnp.exp(scores - log_total[:, head : head + 1])
            grad_probs = dot_nt(jnp.where(mask, grad, zero), values)
            row_dot = jnp.sum(probs * grad_probs, -1, keepdims=True)
            grad_scores = (probs * (grad_probs - row_dot)).astype(BF16)
            outs_q.append(dot_nn(grad_scores, keys))
            outs_k.append(dot_nn(query_t[rows], grad_scores))
            outs_v.append(dot_nn(grad_t[rows], probs.astype(BF16)))
        grad_queries[:, lanes] = (jnp.where(head_mask(0, count), outs_q[0], outs_q[1]) * scale).astype(BF16)
        for where, outs_t in ((lanes, outs_k), (shifted, outs_v)):
            part = jnp.concatenate(outs_t, 0).T.astype(BF16)
            keep[:, where] = part[:count]
            near[:, where] = part[count : 2 * count]
            send[:, where] = part[2 * count :]


def qkv_back_kernel(ids, rows, layer, info, grad_queries, keep, arrived, near, hidden, grad_mid, vec, *refs):
    groups = [len(ids[0]), len(ids[1]), 3, 2]
    path_a, path_b, (grad_hidden, grad_pair, sums), (store, sems) = split_refs(refs, groups)
    copies = attn_copies((path_a, path_b), ids, rows, info[0], ((0, 0), (0, 1), (1, 0)), store, sems)
    for group in copies:
        start_all(group)
    row = VEC_ROWS * layer
    pair = (keep[...].astype(F32) + arrived[...].astype(F32) + near[...].astype(F32)).astype(BF16)
    grad_pair[...] = pair
    grad_q = grad_queries[...]
    wait_all(copies[0])
    total = dot_nt(grad_q, store[0])
    wait_all(copies[1])
    total = total + dot_nt(pair[:, :D], store[1])
    wait_all(copies[2])
    total = total + dot_nt(pair[:, D:], store[2])
    normed, inverse = norm_parts(hidden[...].astype(F32))
    grad_norm, gain_grad, bias_grad = norm_back(total, normed, inverse, vec[row : row + 1])
    grad_hidden[...] = grad_mid[...] + grad_norm
    sums[...] = jnp.zeros_like(sums)
    sums[0:1] = gain_grad[None]
    sums[1:2] = bias_grad[None]
    sums[2:3] = column_sum(grad_q.astype(F32))
    sums[3:4] = column_sum(pair[:, D:].astype(F32))


def reversed_bits(value, width):
    return sum(((value >> bit) & 1) << (width - 1 - bit) for bit in range(width))


def place_parts(value, blocks, width, mat, path, start, outs):
    at, rows = blocks
    at = at if path == 0 else reversed_bits(at, width)
    half = 1 << (width - 1)
    keep, send = outs[path]
    ref = keep if at < half else send
    ref[at % half, mat, start : start + rows] = value


def mlp_weight_kernel(width, half_rows, *refs):
    ins, outs = split_refs(refs, [8, 4])
    act, act_far, pre, pre_far, grad, grad_far, given, given_far = ins
    paths = (outs[:2], outs[2:])
    grad_two = jnp.concatenate([grad[...], grad_far[...]], 0)
    given_two = jnp.concatenate([given[...], given_far[...]], 0)
    rows = 2 * half_rows
    for at in range(1 << width):
        lanes = slice(at * rows, (at + 1) * rows)
        for mat, near, far, right in ((0, pre, pre_far, given_two), (1, act, act_far, grad_two)):
            left = jnp.concatenate([near[:, lanes], far[:, lanes]], 0)
            value = dot_tn(left, right).astype(BF16)
            for path in range(2):
                part = value[path * half_rows : (path + 1) * half_rows]
                place_parts(part, (at, half_rows), width, mat, path, 0, paths)


def attn_weight_kernel(width, rows, *refs):
    ins, outs = split_refs(refs, [10, 4])
    mixed, mixed_far, att, att_far, grad_q, grad_q_far, pair, pair_far, branch, branch_far = ins
    paths = (outs[:2], outs[2:])
    mixed_two = jnp.concatenate([mixed[...], mixed_far[...]], 0)
    att_two = jnp.concatenate([att[...], att_far[...]], 0)
    jobs = (
        (0, 0, mixed_two, jnp.concatenate([grad_q[...], grad_q_far[...]], 0)),
        (0, 1, mixed_two, jnp.concatenate([pair[:, :D], pair_far[:, :D]], 0)),
        (1, 0, mixed_two, jnp.concatenate([pair[:, D:], pair_far[:, D:]], 0)),
        (1, 1, att_two, jnp.concatenate([branch[...], branch_far[...]], 0)),
    )
    for path, mat, left, right in jobs:
        value = dot_tn(left, right).astype(BF16)
        for at in range(1 << width):
            place_parts(value[at * rows : (at + 1) * rows], (at, rows), width, mat, path, 0, paths)


def polynomial_kernel(pieces, rate, *refs):
    mats = len(pieces)
    ins, (master, state, new), scratch = split_refs(refs, [sum(pieces), 3, 5])
    gram, low, mix, cross, moved = scratch
    block = D // 3
    spots = range(0, D, block)
    at_piece = 0
    for mat in range(mats):
        mine = ins[at_piece : at_piece + pieces[mat]]
        at_piece += pieces[mat]
        trace = jnp.zeros((), F32)
        for spot in spots:
            at = slice(spot, spot + block)
            total = jnp.zeros((block, D), F32)
            for ref in mine:
                total = total + dot_tn(ref[:, at], ref[...])
            gram[at] = total
            hot = lax.broadcasted_iota(jnp.int32, (block, D), 0) + spot == lax.broadcasted_iota(
                jnp.int32, (block, D), 1
            )
            trace = trace + jnp.sum(jnp.where(hot, total, 0.0))
        factor = 1.0 / (jnp.sqrt(trace) + 1e-07)
        square = factor * factor
        for spot in spots:
            at = slice(spot, spot + block)
            value = gram[at] * square
            gram[at] = value
            low[at] = value.astype(BF16)
        value = state[mat] * factor
        for step in range(NS_STEPS):
            for spot in spots:
                at = slice(spot, spot + block)
                mix[at] = (COEF_B * gram[at] + COEF_C * dot_nn(low[at], low[...])).astype(BF16)
            value = COEF_A * value + dot_nn(value.astype(BF16), mix[...])
            if step + 1 < NS_STEPS:
                for spot in spots:
                    at = slice(spot, spot + block)
                    moved[at] = dot_nn(mix[at], low[...])
                    cross[at] = moved[at].astype(BF16)
                for spot in spots:
                    at = slice(spot, spot + block)
                    result = (
                        (COEF_A * COEF_A) * gram[at]
                        + (2.0 * COEF_A) * moved[at]
                        + dot_nn(mix[at], cross[...])
                    )
                    gram[at] = result
                for spot in spots:
                    at = slice(spot, spot + block)
                    low[at] = gram[at].astype(BF16)
        new[mat] = master[mat] * (1.0 - rate[mat] * DECAY) - rate[mat] * value


def swap_dp(value, bit):
    size = lax.axis_size("dp")
    return lax.ppermute(value, "dp", [(i, i ^ (1 << bit)) for i in range(size)])


def swap_rep(value, mask):
    size = lax.axis_size("rep")
    return lax.ppermute(value, "rep", [(i, i ^ mask) for i in range(size)])


def link_bits():
    count = lax.axis_size("dp").bit_length() - 1
    return (list(range(1, count)), list(range(count - 1, 0, -1)))


def path_ids(order):
    ids = [0]
    for bit in order:
        ids = ids + [i | (1 << bit) for i in ids]
    return ids


def spread_rep(own):
    rep = lax.axis_index("rep")
    far = swap_rep(own, 2)
    near = swap_rep(jnp.stack([own, far]), 1)
    all_four = jnp.stack([own, near[0], far, near[1]])
    return [
        lax.dynamic_index_in_dim(all_four, rep ^ i, 0, keepdims=False) for i in range(4)
    ]


def own_rep(pair, layer_index):
    rep = lax.axis_index("rep")
    low = rep & 1
    keep = lax.dynamic_index_in_dim(pair, low, 0, keepdims=False)
    send = lax.dynamic_index_in_dim(pair, 1 - low, 0, keepdims=False)
    part = keep.astype(jnp.float32) + swap_rep(send, 1).astype(jnp.float32)
    first = 2 * layer_index
    moves = [(i, i ^ 2) for i in range(4) if i // 2 != layer_index]
    return part + lax.ppermute(part.astype(jnp.bfloat16), "rep", moves).astype(jnp.float32)


def call(kernel, ins, outs, scratch=(), specs=None, mib=40, flops=0, moved=0):
    return pl.pallas_call(
        kernel,
        out_shape=tuple(outs),
        in_specs=specs or [VMEM] * len(ins),
        out_specs=tuple(VMEM for _ in outs),
        scratch_shapes=list(scratch),
        compiler_params=limits(mib),
        cost_estimate=pl.CostEstimate(flops=flops, bytes_accessed=moved, transcendentals=0),
    )(*ins)


def gather_pieces(own, order):
    near, ids = own[None], [0]
    for bit in order[:-1]:
        near = jnp.concatenate([near, swap_dp(near, bit)], 0)
        ids = ids + [i | (1 << bit) for i in ids]
    last = 1 << order[-1]
    far = swap_dp(near, order[-1])
    pieces = [near, far, swap_dp(near, 0), swap_dp(far, 0)]
    far_ids = [i | last for i in ids]
    return pieces, [ids, far_ids, [i | 1 for i in ids], [i | 1 for i in far_ids]]


def gather_rows(low, order):
    near = low
    for bit in order[:-1]:
        near = jnp.concatenate([near, swap_dp(near, bit)], 0)
    far = swap_dp(near, order[-1])
    return [near, far, swap_dp(near, 0), swap_dp(far, 0)]


def natural(pieces, ids):
    me = lax.axis_index("dp")
    flat = [i for group in ids for i in group]
    slot = [0] * len(flat)
    for at, i in enumerate(flat):
        slot[i] = at
    joined = jnp.concatenate(pieces, 0)
    wanted = jnp.asarray(slot, jnp.int32)[jnp.arange(len(flat)) ^ me]
    taken = jnp.take(joined, wanted, axis=0)
    mats, width = taken.shape[1], taken.shape[3]
    return taken.transpose(1, 0, 2, 3).reshape(1, mats, -1, width)


def add_low(keep, arrived):
    return (keep.astype(F32) + arrived.astype(F32)).astype(BF16)


def scatter_path(keep, send, order):
    for step, bit in enumerate(order):
        if step > 0:
            half = value.shape[0] // 2
            keep, send = value[:half], value[half:]
        value = add_low(keep, swap_dp(send, bit))
    return value[0]


def sum_all(rows):
    core = lax.axis_index("dp") & 1
    half = rows.shape[0] // 2
    mine = lax.dynamic_slice_in_dim(rows, core * half, half, 0)
    other = lax.dynamic_slice_in_dim(rows, (1 - core) * half, half, 0)
    total = mine + swap_dp(other, 0)
    for bit in link_bits()[0]:
        total = total + swap_dp(total, bit)
    total = total + swap_rep(total, 1)
    total = total + swap_rep(total, 2)
    other = swap_dp(total, 0)
    first = jnp.where(core == 0, total, other)
    second = jnp.where(core == 0, other, total)
    return jnp.concatenate([first, second], 0)


def local(
    features,
    tile_records,
    patch_counts,
    lead_counts,
    attn_master,
    attn_momentum,
    mlp_master,
    mlp_momentum,
    vectors,
    vec_momentum,
    head_master,
    head_momentum,
):
    rep_size = lax.axis_size("rep")
    dp_size = lax.axis_size("dp")
    me = lax.axis_index("dp")
    core = me & 1
    rep = lax.axis_index("rep")
    rep_low = rep & 1
    rep_high = rep >> 1
    count = features.shape[0]
    seq_len = count * rep_size
    attn_rows = attn_master.shape[1]
    mlp_rows = mlp_master.shape[1]
    half_rows = mlp_rows // 2
    links = dp_size // 2
    width = links.bit_length() - 1
    path_a, path_b = link_bits()
    direct = attn_rows % 16 == 0 and mlp_rows == CHUNK

    moves = []
    for d in range(dp_size):
        for r in range(rep_size):
            to = (d - d % 2 + r // 2) * rep_size + (d % 2) * 2 + r % 2
            moves.append((d * rep_size + r, to))

    def exchange_frames(value):
        return lax.ppermute(value, ("dp", "rep"), moves)

    attn_by_rep = spread_rep(attn_master.astype(BF16))
    features = exchange_frames(features)
    mlp_by_rep = spread_rep(mlp_master[0].astype(BF16))
    tile_records = exchange_frames(tile_records)

    counts = jnp.concatenate([patch_counts, lead_counts]).reshape(1, 2)
    counts = jnp.concatenate([counts, swap_dp(counts, 0)], 0)
    frame_count, lead_value = lax.dynamic_index_in_dim(
        counts, core ^ rep_high, 0, keepdims=False
    )
    for bit in path_a:
        counts = jnp.concatenate([counts, swap_dp(counts, bit)], 0)
    pixel_total = (TILE_CELLS * jnp.sum(counts[:, 0] * counts[:, 1])).astype(F32)
    quarter = 2 * core + rep_low
    info = jnp.stack([me if direct else 0 * me, frame_count, lead_value, quarter]).astype(jnp.int32)
    lead_hot = (jnp.arange(NLEAD) == lead_value - 1).astype(F32)

    position = jnp.arange(D) // attn_rows
    distance = ((position % links) << 1) | (position // links)
    source = ((distance ^ me) * attn_rows + jnp.arange(D) % attn_rows).astype(jnp.int32)[None]
    order = [(at % links) << 1 | at // links for at in range(dp_size)]

    vec_rows = VEC_ROWS * LAYERS + 2
    vec = vectors[: vec_rows * D].reshape(vec_rows, D)
    head_bias = vectors[vec_rows * D :].reshape(1, -1)
    chunks = FF // CHUNK

    attn_pieces, mlp_pieces = [], []
    for layer in range(LAYERS):
        first, ids_a = gather_pieces(attn_by_rep[2 * layer], path_a)
        second, ids_b = gather_pieces(attn_by_rep[2 * layer + 1], path_b)
        if direct:
            attn_pieces.append(first + second)
            attn_ids = (ids_a, ids_b)
        else:
            attn_pieces.append([natural(first, ids_a), natural(second, ids_b)])
            attn_ids = ([[0]], [[0]])
        both = jnp.stack([mlp_by_rep[2 * layer], mlp_by_rep[2 * layer + 1]])
        first, _ = gather_pieces(both[:, :half_rows], path_a)
        second, _ = gather_pieces(both[:, half_rows:], path_b)
        if direct:
            mlp_pieces.append(first + second)
            mlp_sizes = (len(first), len(second))
        else:
            first, second = natural(first, ids_a), natural(second, ids_b)
            shape = (1, 2, dp_size, half_rows, D)
            joined = jnp.concatenate([first.reshape(shape), second.reshape(shape)], 3)
            mlp_pieces.append([joined.reshape(1, 2, FF, D)])
            mlp_sizes = (1, 0)
    if direct:
        chunk_ids = order
        found = [
            {i: (piece, at) for piece, group in enumerate(ids) for at, i in enumerate(group)}
            for ids in (ids_a, ids_b)
        ]
        plan = [
            [(path, *found[path][i], 0, half_rows) for path in range(2)] for i in order
        ]
        place_rows = attn_rows
    else:
        chunk_ids = list(range(chunks))
        plan = [[(0, 0, 0, chunk * CHUNK, CHUNK)] for chunk in range(chunks)]
        place_rows = D
    n_attn = len(attn_pieces[0])
    n_mlp = len(mlp_pieces[0])
    copies_each = sum(len(group) for group in attn_ids[0])
    mlp_copies_all = 2 * sum(len(parts) for parts in plan)
    dma = pltpu.SemaphoreType.DMA
    matrix = D * D
    layer_flops = 2 * count * matrix

    def mlp_rel(first, second):
        if direct:
            return first, second
        whole = jnp.concatenate([first, second], 1).reshape(count, dp_size, mlp_rows)
        whole = jnp.take(whole, jnp.asarray(order, jnp.int32) ^ me, axis=1).reshape(count, FF)
        return whole[:, : FF // 2], whole[:, FF // 2 :]

    hidden = features
    saved = []
    for layer in range(LAYERS):
        outs = call(
            functools.partial(qkv_kernel, attn_ids, place_rows, layer),
            [info, hidden, vec, source] + attn_pieces[layer],
            [
                shape_of(count, D // 2, dtype=BF16),
                shape_of(count, D // 2, dtype=BF16),
                shape_of(count, D, dtype=BF16),
                shape_of(count, 2 * D, dtype=BF16),
            ],
            [pltpu.VMEM((3, D, D), BF16), dma((3 * copies_each,))],
            [SMEM, VMEM, VMEM, VMEM] + [HBM] * n_attn,
            flops=4 * layer_flops,
            moved=6 * matrix + 4 * count * D * 4,
        )
        mixed_own, mixed_other, queries, pair = outs
        near = swap_rep(pair, 1)
        pairs = [pair, near, swap_dp(pair, 0), swap_dp(near, 0)]
        outs = call(
            functools.partial(attend_kernel, attn_ids, place_rows, layer),
            [info, hidden, vec, source, queries] + pairs + attn_pieces[layer],
            [
                shape_of(count, D // 2, dtype=BF16),
                shape_of(count, D // 2, dtype=BF16),
                shape_of(count, 128),
                shape_of(count, D),
                shape_of(count, D, dtype=BF16),
            ],
            [pltpu.VMEM((1, D, D), BF16), pltpu.VMEM((count, D), BF16), dma((copies_each,))],
            [SMEM, VMEM, VMEM, VMEM] + [VMEM] * 5 + [HBM] * n_attn,
            flops=8 * layer_flops,
            moved=2 * matrix + seq_len * D * 4,
        )
        att_own, att_other, log_total, mid, mlp_in = outs
        up_bias = vec[VEC_ROWS * layer + 8 : VEC_ROWS * layer + 12].reshape(chunks, 1, CHUNK)
        outs = call(
            functools.partial(mlp_kernel, mlp_sizes, plan, layer, chunk_ids),
            [info, mid, mlp_in, vec, up_bias] + mlp_pieces[layer],
            [
                shape_of(count, D),
                shape_of(count, FF),
                shape_of(count, FF // 2, dtype=BF16),
                shape_of(count, FF // 2, dtype=BF16),
            ],
            [pltpu.VMEM((2, FF, D), BF16), dma((mlp_copies_all,))],
            [SMEM] + [VMEM] * 4 + [HBM] * n_mlp,
            flops=8 * layer_flops,
            moved=4 * FF * D + count * FF * 6,
        )
        next_hidden, pre_act, act_own, act_other = outs
        saved.append(
            (hidden, mixed_own, mixed_other, queries, pairs, att_own, att_other)
            + (log_total, mid, mlp_in, pre_act, act_own, act_other)
        )
        hidden = next_hidden

    scale = (1.0 / pixel_total).reshape(1)
    outs = call(
        head_kernel,
        [info, scale, hidden, tile_records, vec, head_bias, head_master],
        [shape_of(count, TILE_CELLS), shape_of(D, 128), shape_of(count, D), shape_of(8, D)],
        (),
        [SMEM, SMEM] + [VMEM] * 5,
        flops=layer_flops,
        moved=D * 128 * 8 + count * D * 8,
    )
    prediction, head_grad, grad_hidden, head_sums = outs
    prediction = exchange_frames(prediction)

    attn_shares = [None] * LAYERS
    mlp_shares = [None] * LAYERS
    layer_rows = [None] * LAYERS
    early = None
    back_a, back_b = path_b, path_a
    for layer in reversed(range(LAYERS)):
        (hidden, mixed_own, mixed_other, queries, pairs, att_own, att_other) = saved[layer][:7]
        (log_total, mid, mlp_in, pre_act, act_own, act_other) = saved[layer][7:]
        outs = call(
            functools.partial(
                mlp_back_kernel, attn_ids, place_rows, mlp_sizes, plan, layer, chunk_ids
            ),
            [info, grad_hidden, mid, pre_act, vec] + mlp_pieces[layer] + attn_pieces[layer],
            [
                shape_of(count, D, dtype=BF16),
                shape_of(count, FF // 2, dtype=BF16),
                shape_of(count, FF // 2, dtype=BF16),
                shape_of(count, D),
                shape_of(count, D, dtype=BF16),
                shape_of(count, D, dtype=BF16),
                shape_of(chunks, 1, CHUNK),
                shape_of(8, D),
            ],
            [
                pltpu.VMEM((2, FF, D), BF16),
                pltpu.VMEM((1, D, D), BF16),
                dma((mlp_copies_all,)),
                dma((copies_each,)),
            ],
            [SMEM] + [VMEM] * 4 + [HBM] * (n_mlp + n_attn),
            flops=9 * layer_flops,
            moved=4 * FF * D + 2 * matrix + count * FF * 6,
        )
        grad_low, pre_own, pre_other, grad_mid, branch, grad_attended, up_bias_grad, mlp_sums = outs
        near_pre, other_pre = mlp_rel(pre_own, pre_other)
        near_act, other_act = mlp_rel(act_own, act_other)
        ins = [near_act, swap_dp(other_act, 0), near_pre, swap_dp(other_pre, 0)]
        ins += [grad_low, swap_dp(grad_low, 0), mlp_in, swap_dp(mlp_in, 0)]
        if direct:
            part = shape_of(links // 2, 2, half_rows, D, dtype=BF16)
            parts = call(
                functools.partial(mlp_weight_kernel, width, half_rows),
                ins,
                [part] * 4,
                flops=8 * layer_flops,
                moved=4 * FF * D + count * FF * 8,
            )
        else:
            lefts = [jnp.concatenate(ins[2:4], 0), jnp.concatenate(ins[:2], 0)]
            rights = [jnp.concatenate(ins[6:], 0), jnp.concatenate(ins[4:6], 0)]
            both = jnp.stack([dot_tn(l, r).astype(BF16) for l, r in zip(lefts, rights)])
            both = both.reshape(2, links, 2, half_rows, D).transpose(2, 1, 0, 3, 4)
            flipped = jnp.asarray([reversed_bits(at, width) for at in range(links)], jnp.int32)
            other = jnp.take(both[1], flipped, axis=0)
            parts = [both[0][: links // 2], both[0][links // 2 :]]
            parts += [other[: links // 2], other[links // 2 :]]
        share_a = scatter_path(parts[0], parts[1], back_a)
        share_b = scatter_path(parts[2], parts[3], back_b)
        mlp_shares[layer] = own_rep(jnp.concatenate([share_a, share_b], 1), layer)

        outs = call(
            attend_back_kernel,
            [info, queries, grad_attended, log_total] + pairs,
            [
                shape_of(count, D, dtype=BF16),
                shape_of(count, 2 * D, dtype=BF16),
                shape_of(count, 2 * D, dtype=BF16),
                shape_of(2 * count, 2 * D, dtype=BF16),
            ],
            (),
            [SMEM] + [VMEM] * 7,
            flops=20 * layer_flops,
            moved=seq_len * D * 8,
        )
        grad_queries, keep, near, send = outs
        arrived = swap_dp(send, 0)
        near = swap_rep(add_low(near, arrived[count:]), 1)
        outs = call(
            functools.partial(qkv_back_kernel, attn_ids, place_rows, layer),
            [info, grad_queries, keep, arrived[:count], near, hidden, grad_mid, vec]
            + attn_pieces[layer],
            [shape_of(count, D), shape_of(count, 2 * D, dtype=BF16), shape_of(8, D)],
            [pltpu.VMEM((3, D, D), BF16), dma((3 * copies_each,))],
            [SMEM] + [VMEM] * 7 + [HBM] * n_attn,
            flops=3 * layer_flops,
            moved=6 * matrix + count * D * 20,
        )
        grad_hidden, grad_pair, qkv_sums = outs
        ins = [mixed_own, swap_dp(mixed_other, 0), att_own, swap_dp(att_other, 0)]
        for value in (grad_queries, grad_pair, branch):
            ins += [value, swap_dp(value, 0)]
        if direct:
            part = shape_of(links // 2, 2, attn_rows, D, dtype=BF16)
            parts = call(
                functools.partial(attn_weight_kernel, width, attn_rows),
                ins,
                [part] * 4,
                flops=4 * layer_flops,
                moved=4 * matrix + count * D * 16,
            )
        else:
            mixed_two = jnp.concatenate(ins[:2], 0)
            att_two = jnp.concatenate(ins[2:4], 0)
            q_two, pair_two, branch_two = (
                jnp.concatenate(ins[at : at + 2], 0) for at in (4, 6, 8)
            )
            jobs = [(mixed_two, q_two), (mixed_two, pair_two[:, :D])]
            jobs += [(mixed_two, pair_two[:, D:]), (att_two, branch_two)]
            grads = [dot_tn(l, r).astype(BF16).reshape(links, attn_rows, D) for l, r in jobs]
            first = jnp.stack(grads[:2], 1)
            second = jnp.take(jnp.stack(grads[2:], 1), flipped, axis=0)
            parts = [first[: links // 2], first[links // 2 :]]
            parts += [second[: links // 2], second[links // 2 :]]
        share_a = scatter_path(parts[0], parts[1], back_a)
        share_b = scatter_path(parts[2], parts[3], back_b)
        attn_shares[layer] = own_rep(jnp.stack([share_a, share_b]), layer)
        layer_rows[layer] = jnp.concatenate(
            [
                qkv_sums[:4],
                mlp_sums[:4],
                up_bias_grad.reshape(4, D),
                lead_hot[:, None] * qkv_sums[1:2],
            ],
            0,
        )
        if layer == LAYERS - 1:
            early = sum_all(
                jnp.concatenate(
                    [
                        head_grad,
                        jnp.concatenate([layer_rows[layer], head_sums], 0).reshape(-1, 128),
                        jnp.zeros((8, 128), F32),
                    ],
                    0,
                )
            )
    features_grad = exchange_frames(grad_hidden)
    late = sum_all(
        jnp.concatenate([layer_rows[0].reshape(-1, 128), jnp.zeros((8, 128), F32)], 0)
    )
    lane_rows = VEC_ROWS * D // 128
    head_sum = early[:D]
    layer_sum = early[D : D + lane_rows]
    tail = early[D + lane_rows : D + lane_rows + 8 * D // 128]
    row_lanes = D // 128
    vec_sum = jnp.concatenate(
        [late[:lane_rows], layer_sum, tail[: 2 * row_lanes + 1]], 0
    ).reshape(-1)
    penalty = jnp.sum(tail[3 * row_lanes]) / pixel_total

    attn_share = jnp.where(rep_high == 0, attn_shares[0], attn_shares[1])
    mlp_share = jnp.where(rep_high == 0, mlp_shares[0], mlp_shares[1])[None]
    attn_moment = MOMENTUM * attn_momentum + attn_share
    mlp_moment = MOMENTUM * mlp_momentum + mlp_share
    attn_state = attn_share + MOMENTUM * attn_moment
    mlp_state = mlp_share + MOMENTUM * mlp_moment
    attn_rate = jnp.asarray(ATTN_RATES, F32).reshape(2, 2)[rep_low]
    mlp_rate = jnp.asarray(MLP_RATES, F32)[rep_low].reshape(1)

    def polynomial(groups, master, state, rate):
        pieces = [piece for group in groups for piece in group]
        sizes = [len(group) for group in groups]
        square = pltpu.VMEM((D, D), F32)
        low = pltpu.VMEM((D, D), BF16)
        rows = sum(piece.shape[0] for piece in pieces)
        return call(
            functools.partial(polynomial_kernel, sizes),
            [rate] + pieces + [master, state],
            [shape_of(*master.shape)],
            [square, low, low, low, square],
            [SMEM] + [VMEM] * (len(pieces) + 2),
            flops=2 * matrix * (rows + 4 * D * len(groups)),
            moved=rows * D * 2,
        )[0]

    low = mlp_state[0].astype(BF16)
    group = gather_rows(low[:half_rows], path_a) + gather_rows(low[half_rows:], path_b)
    mlp_new = polynomial([group], mlp_master, mlp_state, mlp_rate)
    low = attn_state.astype(BF16)
    groups = [gather_rows(low[0], path_a), gather_rows(low[1], path_b)]
    attn_new = polynomial(groups, attn_master, attn_state, attn_rate)
    vec_moment = MOMENTUM * vec_momentum + vec_sum
    vec_new = vectors - VEC_RATE * vec_moment
    head_moment = MOMENTUM * head_momentum + head_sum
    head_new = head_master - HEAD_RATE * head_moment
    return (
        prediction,
        features_grad,
        penalty,
        attn_moment,
        attn_new,
        mlp_moment,
        mlp_new,
        vec_moment,
        vec_new,
        head_moment,
        head_new,
    )


def solution(mesh):
    return jax.shard_map(
        local,
        mesh=mesh,
        in_specs=(
            P(("dp", "rep"), None),
            P(("dp", "rep"), None),
            P("dp"),
            P("dp"),
            P("rep", "dp", None),
            P("rep", "dp", None),
            P("rep", "dp", None),
            P("rep", "dp", None),
            P(),
            P(),
            P(),
            P(),
        ),
        out_specs=(
            P(("dp", "rep"), None),
            P(("dp", "rep"), None),
            P(),
            P("rep", "dp", None),
            P("rep", "dp", None),
            P("rep", "dp", None),
            P("rep", "dp", None),
            P(),
            P(),
            P(),
            P(),
        ),
        check_vma=False,
    )
```

```python
import functools

import jax
import jax.numpy as jnp
from jax import lax
from jax.experimental import pallas as pl
from jax.experimental.pallas import tpu as pltpu
from jax.sharding import PartitionSpec as P

D = 768
HEADS = 12
HDIM = 64
FF = 3072
LAYERS = 2
MODEL_NUMBER = 3
TILE_CELLS = 32
NLEAD = 8
NS_STEPS = 2


EPS = 1e-05
NEG = -1e30
MOMENTUM = 0.95
COEF_A = 3.4445
COEF_B = -4.775
COEF_C = 2.0315
PENALTY = 0.5
VEC_RATE = 1000.0
HEAD_RATE = 300.0
DECAY = 0.01
ATTN_RATES = (1.0, 1.0, 1.0, 4.0)
MLP_RATES = (2.0, 1.0)


def norm_parts(hidden):
    centred = hidden - jnp.mean(hidden, -1, keepdims=True)
    variance = jnp.mean(centred * centred, -1, keepdims=True)
    inverse = lax.rsqrt(variance + EPS)
    return (centred * inverse, inverse)


def norm_back(grad_out, normed, inverse, gain):
    scaled = grad_out * gain
    mean_one = jnp.mean(scaled, -1, keepdims=True)
    mean_two = jnp.mean(scaled * normed, -1, keepdims=True)
    grad_in = inverse * (scaled - mean_one - normed * mean_two)
    return (grad_in, jnp.sum(grad_out * normed, 0), jnp.sum(grad_out, 0))


ROOT_TWO_OVER_PI = 0.7978845608028654
CUBE = 0.044715
VEC_ROWS = 20
VMEM = pl.BlockSpec(memory_space=pltpu.VMEM)
SMEM = pl.BlockSpec(memory_space=pltpu.SMEM)
IN_HBM = pl.BlockSpec(memory_space=pltpu.HBM)
BF16 = jnp.bfloat16
F32 = jnp.float32


def shape_of(*dims, dtype=F32):
    return jax.ShapeDtypeStruct(dims, dtype)


def limits(mib):
    return pltpu.CompilerParams(vmem_limit_bytes=mib * 1024 * 1024)


def dot_nn(left, right):
    return jnp.dot(left, right, preferred_element_type=F32)


def dot_nt(left, right):
    return lax.dot_general(left, right, (((1,), (1,)), ((), ())), preferred_element_type=F32)


def dot_tn(left, right):
    return lax.dot_general(left, right, (((0,), (0,)), ((), ())), preferred_element_type=F32)


def column_sum(value):
    return jnp.sum(value, 0, keepdims=True)


def add_low(keep, arrived):
    return (keep.astype(F32) + arrived.astype(F32)).astype(BF16)


def start_all(copies):
    for copy in copies:
        copy.start()


def wait_all(copies):
    for copy in copies:
        copy.wait()


def attn_copies(refs, ids, rows, me, wanted, store, sems):
    result = []
    count = 0
    for place_at, (path, mat) in enumerate(wanted):
        copies = []
        for ref, ref_ids in zip(refs[path], ids[path]):
            for at, i in enumerate(ref_ids):
                first = pl.multiple_of((me ^ i) * rows, rows)
                copies.append(
                    pltpu.make_async_copy(
                        ref.at[at, mat], store.at[place_at, pl.ds(first, rows)], sems.at[count]
                    )
                )
                count += 1
        result.append(copies)
    return result


def mlp_copies(refs, plan, store, sems):
    result = []
    count = 0
    for chunk, parts in enumerate(plan):
        pair = []
        for mat in range(2):
            copies = []
            first = chunk * CHUNK
            for path, piece, at, start, rows in parts:
                copies.append(
                    pltpu.make_async_copy(
                        refs[path][piece].at[at, mat, pl.ds(start, rows)],
                        store.at[mat, pl.ds(first, rows)],
                        sems.at[count],
                    )
                )
                first += rows
                count += 1
            pair.append(copies)
        result.append(pair)
    return result


CHUNK = 384


def split_refs(refs, sizes):
    out = []
    at = 0
    for size in sizes:
        out.append(refs[at : at + size])
        at += size
    assert at == len(refs)
    return out


def select_matrix(source):
    rows = lax.broadcasted_iota(jnp.int32, (D, D), 0)
    return (rows == source).astype(F32).astype(BF16)


def qkv_kernel(ids, rows, info, hidden, vec, source, *refs):
    sizes = [len(ids[0]), len(ids[1]), 4, 2]
    path_a, path_b, (own, other, queries, pair), (store, sems) = split_refs(refs, sizes)
    copies = attn_copies((path_a, path_b), ids, rows, info[0], ((0, 0), (0, 1), (1, 0)), store, sems)
    for group in copies:
        start_all(group)
    lead_row = 12 + info[2] - 1
    normed, _ = norm_parts(hidden[...].astype(F32))
    mixed = (normed * vec[0:1] + vec[1:2] + vec[pl.ds(lead_row, 1)]).astype(BF16)
    moved = dot_nn(mixed, select_matrix(source[...])).astype(BF16)
    own[...] = moved[:, : D // 2]
    other[...] = moved[:, D // 2 :]
    wait_all(copies[0])
    queries[...] = (dot_nn(mixed, store[0]) + vec[2:3]).astype(BF16)
    wait_all(copies[1])
    pair[:, :D] = dot_nn(mixed, store[1]).astype(BF16)
    wait_all(copies[2])
    pair[:, D:] = (dot_nn(mixed, store[2]) + vec[3:4]).astype(BF16)


def valid_row(quarter, count, rows, total):
    at = lax.broadcasted_iota(jnp.int32, (1, total), 1)
    block = jnp.zeros((1, total), jnp.int32)
    for step in range(1, total // rows):
        block = block + (at >= step * rows).astype(jnp.int32)
    return ((quarter ^ block) - block) * rows + at < count


def head_mask(sub, rows):
    lanes = lax.broadcasted_iota(jnp.int32, (rows, 2 * HDIM), 1)
    return (lanes < HDIM) if sub == 0 else (lanes >= HDIM)


def attend_kernel(ids, rows, info, hidden, vec, source, queries, *refs):
    sizes = [2, len(ids[0]), len(ids[1]), 5, 3]
    pairs, path_a, path_b, (own, other, log_total, mid, mlp_in), (store, joined, sems) = split_refs(refs, sizes)
    copies = attn_copies((path_a, path_b), ids, rows, info[0], ((1, 1),), store, sems)
    start_all(copies[0])
    count = queries.shape[0]
    total = count * len(pairs)
    valid = valid_row(info[3], info[1], count, total)
    log_total[...] = jnp.zeros_like(log_total)
    for pair in range(HEADS // 2):
        lanes = slice(2 * HDIM * pair, 2 * HDIM * (pair + 1))
        shifted = slice(D + 2 * HDIM * pair, D + 2 * HDIM * (pair + 1))
        query = queries[:, lanes] * jnp.asarray(HDIM ** (-0.5), BF16)
        keys = jnp.concatenate([ref[:, lanes] for ref in pairs], 0)
        values = jnp.concatenate([ref[:, shifted] for ref in pairs], 0)
        outs = []
        for sub in range(2):
            mask = head_mask(sub, count)
            scores = dot_nt(jnp.where(mask, query, jnp.zeros_like(query)), keys)
            scores = jnp.where(valid, scores, NEG)
            top = jnp.max(scores, -1, keepdims=True)
            expo = jnp.exp(scores - top)
            sums = jnp.sum(expo, -1, keepdims=True)
            probs = (expo * (1.0 / sums)).astype(BF16)
            outs.append(dot_nn(probs, values))
            head = 2 * pair + sub
            log_total[:, head : head + 1] = top + jnp.log(sums)
        joined[:, lanes] = jnp.where(head_mask(0, count), outs[0], outs[1]).astype(BF16)
    attended = joined[...]
    moved = dot_nn(attended, select_matrix(source[...])).astype(BF16)
    own[...] = moved[:, : D // 2]
    other[...] = moved[:, D // 2 :]
    wait_all(copies[0])
    hidden_mid = hidden[...].astype(F32) + dot_nn(attended, store[0]) + vec[4:5]
    mid[...] = hidden_mid
    normed, _ = norm_parts(hidden_mid)
    mlp_in[...] = (normed * vec[5:6] + vec[6:7]).astype(BF16)


def gelu_parts(value):
    inner = ROOT_TWO_OVER_PI * (value + CUBE * (value * value * value))
    return jnp.tanh(inner)


def mlp_kernel(sizes, plan, chunk_ids, info, mid, mlp_in, vec, up_bias, *refs):
    count_a, count_b = sizes
    path_a, path_b, outs, (store, sems) = split_refs(refs, [count_a, count_b, 5, 2])
    hidden, hidden_low, pre_act, act_own, act_other = outs
    copies = mlp_copies((path_a, path_b), plan, store, sems)
    for pair in copies:
        start_all(pair[0])
        start_all(pair[1])
    total = mid[...] + vec[7:8]
    given = mlp_in[...]
    chunks = len(plan)
    for chunk in range(chunks):
        at = slice(chunk * CHUNK, (chunk + 1) * CHUNK)
        wait_all(copies[chunk][0])
        bias = up_bias[pl.ds(info[0] ^ chunk_ids[chunk], 1)].reshape(1, CHUNK)
        value = dot_nt(given, store[0, at]) + bias
        pre_act[:, at] = value
        active = (value * (0.5 * (1.0 + gelu_parts(value)))).astype(BF16)
        if chunk < chunks // 2:
            act_own[:, at] = active
        else:
            act_other[:, (chunk - chunks // 2) * CHUNK : (chunk - chunks // 2 + 1) * CHUNK] = active
        wait_all(copies[chunk][1])
        total = total + dot_nn(active, store[1, at])
    hidden[...] = total
    hidden_low[...] = total.astype(BF16)


def head_kernel(info, scale, hidden, tiles, vec, head_bias, head, *outs):
    prediction, head_grad, grad_hidden, sums = outs
    gain = vec[0:1]
    count = hidden.shape[0]
    normed, inverse = norm_parts(hidden[...])
    final_in = (normed * gain + vec[1:2]).astype(BF16)
    low = head[...].astype(BF16)
    out = dot_nn(final_in, low) + head_bias[...]
    lanes = lax.broadcasted_iota(jnp.int32, out.shape, 1)
    last = lanes >= MODEL_NUMBER * TILE_CELLS

    def over(value, join):
        result = value
        for step in range(1, MODEL_NUMBER + 1):
            result = join(result, pltpu.roll(value, step * TILE_CELLS, 1))
        return result

    def add(left, right):
        return left + right

    record = tiles[...]
    logits = jnp.where(last, NEG, out)
    shifted = logits - over(logits, jnp.maximum)
    log_gate = shifted - jnp.log(over(jnp.exp(shifted), add))
    gate = jnp.where(last, 0.0, jnp.exp(log_gate))
    blend = over(gate * record, add)
    estimate = blend + over(jnp.where(last, out, 0.0), add)
    error = estimate - over(jnp.where(last, record, 0.0), add)
    entropy = over(gate * log_gate, add)
    row_ids = info[3] * count + lax.broadcasted_iota(jnp.int32, (count, 1), 0)
    valid = (row_ids < info[1]).astype(F32)
    weight = valid * info[2].astype(F32)
    share = weight * scale[0]
    factor = share * error
    grads = gate * (factor * (record - blend) + PENALTY * share * (log_gate - entropy))
    grads = jnp.where(last, factor, grads).astype(BF16)
    prediction[...] = (estimate * valid)[:, :TILE_CELLS]
    head_rows = dot_tn(final_in, grads)
    for at in range(0, D, 128):
        head_grad[:, at : at + 128] = head_rows[at : at + 128]
    grad_final = dot_nt(grads, low)
    grad_in, gain_grad, bias_grad = norm_back(grad_final, normed, inverse, gain)
    grad_hidden[...] = grad_in
    sums[...] = jnp.zeros_like(sums)
    sums[0:1] = gain_grad[None]
    sums[1:2] = bias_grad[None]
    sums[2:3, :128] = column_sum(grads.astype(F32))
    sums[3:4, :128] = column_sum(jnp.where(lanes < TILE_CELLS, weight * entropy, 0.0))


def mlp_back_kernel(ids, rows, sizes, plan, chunk_ids, info, grad, mid, pre_act, vec, *refs):
    groups = [sizes[0], sizes[1], len(ids[0]), len(ids[1]), 8, 4]
    mlp_a, mlp_b, path_a, path_b, outs, scratch = split_refs(refs, groups)
    grad_low, pre_own, pre_other, grad_mid, grad_branch, grad_attended, up_bias_grad, sums = outs
    store, out_store, sems, out_sems = scratch
    copies = mlp_copies((mlp_a, mlp_b), plan, store, sems)
    for pair in copies:
        start_all(pair[1])
        start_all(pair[0])
    out_copies = attn_copies((path_a, path_b), ids, rows, info[0], ((1, 1),), out_store, out_sems)
    start_all(out_copies[0])
    upper = grad[...].astype(F32)
    low = upper.astype(BF16)
    grad_low[...] = low
    total = jnp.zeros(upper.shape, F32)
    chunks = len(plan)
    for chunk in range(chunks):
        at = slice(chunk * CHUNK, (chunk + 1) * CHUNK)
        wait_all(copies[chunk][1])
        grad_active = dot_nt(low, store[1, at])
        value = pre_act[:, at]
        tanh = gelu_parts(value)
        slope = 0.5 * (1.0 + tanh) + (0.5 * ROOT_TWO_OVER_PI) * value * (1.0 - tanh * tanh) * (
            1.0 + (3.0 * CUBE) * (value * value)
        )
        grad_pre = (grad_active * slope).astype(BF16)
        if chunk < chunks // 2:
            pre_own[:, at] = grad_pre
        else:
            pre_other[:, (chunk - chunks // 2) * CHUNK : (chunk - chunks // 2 + 1) * CHUNK] = grad_pre
        up_bias_grad[pl.ds(info[0] ^ chunk_ids[chunk], 1)] = column_sum(grad_pre.astype(F32)).reshape(1, 1, CHUNK)
        wait_all(copies[chunk][0])
        total = total + dot_nn(grad_pre, store[0, at])
    normed, inverse = norm_parts(mid[...])
    grad_norm, gain_grad, bias_grad = norm_back(total, normed, inverse, vec[5:6])
    grad_sum = upper + grad_norm
    grad_mid[...] = grad_sum
    branch = grad_sum.astype(BF16)
    grad_branch[...] = branch
    sums[...] = jnp.zeros_like(sums)
    sums[0:1] = column_sum(branch.astype(F32))
    sums[1:2] = gain_grad[None]
    sums[2:3] = bias_grad[None]
    sums[3:4] = column_sum(low.astype(F32))
    wait_all(out_copies[0])
    grad_attended[...] = dot_nt(branch, out_store[0]).astype(BF16)


def attend_back_kernel(info, queries, grad_attended, log_total, *refs):
    pairs, outs = split_refs(refs, [2, 3])
    grad_queries, keep, send = outs
    count = queries.shape[0]
    total = count * len(pairs)
    valid = valid_row(info[3], info[1], count, total)
    scale = HDIM ** (-0.5)
    for pair in range(HEADS // 2):
        lanes = slice(2 * HDIM * pair, 2 * HDIM * (pair + 1))
        shifted = slice(D + 2 * HDIM * pair, D + 2 * HDIM * (pair + 1))
        query = queries[:, lanes] * jnp.asarray(scale, BF16)
        grad = grad_attended[:, lanes]
        query_t = query.astype(F32).T.astype(BF16)
        grad_t = grad.astype(F32).T.astype(BF16)
        keys = jnp.concatenate([ref[:, lanes] for ref in pairs], 0)
        values = jnp.concatenate([ref[:, shifted] for ref in pairs], 0)
        outs_q, outs_k, outs_v = [], [], []
        for sub in range(2):
            mask = head_mask(sub, count)
            head = 2 * pair + sub
            rows = slice(HDIM * sub, HDIM * (sub + 1))
            zero = jnp.zeros_like(query)
            scores = dot_nt(jnp.where(mask, query, zero), keys)
            scores = jnp.where(valid, scores, NEG)
            probs = jnp.exp(scores - log_total[:, head : head + 1])
            grad_probs = dot_nt(jnp.where(mask, grad, zero), values)
            row_dot = jnp.sum(probs * grad_probs, -1, keepdims=True)
            grad_scores = (probs * (grad_probs - row_dot)).astype(BF16)
            outs_q.append(dot_nn(grad_scores, keys))
            outs_k.append(dot_nn(query_t[rows], grad_scores))
            outs_v.append(dot_nn(grad_t[rows], probs.astype(BF16)))
        grad_queries[:, lanes] = (jnp.where(head_mask(0, count), outs_q[0], outs_q[1]) * scale).astype(BF16)
        for where, outs_t in ((lanes, outs_k), (shifted, outs_v)):
            part = jnp.concatenate(outs_t, 0).T.astype(BF16)
            keep[:, where] = part[:count]
            send[:, where] = part[count:]


def qkv_back_kernel(ids, rows, info, grad_queries, keep, arrived, hidden, grad_mid, vec, *refs):
    groups = [len(ids[0]), len(ids[1]), 4, 2]
    path_a, path_b, outs, (store, sems) = split_refs(refs, groups)
    grad_hidden, hidden_low, grad_pair, sums = outs
    copies = attn_copies((path_a, path_b), ids, rows, info[0], ((0, 0), (0, 1), (1, 0)), store, sems)
    for group in copies:
        start_all(group)
    pair = add_low(keep[...], arrived[...])
    grad_pair[...] = pair
    grad_q = grad_queries[...]
    wait_all(copies[0])
    total = dot_nt(grad_q, store[0])
    wait_all(copies[1])
    total = total + dot_nt(pair[:, :D], store[1])
    wait_all(copies[2])
    total = total + dot_nt(pair[:, D:], store[2])
    normed, inverse = norm_parts(hidden[...].astype(F32))
    grad_norm, gain_grad, bias_grad = norm_back(total, normed, inverse, vec[0:1])
    result = grad_mid[...] + grad_norm
    grad_hidden[...] = result
    hidden_low[...] = result.astype(BF16)
    sums[...] = jnp.zeros_like(sums)
    sums[0:1] = gain_grad[None]
    sums[1:2] = bias_grad[None]
    sums[2:3] = column_sum(grad_q.astype(F32))
    sums[3:4] = column_sum(pair[:, D:].astype(F32))
    lead = lax.broadcasted_iota(jnp.int32, (NLEAD, D), 0) == info[2] - 1
    sums[8:] = jnp.where(lead, bias_grad[None], 0.0)


def reversed_bits(value, width):
    return sum(((value >> bit) & 1) << (width - 1 - bit) for bit in range(width))


def place_parts(value, blocks, width, mat, path, start, outs):
    at, rows = blocks
    at = at if path == 0 else reversed_bits(at, width)
    half = 1 << (width - 1)
    keep, send = outs[path]
    ref = keep if at < half else send
    ref[at % half, mat, start : start + rows] = value


def keep_earlier(info, earlier, outs, compute):
    if not earlier:
        compute()
        return
    later = info[4] == 1

    @pl.when(later)
    def _():
        for value, out in zip(earlier, outs):
            out[...] = value[...]

    @pl.when(jnp.logical_not(later))
    def _():
        compute()


def mlp_weight_kernel(width, half_rows, count, info, *refs):
    ins, earlier, outs = split_refs(refs, [8, count, 4])
    keep_earlier(info, earlier, outs, lambda: mlp_weight_body(width, half_rows, ins, outs))


def mlp_weight_body(width, half_rows, ins, outs):
    act, act_far, pre, pre_far, grad, grad_far, given, given_far = ins
    paths = (outs[:2], outs[2:])
    grad_two = jnp.concatenate([grad[...], grad_far[...]], 0)
    given_two = jnp.concatenate([given[...], given_far[...]], 0)
    rows = 2 * half_rows
    for at in range(1 << width):
        lanes = slice(at * rows, (at + 1) * rows)
        for mat, near, far, right in ((0, pre, pre_far, given_two), (1, act, act_far, grad_two)):
            left = jnp.concatenate([near[:, lanes], far[:, lanes]], 0)
            value = dot_tn(left, right).astype(BF16)
            for path in range(2):
                part = value[path * half_rows : (path + 1) * half_rows]
                place_parts(part, (at, half_rows), width, mat, path, 0, paths)


def attn_weight_kernel(width, rows, count, info, *refs):
    ins, earlier, outs = split_refs(refs, [10, count, 4])
    keep_earlier(info, earlier, outs, lambda: attn_weight_body(width, rows, ins, outs))


def attn_weight_body(width, rows, ins, outs):
    mixed, mixed_far, att, att_far, grad_q, grad_q_far, pair, pair_far, branch, branch_far = ins
    paths = (outs[:2], outs[2:])
    mixed_two = jnp.concatenate([mixed[...], mixed_far[...]], 0)
    att_two = jnp.concatenate([att[...], att_far[...]], 0)
    jobs = (
        (0, 0, mixed_two, jnp.concatenate([grad_q[...], grad_q_far[...]], 0)),
        (0, 1, mixed_two, jnp.concatenate([pair[:, :D], pair_far[:, :D]], 0)),
        (1, 0, mixed_two, jnp.concatenate([pair[:, D:], pair_far[:, D:]], 0)),
        (1, 1, att_two, jnp.concatenate([branch[...], branch_far[...]], 0)),
    )
    for path, mat, left, right in jobs:
        value = dot_tn(left, right).astype(BF16)
        for at in range(1 << width):
            place_parts(value[at * rows : (at + 1) * rows], (at, rows), width, mat, path, 0, paths)


def polynomial_kernel(pieces, rate, *refs):
    mats = len(pieces)
    ins, (master, state, new), scratch = split_refs(refs, [sum(pieces), 3, 5])
    gram, low, mix, cross, moved = scratch
    block = D // 3
    spots = range(0, D, block)
    at_piece = 0
    for mat in range(mats):
        mine = ins[at_piece : at_piece + pieces[mat]]
        at_piece += pieces[mat]
        trace = jnp.zeros((), F32)
        for spot in spots:
            at = slice(spot, spot + block)
            total = jnp.zeros((block, D), F32)
            for ref in mine:
                total = total + dot_tn(ref[:, at], ref[...])
            gram[at] = total
            hot = lax.broadcasted_iota(jnp.int32, (block, D), 0) + spot == lax.broadcasted_iota(
                jnp.int32, (block, D), 1
            )
            trace = trace + jnp.sum(jnp.where(hot, total, 0.0))
        factor = 1.0 / (jnp.sqrt(trace) + 1e-07)
        square = factor * factor
        for spot in spots:
            at = slice(spot, spot + block)
            value = gram[at] * square
            gram[at] = value
            low[at] = value.astype(BF16)
        value = state[mat] * factor
        for step in range(NS_STEPS):
            for spot in spots:
                at = slice(spot, spot + block)
                mix[at] = (COEF_B * gram[at] + COEF_C * dot_nn(low[at], low[...])).astype(BF16)
            value = COEF_A * value + dot_nn(value.astype(BF16), mix[...])
            if step + 1 < NS_STEPS:
                for spot in spots:
                    at = slice(spot, spot + block)
                    moved[at] = dot_nn(mix[at], low[...])
                    cross[at] = moved[at].astype(BF16)
                for spot in spots:
                    at = slice(spot, spot + block)
                    result = (
                        (COEF_A * COEF_A) * gram[at]
                        + (2.0 * COEF_A) * moved[at]
                        + dot_nn(mix[at], cross[...])
                    )
                    gram[at] = result
                for spot in spots:
                    at = slice(spot, spot + block)
                    low[at] = gram[at].astype(BF16)
        new[mat] = master[mat] * (1.0 - rate[mat] * DECAY) - rate[mat] * value


def swap_dp(value, bit):
    size = lax.axis_size("dp")
    return lax.ppermute(value, "dp", [(i, i ^ (1 << bit)) for i in range(size)])


def swap_rep(value, mask):
    size = lax.axis_size("rep")
    return lax.ppermute(value, "rep", [(i, i ^ mask) for i in range(size)])


def link_bits():
    count = lax.axis_size("dp").bit_length() - 1
    return (list(range(1, count)), list(range(count - 1, 0, -1)))


def path_ids(order):
    ids = [0]
    for bit in order:
        ids = ids + [i | (1 << bit) for i in ids]
    return ids


def call(kernel, ins, outs, scratch=(), specs=None, mib=56, flops=0, moved=0):
    return list(pl.pallas_call(
        kernel,
        out_shape=tuple(outs),
        in_specs=specs or [VMEM] * len(ins),
        out_specs=tuple(VMEM for _ in outs),
        scratch_shapes=list(scratch),
        compiler_params=limits(mib),
        cost_estimate=pl.CostEstimate(flops=flops, bytes_accessed=moved, transcendentals=0),
    )(*ins))


def after(value, *others):
    return lax.optimization_barrier((value, others))[0]


def piece_ids(order):
    ids = [0]
    for bit in order[:-1]:
        ids = ids + [i | (1 << bit) for i in ids]
    far = [i | (1 << order[-1]) for i in ids]
    return [ids, far, [i | 1 for i in ids], [i | 1 for i in far]]


def gather_steps(firsts, orders, axis=0):
    nears = firsts
    for step in range(len(orders[0]) - 1):
        arrived = [swap_dp(near, order[step]) for near, order in zip(nears, orders)]
        ties = yield nears
        nears = [
            jnp.concatenate([near, after(value, *ties)], axis)
            for near, value in zip(nears, arrived)
        ]
    arrived = [swap_dp(near, order[-1]) for near, order in zip(nears, orders)]
    others = [swap_dp(near, 0) for near in nears]
    ties = yield nears
    fars = [after(value, *ties) for value in arrived]
    ends = [swap_dp(far, 0) for far in fars]
    yield fars
    yield [list(value) for value in zip(nears, fars, others, ends)]


def natural(pieces, ids):
    me = lax.axis_index("dp")
    flat = [i for group in ids for i in group]
    slot = [0] * len(flat)
    for at, i in enumerate(flat):
        slot[i] = at
    joined = jnp.concatenate(pieces, 0)
    wanted = jnp.asarray(slot, jnp.int32)[jnp.arange(len(flat)) ^ me]
    taken = jnp.take(joined, wanted, axis=0)
    mats, width = taken.shape[1], taken.shape[3]
    return taken.transpose(1, 0, 2, 3).reshape(1, mats, -1, width)


def scatter_steps(parts, orders, join):
    low = lax.axis_index("rep") & 1
    keeps, sends = [parts[0], parts[2]], [parts[1], parts[3]]
    values = keeps
    for step in range(len(orders[0])):
        arrived = [swap_dp(send, order[step]) for send, order in zip(sends, orders)]
        ties = yield values
        values = [add_low(keep, after(value, *ties)) for keep, value in zip(keeps, arrived)]
        half = values[0].shape[0] // 2
        keeps = [value[:half] for value in values]
        sends = [value[half:] for value in values]
    pair = join([value[0] for value in values])
    keep = lax.dynamic_index_in_dim(pair, low, 0, keepdims=False)
    arrived = swap_rep(lax.dynamic_index_in_dim(pair, 1 - low, 0, keepdims=False), 1)
    ties = yield keep
    yield keep.astype(F32) + after(arrived, *ties).astype(F32)


def sum_steps(rows):
    core = lax.axis_index("dp") & 1
    high = lax.axis_index("rep") >> 1
    half = rows.shape[0] // 2
    total = lax.dynamic_slice_in_dim(rows, core * half, half, 0)
    swaps = [functools.partial(swap_dp, bit=bit) for bit in link_bits()[0]]
    swaps.append(functools.partial(swap_rep, mask=1))
    arrived = swap_dp(lax.dynamic_slice_in_dim(rows, (1 - core) * half, half, 0), 0)
    for swap in swaps:
        ties = yield total
        total = total + after(arrived, *ties)
        arrived = swap(total)
    ties = yield total
    total = total + after(arrived, *ties)
    arrived = swap_rep(total, 2)
    ties = yield total
    other = after(arrived, *ties)
    both = jnp.where(high == 0, jnp.stack([total, other]), jnp.stack([other, total]))
    arrived = swap_dp(both, 0)
    ties = yield both
    other = after(arrived, *ties)
    first = jnp.where(core == 0, both, other)
    second = jnp.where(core == 0, other, both)
    yield jnp.concatenate([first, second], 1)


class Steps:
    def __init__(self, steps):
        self.steps = steps
        self.last = next(steps)

    def go(self, *ties):
        self.last = self.steps.send(ties)
        return self.last

    def finish(self, *ties):
        try:
            while True:
                self.go(*ties)
        except StopIteration:
            return self.last


def local(
    features,
    tile_records,
    patch_counts,
    lead_counts,
    attn_master,
    attn_momentum,
    mlp_master,
    mlp_momentum,
    vectors,
    vec_momentum,
    head_master,
    head_momentum,
):
    rep_size = lax.axis_size("rep")
    dp_size = lax.axis_size("dp")
    me = lax.axis_index("dp")
    core = me & 1
    rep = lax.axis_index("rep")
    rep_low = rep & 1
    rep_high = rep >> 1
    quarter_rows = features.shape[0]
    count = 2 * quarter_rows
    attn_rows = attn_master.shape[1]
    mlp_rows = mlp_master.shape[1]
    half_rows = mlp_rows // 2
    links = dp_size // 2
    width = links.bit_length() - 1
    paths = link_bits()
    path_a, path_b = paths
    back_orders = (path_b, path_a)
    direct = attn_rows % 16 == 0 and mlp_rows == CHUNK
    assert LAYERS == 2 and rep_size == 2 * LAYERS

    def frame_moves(upper):
        moves = ([], [])
        for d in range(dp_size):
            for r in range(rep_size):
                to = (d - d % 2 + r // 2) * rep_size + 2 * upper + d % 2
                moves[r % 2].append((d * rep_size + r, to))
        return moves

    def bring(value, upper):
        both = [lax.ppermute(value, ("dp", "rep"), pairs) for pairs in frame_moves(upper)]
        return jnp.concatenate(both, 0)

    def take_back(value, upper):
        parts = [
            lax.ppermute(
                value[at * quarter_rows : (at + 1) * quarter_rows],
                ("dp", "rep"),
                [(to, came) for came, to in pairs],
            )
            for at, pairs in enumerate(frame_moves(upper))
        ]
        return jnp.where(rep_low == 0, parts[0], parts[1])

    def up_layer(value):
        return lax.ppermute(value, "rep", [(0, 2), (1, 3)])

    def down_layer(value):
        return lax.ppermute(value, "rep", [(2, 0), (3, 1)])

    def both_owners(own, near):
        pair = jnp.stack([own, near])
        return [lax.dynamic_index_in_dim(pair, rep_low ^ i, 0, keepdims=False) for i in (0, 1)]

    attn_low = attn_master.astype(BF16)
    attn_near = swap_rep(attn_low, 1)
    features = bring(features, 0)
    mlp_low = mlp_master[0].astype(BF16)
    mlp_near = swap_rep(after(mlp_low, attn_near), 1)

    counts = jnp.concatenate([patch_counts, lead_counts]).reshape(1, 2)
    counts = jnp.concatenate([counts, swap_dp(counts, 0)], 0)
    frame_count, lead_value = lax.dynamic_index_in_dim(counts, core ^ rep_low, 0, keepdims=False)
    info = jnp.stack(
        [me if direct else 0 * me, frame_count, lead_value, core, rep_high]
    ).astype(jnp.int32)

    position = jnp.arange(D) // attn_rows
    distance = ((position % links) << 1) | (position // links)
    source = ((distance ^ me) * attn_rows + jnp.arange(D) % attn_rows).astype(jnp.int32)[None]
    order = [(at % links) << 1 | at // links for at in range(dp_size)]

    vec_rows = VEC_ROWS * LAYERS + 2
    vec_all = vectors[: vec_rows * D].reshape(vec_rows, D)
    vec = lax.dynamic_slice_in_dim(vec_all, VEC_ROWS * rep_high, VEC_ROWS, 0)
    vec_tail = vec_all[VEC_ROWS * LAYERS :]
    head_bias = vectors[vec_rows * D :].reshape(1, -1)
    chunks = FF // CHUNK
    up_bias = vec[8:12].reshape(chunks, 1, CHUNK)

    ids_a, ids_b = piece_ids(path_a), piece_ids(path_b)
    if direct:
        chunk_ids = order
        found = [
            {i: (piece, at) for piece, group in enumerate(ids) for at, i in enumerate(group)}
            for ids in (ids_a, ids_b)
        ]
        plan = [[(path, *found[path][i], 0, half_rows) for path in range(2)] for i in order]
        attn_ids = (ids_a, ids_b)
        mlp_sizes = (4, 4)
        place_rows = attn_rows
    else:
        chunk_ids = list(range(chunks))
        plan = [[(0, 0, 0, chunk * CHUNK, CHUNK)] for chunk in range(chunks)]
        attn_ids = ([[0]], [[0]])
        mlp_sizes = (1, 0)
        place_rows = D
    n_attn = sum(len(group) for group in attn_ids)
    n_mlp = sum(mlp_sizes)
    copies_each = sum(len(group) for group in attn_ids[0])
    mlp_copies_all = 2 * sum(len(parts) for parts in plan)
    dma = pltpu.SemaphoreType.DMA
    matrix = D * D
    layer_flops = 2 * count * matrix

    def mlp_rel(first, second):
        if direct:
            return first, second
        whole = jnp.concatenate([first, second], 1).reshape(count, dp_size, mlp_rows)
        whole = jnp.take(whole, jnp.asarray(order, jnp.int32) ^ me, axis=1).reshape(count, FF)
        return whole[:, : FF // 2], whole[:, FF // 2 :]

    def qkv(hidden):
        own, other, queries, pair = call(
            functools.partial(qkv_kernel, attn_ids, place_rows),
            [info, hidden, vec, source] + attn_pieces,
            [
                shape_of(count, D // 2, dtype=BF16),
                shape_of(count, D // 2, dtype=BF16),
                shape_of(count, D, dtype=BF16),
                shape_of(count, 2 * D, dtype=BF16),
            ],
            [pltpu.VMEM((3, D, D), BF16), dma((3 * copies_each,))],
            [SMEM, VMEM, VMEM, VMEM] + [IN_HBM] * n_attn,
            flops=4 * layer_flops,
            moved=6 * matrix + 4 * count * D * 4,
        )
        return [hidden, own, other, queries, [pair, swap_dp(pair, 0)]]

    def attend(saved):
        return saved + call(
            functools.partial(attend_kernel, attn_ids, place_rows),
            [info, saved[0], vec, source, saved[3]] + saved[4] + attn_pieces,
            [
                shape_of(count, D // 2, dtype=BF16),
                shape_of(count, D // 2, dtype=BF16),
                shape_of(count, 128),
                shape_of(count, D),
                shape_of(count, D, dtype=BF16),
            ],
            [pltpu.VMEM((1, D, D), BF16), pltpu.VMEM((count, D), BF16), dma((copies_each,))],
            [SMEM, VMEM, VMEM, VMEM] + [VMEM] * 3 + [IN_HBM] * n_attn,
            flops=8 * layer_flops,
            moved=2 * matrix + count * D * 8,
        )

    def feed(saved):
        outs = call(
            functools.partial(mlp_kernel, mlp_sizes, plan, chunk_ids),
            [info, saved[8], saved[9], vec, up_bias] + mlp_pieces,
            [
                shape_of(count, D),
                shape_of(count, D, dtype=BF16),
                shape_of(count, FF),
                shape_of(count, FF // 2, dtype=BF16),
                shape_of(count, FF // 2, dtype=BF16),
            ],
            [pltpu.VMEM((2, FF, D), BF16), dma((mlp_copies_all,))],
            [SMEM] + [VMEM] * 4 + [IN_HBM] * n_mlp,
            flops=8 * layer_flops,
            moved=4 * FF * D + count * FF * 6,
        )
        return outs[0], outs[1], saved + outs[2:]

    def mlp_back(saved, grad):
        return call(
            functools.partial(mlp_back_kernel, attn_ids, place_rows, mlp_sizes, plan, chunk_ids),
            [info, grad, saved[8], saved[10], vec] + mlp_pieces + attn_pieces,
            [
                shape_of(count, D, dtype=BF16),
                shape_of(count, FF // 2, dtype=BF16),
                shape_of(count, FF // 2, dtype=BF16),
                shape_of(count, D),
                shape_of(count, D, dtype=BF16),
                shape_of(count, D, dtype=BF16),
                shape_of(chunks, 1, CHUNK),
                shape_of(8, D),
            ],
            [
                pltpu.VMEM((2, FF, D), BF16),
                pltpu.VMEM((1, D, D), BF16),
                dma((mlp_copies_all,)),
                dma((copies_each,)),
            ],
            [SMEM] + [VMEM] * 4 + [IN_HBM] * (n_mlp + n_attn),
            flops=9 * layer_flops,
            moved=4 * FF * D + 2 * matrix + count * FF * 6,
        )

    def attend_back(saved, grad_attended):
        grad_queries, keep, send = call(
            attend_back_kernel,
            [info, saved[3], grad_attended, saved[7]] + saved[4],
            [
                shape_of(count, D, dtype=BF16),
                shape_of(count, 2 * D, dtype=BF16),
                shape_of(count, 2 * D, dtype=BF16),
            ],
            (),
            [SMEM] + [VMEM] * 5,
            flops=20 * layer_flops,
            moved=count * D * 16,
        )
        return grad_queries, keep, swap_dp(send, 0)

    def qkv_back(saved, grad_queries, keep, arrived, grad_mid):
        return call(
            functools.partial(qkv_back_kernel, attn_ids, place_rows),
            [info, grad_queries, keep, arrived, saved[0], grad_mid, vec] + attn_pieces,
            [
                shape_of(count, D),
                shape_of(count, D, dtype=BF16),
                shape_of(count, 2 * D, dtype=BF16),
                shape_of(8 + NLEAD, D),
            ],
            [pltpu.VMEM((3, D, D), BF16), dma((3 * copies_each,))],
            [SMEM] + [VMEM] * 6 + [IN_HBM] * n_attn,
            flops=3 * layer_flops,
            moved=6 * matrix + count * D * 20,
        )

    flipped = jnp.asarray([reversed_bits(at, width) for at in range(links)], jnp.int32)

    def mlp_weights(saved, back, earlier, *ties):
        near_pre, other_pre = mlp_rel(back[1], back[2])
        near_act, other_act = mlp_rel(saved[11], saved[12])
        ins = [after(near_act, *ties), swap_dp(other_act, 0), near_pre, swap_dp(other_pre, 0)]
        ins += [back[0], swap_dp(back[0], 0), saved[9], swap_dp(saved[9], 0)]
        if direct:
            part = shape_of(links // 2, 2, half_rows, D, dtype=BF16)
            return call(
                functools.partial(mlp_weight_kernel, width, half_rows, len(earlier)),
                [info] + ins + earlier,
                [part] * 4,
                specs=[SMEM] + [VMEM] * (8 + len(earlier)),
                flops=8 * layer_flops,
                moved=4 * FF * D + count * FF * 8,
            )
        lefts = [jnp.concatenate(ins[2:4], 0), jnp.concatenate(ins[:2], 0)]
        rights = [jnp.concatenate(ins[6:], 0), jnp.concatenate(ins[4:6], 0)]
        both = jnp.stack([dot_tn(l, r).astype(BF16) for l, r in zip(lefts, rights)])
        both = both.reshape(2, links, 2, half_rows, D).transpose(2, 1, 0, 3, 4)
        return choose([both[0], jnp.take(both[1], flipped, axis=0)], earlier)

    def choose(paths_of, earlier):
        half = links // 2
        parts = [part for path in paths_of for part in (path[:half], path[half:])]
        if earlier:
            parts = [jnp.where(rep_high == 1, old, new) for old, new in zip(earlier, parts)]
        return parts

    def attn_weights(saved, grad_queries, grad_pair, branch, earlier, *ties):
        ins = [after(saved[1], *ties), swap_dp(saved[2], 0), saved[5], swap_dp(saved[6], 0)]
        for value in (grad_queries, grad_pair, branch):
            ins += [value, swap_dp(value, 0)]
        if direct:
            part = shape_of(links // 2, 2, attn_rows, D, dtype=BF16)
            return call(
                functools.partial(attn_weight_kernel, width, attn_rows, len(earlier)),
                [info] + ins + earlier,
                [part] * 4,
                specs=[SMEM] + [VMEM] * (10 + len(earlier)),
                flops=4 * layer_flops,
                moved=4 * matrix + count * D * 16,
            )
        mixed_two, att_two, q_two, pair_two, branch_two = (
            jnp.concatenate(ins[at : at + 2], 0) for at in (0, 2, 4, 6, 8)
        )
        jobs = [(mixed_two, q_two), (mixed_two, pair_two[:, :D])]
        jobs += [(mixed_two, pair_two[:, D:]), (att_two, branch_two)]
        grads = [dot_tn(l, r).astype(BF16).reshape(links, attn_rows, D) for l, r in jobs]
        second = jnp.take(jnp.stack(grads[2:], 1), flipped, axis=0)
        return choose([jnp.stack(grads[:2], 1), second], earlier)

    def rows_of(qkv_sums, back):
        return jnp.concatenate(
            [qkv_sums, back[7], jnp.pad(back[6].reshape(4, D), ((0, 4), (0, 0)))], 0
        )

    attn_all = Steps(
        gather_steps([value[None] for value in both_owners(attn_low, attn_near)], paths)
    )
    both = jnp.stack(both_owners(mlp_low, after(mlp_near, attn_all.last)))
    tie = attn_all.go(both)
    mlp_all = Steps(
        gather_steps([both[None, :, :half_rows], both[None, :, half_rows:]], paths)
    )
    tie = attn_all.go(mlp_all.last)
    ends = attn_all.finish(tie)
    if direct:
        attn_pieces = ends[0] + ends[1]
    else:
        attn_pieces = [natural(ends[0], ids_a), natural(ends[1], ids_b)]

    saved_0 = qkv(after(features, tie))
    tie = mlp_all.go(saved_0[3])
    for bit in path_a:
        counts = jnp.concatenate([counts, swap_dp(after(counts, tie), bit)], 0)
    pixel_total = (TILE_CELLS * jnp.sum(counts[:, 0] * counts[:, 1])).astype(F32)
    saved_0 = attend(saved_0)
    tie = mlp_all.go(saved_0[8])
    ends = mlp_all.finish(tie)
    if direct:
        mlp_pieces = ends[0] + ends[1]
    else:
        shape = (1, 2, dp_size, half_rows, D)
        parts = [natural(end, ids).reshape(shape) for end, ids in zip(ends, (ids_a, ids_b))]
        mlp_pieces = [jnp.concatenate(parts, 3).reshape(1, 2, FF, D)]
    _, hidden_low, saved_0 = feed(saved_0)

    tile_records = bring(after(tile_records, tie), 1)
    hidden_low = up_layer(hidden_low)
    hidden, _, saved_1 = feed(attend(qkv(hidden_low)))
    scale = (1.0 / pixel_total).reshape(1)
    prediction, head_grad, grad_hidden, head_sums = call(
        head_kernel,
        [info, scale, hidden, tile_records, vec_tail, head_bias, head_master],
        [shape_of(count, TILE_CELLS), shape_of(128, D), shape_of(count, D), shape_of(8, D)],
        (),
        [SMEM, SMEM] + [VMEM] * 5,
        flops=layer_flops,
        moved=D * 128 * 8 + count * D * 8,
    )
    back_1 = mlp_back(saved_1, grad_hidden)
    grad_q_1, keep, arrived = attend_back(saved_1, back_1[5])
    _, grad_low, grad_pair_1, sums_1 = qkv_back(saved_1, grad_q_1, keep, arrived, back_1[3])
    grad_low = down_layer(grad_low)
    mlp_grads = mlp_weights(saved_1, back_1, [], grad_pair_1)
    attn_grads = attn_weights(saved_1, grad_q_1, grad_pair_1, back_1[4], [], mlp_grads[0])
    prediction = take_back(after(prediction, attn_grads[0]), 1)

    back_0 = mlp_back(saved_0, after(grad_low, attn_grads[0]))
    grad_q_0, keep, arrived = attend_back(saved_0, back_0[5])
    mlp_grads = mlp_weights(saved_0, back_0, mlp_grads, grad_q_0)
    tie = mlp_grads[0]
    mlp_steps = Steps(scatter_steps(mlp_grads, back_orders, lambda parts: jnp.concatenate(parts, 1)))
    grad_hidden, _, grad_pair_0, sums_0 = qkv_back(
        saved_0, grad_q_0, keep, after(arrived, tie), back_0[3]
    )
    attn_grads = attn_weights(
        saved_0, grad_q_0, grad_pair_0, back_0[4], attn_grads, grad_hidden
    )
    tie = attn_grads[0]
    attn_steps = Steps(scatter_steps(attn_grads, back_orders, jnp.stack))
    layer_rows = jnp.where(rep_high == 0, rows_of(sums_0, back_0), rows_of(sums_1, back_1))
    sums = Steps(sum_steps(jnp.concatenate([head_grad, head_sums, layer_rows], 0)))
    for steps in (mlp_steps, sums, attn_steps, mlp_steps, sums, attn_steps):
        tie = steps.go(tie)
    mlp_share = mlp_steps.finish(tie)[None]
    mlp_moment = MOMENTUM * mlp_momentum + mlp_share
    mlp_state = mlp_share + MOMENTUM * mlp_moment
    low = mlp_state[0].astype(BF16)
    mlp_all = Steps(gather_steps([low[:half_rows], low[half_rows:]], paths))
    tie = sums.go(mlp_share)
    attn_share = attn_steps.finish(tie)
    attn_moment = MOMENTUM * attn_momentum + attn_share
    attn_state = attn_share + MOMENTUM * attn_moment
    low = attn_state.astype(BF16)
    attn_all = Steps(gather_steps([low[0], low[1]], paths))
    tie = mlp_all.go(attn_share)
    features_grad = take_back(after(grad_hidden, tie), 0)
    tie = sums.go(tie)
    tie = attn_all.go(tie)
    tie = mlp_all.go(tie)
    tie = attn_all.go(tie)
    mlp_all, attn_all = mlp_all.finish(tie), attn_all.finish(tie)
    tie = sums.go(tie)
    sums = sums.finish(tie)

    def layer_of(rows):
        return [rows[:4], rows[16:20], rows[24:28], rows[8:16]]

    head_sum = jnp.concatenate(
        [sums[1, :128, at : at + 128] for at in range(0, D, 128)], 0
    )
    head_sums = sums[1, 128:136]
    vec_sum = layer_of(sums[0, 136:]) + layer_of(sums[1, 136:]) + [head_sums[:2]]
    vec_sum = jnp.concatenate(
        [jnp.concatenate(vec_sum, 0).reshape(-1), head_sums[2, :128]]
    )
    penalty = jnp.sum(head_sums[3, :128]) / pixel_total

    attn_rate = jnp.asarray(ATTN_RATES, F32).reshape(2, 2)[rep_low]
    mlp_rate = jnp.asarray(MLP_RATES, F32)[rep_low].reshape(1)

    def polynomial(groups, master, state, rate):
        pieces = [piece for group in groups for piece in group]
        sizes = [len(group) for group in groups]
        square = pltpu.VMEM((D, D), F32)
        low = pltpu.VMEM((D, D), BF16)
        rows = sum(piece.shape[0] for piece in pieces)
        return call(
            functools.partial(polynomial_kernel, sizes),
            [rate] + pieces + [master, state],
            [shape_of(*master.shape)],
            [square, low, low, low, square],
            [SMEM] + [VMEM] * (len(pieces) + 2),
            flops=2 * matrix * (rows + 4 * D * len(groups)),
            moved=rows * D * 2,
        )[0]

    mlp_new = polynomial([mlp_all[0] + mlp_all[1]], mlp_master, mlp_state, mlp_rate)
    attn_new = polynomial(attn_all, attn_master, attn_state, attn_rate)
    vec_moment = MOMENTUM * vec_momentum + vec_sum
    vec_new = vectors - VEC_RATE * vec_moment
    head_moment = MOMENTUM * head_momentum + head_sum
    head_new = head_master - HEAD_RATE * head_moment
    return (
        prediction,
        features_grad,
        penalty,
        attn_moment,
        attn_new,
        mlp_moment,
        mlp_new,
        vec_moment,
        vec_new,
        head_moment,
        head_new,
    )


def solution(mesh):
    return jax.shard_map(
        local,
        mesh=mesh,
        in_specs=(
            P(("dp", "rep"), None),
            P(("dp", "rep"), None),
            P("dp"),
            P("dp"),
            P("rep", "dp", None),
            P("rep", "dp", None),
            P("rep", "dp", None),
            P("rep", "dp", None),
            P(),
            P(),
            P(),
            P(),
        ),
        out_specs=(
            P(("dp", "rep"), None),
            P(("dp", "rep"), None),
            P(),
            P("rep", "dp", None),
            P("rep", "dp", None),
            P("rep", "dp", None),
            P("rep", "dp", None),
            P(),
            P(),
            P(),
            P(),
        ),
        check_vma=False,
    )
```

```python
import functools

import jax
import jax.numpy as jnp
from jax import lax
from jax.experimental import pallas as pl
from jax.experimental.pallas import tpu as pltpu
from jax.sharding import PartitionSpec as P

D = 768
HEADS = 12
HDIM = 64
FF = 3072
LAYERS = 2
MODEL_NUMBER = 3
TILE_CELLS = 32
NLEAD = 8
NS_STEPS = 2


EPS = 1e-05
NEG = -1e30
MOMENTUM = 0.95
COEF_A = 3.4445
COEF_B = -4.775
COEF_C = 2.0315
PENALTY = 0.5
VEC_RATE = 1000.0
HEAD_RATE = 300.0
DECAY = 0.01
ATTN_RATES = (1.0, 1.0, 1.0, 4.0)
MLP_RATES = (2.0, 1.0)


def norm_parts(hidden):
    centred = hidden - jnp.mean(hidden, -1, keepdims=True)
    variance = jnp.mean(centred * centred, -1, keepdims=True)
    inverse = lax.rsqrt(variance + EPS)
    return (centred * inverse, inverse)


def norm_back(grad_out, normed, inverse, gain):
    scaled = grad_out * gain
    mean_one = jnp.mean(scaled, -1, keepdims=True)
    mean_two = jnp.mean(scaled * normed, -1, keepdims=True)
    grad_in = inverse * (scaled - mean_one - normed * mean_two)
    return (grad_in, jnp.sum(grad_out * normed, 0), jnp.sum(grad_out, 0))


ROOT_TWO_OVER_PI = 0.7978845608028654
CUBE = 0.044715
VEC_ROWS = 20
VMEM = pl.BlockSpec(memory_space=pltpu.VMEM)
SMEM = pl.BlockSpec(memory_space=pltpu.SMEM)
IN_HBM = pl.BlockSpec(memory_space=pltpu.HBM)
BF16 = jnp.bfloat16
F32 = jnp.float32


def shape_of(*dims, dtype=F32):
    return jax.ShapeDtypeStruct(dims, dtype)


def limits(mib):
    return pltpu.CompilerParams(vmem_limit_bytes=mib * 1024 * 1024)


def dot_nn(left, right):
    return jnp.dot(left, right, preferred_element_type=F32)


def dot_nt(left, right):
    return lax.dot_general(left, right, (((1,), (1,)), ((), ())), preferred_element_type=F32)


def dot_tn(left, right):
    return lax.dot_general(left, right, (((0,), (0,)), ((), ())), preferred_element_type=F32)


def column_sum(value):
    return jnp.sum(value, 0, keepdims=True)


def add_low(keep, arrived):
    return (keep.astype(F32) + arrived.astype(F32)).astype(BF16)


def start_all(copies):
    for copy in copies:
        copy.start()


def wait_all(copies):
    for copy in copies:
        copy.wait()


def attn_copies(refs, ids, rows, me, wanted, store, sems):
    result = []
    count = 0
    for place_at, (path, mat) in enumerate(wanted):
        copies = []
        for ref, ref_ids in zip(refs[path], ids[path]):
            for at, i in enumerate(ref_ids):
                first = pl.multiple_of((me ^ i) * rows, rows)
                copies.append(
                    pltpu.make_async_copy(
                        ref.at[at, mat], store.at[place_at, pl.ds(first, rows)], sems.at[count]
                    )
                )
                count += 1
        result.append(copies)
    return result


def mlp_copies(refs, plan, store, sems):
    result = []
    count = 0
    for chunk, parts in enumerate(plan):
        pair = []
        for mat in range(2):
            copies = []
            first = chunk * WIDE
            for path, piece, at, start, rows in parts:
                copies.append(
                    pltpu.make_async_copy(
                        refs[path][piece].at[at, mat, pl.ds(start, rows)],
                        store.at[mat, pl.ds(first, rows)],
                        sems.at[count],
                    )
                )
                first += rows
                count += 1
            pair.append(copies)
        result.append(pair)
    return result


CHUNK = 384
AHEAD = 2
WIDE = 2 * CHUNK


def split_refs(refs, sizes):
    out = []
    at = 0
    for size in sizes:
        out.append(refs[at : at + size])
        at += size
    assert at == len(refs)
    return out


def select_matrix(source):
    rows = lax.broadcasted_iota(jnp.int32, (D, D), 0)
    return (rows == source).astype(F32).astype(BF16)


def qkv_kernel(ids, rows, info, hidden, vec, source, *refs):
    sizes = [len(ids[0]), len(ids[1]), 4, 2]
    path_a, path_b, (own, other, queries, pair), (store, sems) = split_refs(refs, sizes)
    copies = attn_copies((path_a, path_b), ids, rows, info[0], ((0, 0), (0, 1), (1, 0)), store, sems)
    for group in copies:
        start_all(group)
    lead_row = 12 + info[2] - 1
    normed, _ = norm_parts(hidden[...].astype(F32))
    mixed = (normed * vec[0:1] + vec[1:2] + vec[pl.ds(lead_row, 1)]).astype(BF16)
    moved = dot_nn(mixed, select_matrix(source[...])).astype(BF16)
    own[...] = moved[:, : D // 2]
    other[...] = moved[:, D // 2 :]
    wait_all(copies[0])
    queries[...] = (dot_nn(mixed, store[0]) + vec[2:3]).astype(BF16)
    wait_all(copies[1])
    pair[:, :D] = dot_nn(mixed, store[1]).astype(BF16)
    wait_all(copies[2])
    pair[:, D:] = (dot_nn(mixed, store[2]) + vec[3:4]).astype(BF16)


def valid_row(quarter, count, rows, total):
    at = lax.broadcasted_iota(jnp.int32, (1, total), 1)
    block = jnp.zeros((1, total), jnp.int32)
    for step in range(1, total // rows):
        block = block + (at >= step * rows).astype(jnp.int32)
    return ((quarter ^ block) - block) * rows + at < count


def head_mask(sub, rows):
    lanes = lax.broadcasted_iota(jnp.int32, (rows, 2 * HDIM), 1)
    return (lanes < HDIM) if sub == 0 else (lanes >= HDIM)


def attend_kernel(ids, rows, info, hidden, vec, source, queries, *refs):
    sizes = [2, len(ids[0]), len(ids[1]), 5, 3]
    pairs, path_a, path_b, (own, other, log_total, mid, mlp_in), (store, joined, sems) = split_refs(refs, sizes)
    copies = attn_copies((path_a, path_b), ids, rows, info[0], ((1, 1),), store, sems)
    start_all(copies[0])
    count = queries.shape[0]
    total = count * len(pairs)
    valid = valid_row(info[3], info[1], count, total)
    log_total[...] = jnp.zeros_like(log_total)
    for pair in range(HEADS // 2):
        lanes = slice(2 * HDIM * pair, 2 * HDIM * (pair + 1))
        shifted = slice(D + 2 * HDIM * pair, D + 2 * HDIM * (pair + 1))
        query = queries[:, lanes] * jnp.asarray(HDIM ** (-0.5), BF16)
        keys = jnp.concatenate([ref[:, lanes] for ref in pairs], 0)
        values = jnp.concatenate([ref[:, shifted] for ref in pairs], 0)
        outs = []
        for sub in range(2):
            mask = head_mask(sub, count)
            scores = dot_nt(jnp.where(mask, query, jnp.zeros_like(query)), keys)
            scores = jnp.where(valid, scores, NEG)
            top = jnp.max(scores, -1, keepdims=True)
            expo = jnp.exp(scores - top)
            sums = jnp.sum(expo, -1, keepdims=True)
            probs = (expo * (1.0 / sums)).astype(BF16)
            outs.append(dot_nn(probs, values))
            head = 2 * pair + sub
            log_total[:, head : head + 1] = top + jnp.log(sums)
        joined[:, lanes] = jnp.where(head_mask(0, count), outs[0], outs[1]).astype(BF16)
    attended = joined[...]
    moved = dot_nn(attended, select_matrix(source[...])).astype(BF16)
    own[...] = moved[:, : D // 2]
    other[...] = moved[:, D // 2 :]
    wait_all(copies[0])
    hidden_mid = hidden[...].astype(F32) + dot_nn(attended, store[0]) + vec[4:5]
    mid[...] = hidden_mid
    normed, _ = norm_parts(hidden_mid)
    mlp_in[...] = (normed * vec[5:6] + vec[6:7]).astype(BF16)


def gelu_and_slope(value):
    square = value * value
    tanh = jnp.tanh(value * (ROOT_TWO_OVER_PI + (ROOT_TWO_OVER_PI * CUBE) * square))
    half = 0.5 + 0.5 * tanh
    rise = value * (ROOT_TWO_OVER_PI + (3.0 * ROOT_TWO_OVER_PI * CUBE) * square)
    return value * half, half * (1.0 + (1.0 - tanh) * rise)


def row_sum(value):
    return dot_nn(jnp.ones((8, value.shape[0]), BF16), value)[:1]


def split_copies(store, first, second, chunk, chunks, sem):
    at = chunk * WIDE
    half = chunks // 2 * WIDE
    target, spot = (first, at) if at < half else (second, at - half)
    return pltpu.make_async_copy(store.at[:, pl.ds(at, WIDE)], target.at[:, pl.ds(spot, WIDE)], sem)


def mlp_kernel(sizes, plan, chunk_ids, info, mid, mlp_in, vec, up_bias, *refs):
    count_a, count_b = sizes
    path_a, path_b, outs, scratch = split_refs(refs, [count_a, count_b, 5, 6])
    hidden, hidden_low, slopes, act_own, act_other = outs
    store, sems, slope_store, act_store, slope_sems, act_sems = scratch
    copies = mlp_copies((path_a, path_b), plan, store, sems)
    for pair in copies[:AHEAD]:
        start_all(pair[0])
        start_all(pair[1])
    total = mid[...] + vec[7:8]
    given = mlp_in[...]
    chunks = len(plan)
    sent = []
    for chunk in range(chunks):
        at = slice(chunk * WIDE, (chunk + 1) * WIDE)
        bias = [
            up_bias[pl.ds(info[0] ^ i, 1)].reshape(1, CHUNK)
            for i in chunk_ids[2 * chunk : 2 * chunk + 2]
        ]
        wait_all(copies[chunk][0])
        for pair in copies[chunk + AHEAD : chunk + AHEAD + 1]:
            start_all(pair[0])
            start_all(pair[1])
        value, slope = gelu_and_slope(dot_nt(given, store[0, at]) + jnp.concatenate(bias, 1))
        active = value.astype(BF16)
        slope_store[:, at] = slope
        act_store[:, at] = active
        span = pl.ds(chunk * WIDE, WIDE)
        out = [
            pltpu.make_async_copy(slope_store.at[:, span], slopes.at[:, span], slope_sems.at[chunk]),
            split_copies(act_store, act_own, act_other, chunk, chunks, act_sems.at[chunk]),
        ]
        start_all(out)
        sent += out
        wait_all(copies[chunk][1])
        total = total + dot_nn(active, store[1, at])
    hidden[...] = total
    hidden_low[...] = total.astype(BF16)
    wait_all(sent)


def head_kernel(info, scale, hidden, tiles, vec, head_bias, head, *outs):
    prediction, head_grad, grad_hidden, sums = outs
    gain = vec[0:1]
    count = hidden.shape[0]
    normed, inverse = norm_parts(hidden[...])
    final_in = (normed * gain + vec[1:2]).astype(BF16)
    low = head[...].astype(BF16)
    out = dot_nn(final_in, low) + head_bias[...]
    lanes = lax.broadcasted_iota(jnp.int32, out.shape, 1)
    last = lanes >= MODEL_NUMBER * TILE_CELLS

    def over(value, join):
        result = value
        for step in range(1, MODEL_NUMBER + 1):
            result = join(result, pltpu.roll(value, step * TILE_CELLS, 1))
        return result

    def add(left, right):
        return left + right

    record = tiles[...]
    logits = jnp.where(last, NEG, out)
    shifted = logits - over(logits, jnp.maximum)
    log_gate = shifted - jnp.log(over(jnp.exp(shifted), add))
    gate = jnp.where(last, 0.0, jnp.exp(log_gate))
    blend = over(gate * record, add)
    estimate = blend + over(jnp.where(last, out, 0.0), add)
    error = estimate - over(jnp.where(last, record, 0.0), add)
    entropy = over(gate * log_gate, add)
    row_ids = info[3] * count + lax.broadcasted_iota(jnp.int32, (count, 1), 0)
    valid = (row_ids < info[1]).astype(F32)
    weight = valid * info[2].astype(F32)
    share = weight * scale[0]
    factor = share * error
    grads = gate * (factor * (record - blend) + PENALTY * share * (log_gate - entropy))
    grads = jnp.where(last, factor, grads).astype(BF16)
    prediction[...] = (estimate * valid)[:, :TILE_CELLS]
    head_rows = dot_tn(final_in, grads)
    for at in range(0, D, 128):
        head_grad[:, at : at + 128] = head_rows[at : at + 128]
    grad_final = dot_nt(grads, low)
    grad_in, gain_grad, bias_grad = norm_back(grad_final, normed, inverse, gain)
    grad_hidden[...] = grad_in
    sums[...] = jnp.zeros_like(sums)
    sums[0:1] = gain_grad[None]
    sums[1:2] = bias_grad[None]
    sums[2:3, :128] = column_sum(grads.astype(F32))
    sums[3:4, :128] = column_sum(jnp.where(lanes < TILE_CELLS, weight * entropy, 0.0))


def mlp_back_kernel(ids, rows, sizes, plan, chunk_ids, info, grad, mid, slopes, vec, *refs):
    groups = [sizes[0], sizes[1], len(ids[0]), len(ids[1]), 8, 8]
    mlp_a, mlp_b, path_a, path_b, outs, scratch = split_refs(refs, groups)
    grad_low, pre_own, pre_other, grad_mid, grad_branch, grad_attended, up_bias_grad, sums = outs
    store, out_store, sems, out_sems, slope_store, pre_store, slope_sems, pre_sems = scratch
    copies = mlp_copies((mlp_a, mlp_b), plan, store, sems)
    chunks = len(plan)
    slope_copies = []
    for chunk, pair in enumerate(copies):
        span = pl.ds(chunk * WIDE, WIDE)
        slope_copies.append(
            pltpu.make_async_copy(slopes.at[:, span], slope_store.at[:, span], slope_sems.at[chunk])
        )
    out_copies = attn_copies((path_a, path_b), ids, rows, info[0], ((1, 1),), out_store, out_sems)
    order = [[*pair[1], slope_copies[chunk], *pair[0]] for chunk, pair in enumerate(copies)]
    order[-1] += out_copies[0]
    for group in order[:AHEAD]:
        start_all(group)
    upper = grad[...].astype(F32)
    low = upper.astype(BF16)
    grad_low[...] = low
    up_bias_grad[...] = jnp.zeros_like(up_bias_grad)
    total = jnp.zeros(upper.shape, F32)
    sent = []
    for chunk in range(chunks):
        at = slice(chunk * WIDE, (chunk + 1) * WIDE)
        wait_all(copies[chunk][1])
        for group in order[chunk + AHEAD : chunk + AHEAD + 1]:
            start_all(group)
        grad_active = dot_nt(low, store[1, at])
        slope_copies[chunk].wait()
        grad_pre = (grad_active * slope_store[:, at]).astype(BF16)
        pre_store[:, at] = grad_pre
        out = split_copies(pre_store, pre_own, pre_other, chunk, chunks, pre_sems.at[chunk])
        out.start()
        sent.append(out)
        bias_grad = row_sum(grad_pre)
        for which in range(2):
            i = info[0] ^ chunk_ids[2 * chunk + which]
            lanes = pl.ds(pl.multiple_of((i & 1) * CHUNK, CHUNK), CHUNK)
            up_bias_grad[pl.ds(i >> 1, 1), lanes] = bias_grad[:, which * CHUNK : (which + 1) * CHUNK]
        wait_all(copies[chunk][0])
        total = total + dot_nn(grad_pre, store[0, at])
    normed, inverse = norm_parts(mid[...])
    grad_norm, gain_grad, bias_grad = norm_back(total, normed, inverse, vec[5:6])
    grad_sum = upper + grad_norm
    grad_mid[...] = grad_sum
    branch = grad_sum.astype(BF16)
    grad_branch[...] = branch
    sums[...] = jnp.zeros_like(sums)
    sums[0:1] = row_sum(branch)
    sums[1:2] = gain_grad[None]
    sums[2:3] = bias_grad[None]
    sums[3:4] = row_sum(low)
    wait_all(out_copies[0])
    grad_attended[...] = dot_nt(branch, out_store[0]).astype(BF16)
    wait_all(sent)


def attend_back_kernel(info, queries, grad_attended, log_total, *refs):
    pairs, outs = split_refs(refs, [2, 4])
    grad_queries, keep, send_keys, send_values = outs
    count = queries.shape[0]
    total = count * len(pairs)
    valid = valid_row(info[3], info[1], count, total)
    scale = HDIM ** (-0.5)
    for pair in range(HEADS // 2):
        lanes = slice(2 * HDIM * pair, 2 * HDIM * (pair + 1))
        shifted = slice(D + 2 * HDIM * pair, D + 2 * HDIM * (pair + 1))
        query = queries[:, lanes] * jnp.asarray(scale, BF16)
        grad = grad_attended[:, lanes]
        query_t = query.astype(F32).T.astype(BF16)
        grad_t = grad.astype(F32).T.astype(BF16)
        keys = jnp.concatenate([ref[:, lanes] for ref in pairs], 0)
        values = jnp.concatenate([ref[:, shifted] for ref in pairs], 0)
        outs_q, outs_k, outs_v = [], [], []
        for sub in range(2):
            mask = head_mask(sub, count)
            head = 2 * pair + sub
            rows = slice(HDIM * sub, HDIM * (sub + 1))
            zero = jnp.zeros_like(query)
            scores = dot_nt(jnp.where(mask, query, zero), keys)
            scores = jnp.where(valid, scores, NEG)
            probs = jnp.exp(scores - log_total[:, head : head + 1])
            grad_probs = dot_nt(jnp.where(mask, grad, zero), values)
            row_dot = jnp.sum(probs * grad_probs, -1, keepdims=True)
            grad_scores = (probs * (grad_probs - row_dot)).astype(BF16)
            outs_q.append(dot_nn(grad_scores, keys))
            outs_k.append(dot_nn(query_t[rows], grad_scores))
            outs_v.append(dot_nn(grad_t[rows], probs.astype(BF16)))
        grad_queries[:, lanes] = (jnp.where(head_mask(0, count), outs_q[0], outs_q[1]) * scale).astype(BF16)
        for where, outs_t, send in ((lanes, outs_k, send_keys), (shifted, outs_v, send_values)):
            part = jnp.concatenate(outs_t, 0).T.astype(BF16)
            keep[:, where] = part[:count]
            send[:, lanes] = part[count:]


def qkv_back_kernel(ids, rows, info, grad_queries, keep, came_keys, came_values, hidden, grad_mid, vec, *refs):
    groups = [len(ids[0]), len(ids[1]), 4, 2]
    path_a, path_b, outs, (store, sems) = split_refs(refs, groups)
    grad_hidden, hidden_low, grad_pair, sums = outs
    copies = attn_copies((path_a, path_b), ids, rows, info[0], ((0, 0), (0, 1), (1, 0)), store, sems)
    for group in copies:
        start_all(group)
    came = jnp.concatenate([came_keys[...], came_values[...]], 1)
    pair = add_low(keep[...], came)
    grad_pair[...] = pair
    grad_q = grad_queries[...]
    wait_all(copies[0])
    total = dot_nt(grad_q, store[0])
    wait_all(copies[1])
    total = total + dot_nt(pair[:, :D], store[1])
    wait_all(copies[2])
    total = total + dot_nt(pair[:, D:], store[2])
    normed, inverse = norm_parts(hidden[...].astype(F32))
    grad_norm, gain_grad, bias_grad = norm_back(total, normed, inverse, vec[0:1])
    result = grad_mid[...] + grad_norm
    grad_hidden[...] = result
    hidden_low[...] = result.astype(BF16)
    sums[...] = jnp.zeros_like(sums)
    sums[0:1] = gain_grad[None]
    sums[1:2] = bias_grad[None]
    sums[2:3] = row_sum(grad_q)
    sums[3:4] = row_sum(pair[:, D:])
    lead = lax.broadcasted_iota(jnp.int32, (NLEAD, D), 0) == info[2] - 1
    sums[8:] = jnp.where(lead, bias_grad[None], 0.0)


def reversed_bits(value, width):
    return sum(((value >> bit) & 1) << (width - 1 - bit) for bit in range(width))


def place_parts(value, blocks, width, mat, path, start, outs):
    at, rows = blocks
    at = at if path == 0 else reversed_bits(at, width)
    half = 1 << (width - 1)
    keep, send = outs[path]
    ref = keep if at < half else send
    ref[at % half, mat, start : start + rows] = value


def keep_earlier(info, earlier, outs, compute):
    if not earlier:
        compute()
        return
    later = info[4] == 1

    @pl.when(later)
    def _():
        for value, out in zip(earlier, outs):
            out[...] = value[...]

    @pl.when(jnp.logical_not(later))
    def _():
        compute()


def mlp_weight_kernel(width, half_rows, count, info, *refs):
    ins, earlier, outs = split_refs(refs, [8, count, 4])
    keep_earlier(info, earlier, outs, lambda: mlp_weight_body(width, half_rows, ins, outs))


def mlp_weight_body(width, half_rows, ins, outs):
    act, act_far, pre, pre_far, grad, grad_far, given, given_far = ins
    paths = (outs[:2], outs[2:])
    grad_two = jnp.concatenate([grad[...], grad_far[...]], 0)
    given_two = jnp.concatenate([given[...], given_far[...]], 0)
    rows = 2 * half_rows
    for first in range(0, 1 << width, 2):
        lanes = slice(first * rows, (first + 2) * rows)
        for mat, near, far, right in ((0, pre, pre_far, given_two), (1, act, act_far, grad_two)):
            left = jnp.concatenate([near[:, lanes], far[:, lanes]], 0)
            value = dot_tn(left, right).astype(BF16)
            for at in (first, first + 1):
                for path in range(2):
                    start = (at - first) * rows + path * half_rows
                    part = value[start : start + half_rows]
                    place_parts(part, (at, half_rows), width, mat, path, 0, paths)


def attn_weight_kernel(width, rows, count, info, *refs):
    ins, earlier, outs = split_refs(refs, [10, count, 4])
    keep_earlier(info, earlier, outs, lambda: attn_weight_body(width, rows, ins, outs))


def attn_weight_body(width, rows, ins, outs):
    mixed, mixed_far, att, att_far, grad_q, grad_q_far, pair, pair_far, branch, branch_far = ins
    paths = (outs[:2], outs[2:])
    mixed_two = jnp.concatenate([mixed[...], mixed_far[...]], 0)
    att_two = jnp.concatenate([att[...], att_far[...]], 0)
    jobs = (
        (0, 0, mixed_two, jnp.concatenate([grad_q[...], grad_q_far[...]], 0)),
        (0, 1, mixed_two, jnp.concatenate([pair[:, :D], pair_far[:, :D]], 0)),
        (1, 0, mixed_two, jnp.concatenate([pair[:, D:], pair_far[:, D:]], 0)),
        (1, 1, att_two, jnp.concatenate([branch[...], branch_far[...]], 0)),
    )
    for path, mat, left, right in jobs:
        value = dot_tn(left, right).astype(BF16)
        for at in range(1 << width):
            place_parts(value[at * rows : (at + 1) * rows], (at, rows), width, mat, path, 0, paths)


def polynomial_kernel(pieces, rate, *refs):
    mats = len(pieces)
    ins, (master, state, new), scratch = split_refs(refs, [sum(pieces), 3, 5])
    gram, low, mix, cross, moved = scratch
    block = D // 3
    spots = range(0, D, block)

    def square(store, left_of, right_of, finish):
        for spot in spots:
            at, rest = slice(spot, spot + block), slice(spot, D)
            value = finish(at, rest, left_of(at), right_of(rest))
            store[at, rest] = value.astype(store.dtype)
            for other in range(spot + block, D, block):
                part = value[:, other - spot : other - spot + block]
                store[other : other + block, at] = part.T.astype(store.dtype)

    at_piece = 0
    for mat in range(mats):
        mine = ins[at_piece : at_piece + pieces[mat]]
        at_piece += pieces[mat]

        def gram_block(at, rest, left, right):
            total = dot_tn(mine[0][:, at], mine[0][:, rest])
            for ref in mine[1:]:
                total = total + dot_tn(ref[:, at], ref[:, rest])
            return total

        square(gram, lambda at: None, lambda rest: None, gram_block)
        trace = jnp.zeros((), F32)
        for spot in spots:
            at = slice(spot, spot + block)
            hot = lax.broadcasted_iota(jnp.int32, (block, block), 0) == lax.broadcasted_iota(
                jnp.int32, (block, block), 1
            )
            trace = trace + jnp.sum(jnp.where(hot, gram[at, at], 0.0))
        factor = 1.0 / (jnp.sqrt(trace) + 1e-07)
        scaled = factor * factor
        for spot in spots:
            at = slice(spot, spot + block)
            value = gram[at] * scaled
            gram[at] = value
            low[at] = value.astype(BF16)

        def mixed(at, rest, left, right):
            return COEF_B * gram[at, rest] + COEF_C * dot_nn(left, right)

        def crossed(at, rest, left, right):
            return dot_nn(left, right)

        def moved_gram(at, rest, left, right):
            result = (COEF_A * COEF_A) * gram[at, rest] + (2.0 * COEF_A) * moved[at, rest]
            return result + dot_nn(left, right)

        value = state[mat] * factor
        square(mix, lambda at: low[at], lambda rest: low[:, rest], mixed)
        value = COEF_A * value + dot_nn(value.astype(BF16), mix[...])
        square(moved, lambda at: mix[at], lambda rest: low[:, rest], crossed)
        cross[...] = moved[...].astype(BF16)
        square(low, lambda at: mix[at], lambda rest: cross[:, rest], moved_gram)
        once = dot_nn(value.astype(BF16), low[...])
        twice = dot_nn(once.astype(BF16), low[...])
        value = COEF_A * value + COEF_B * once + COEF_C * twice
        new[mat] = master[mat] * (1.0 - rate[mat] * DECAY) - rate[mat] * value


def swap_dp(value, bit):
    size = lax.axis_size("dp")
    return lax.ppermute(value, "dp", [(i, i ^ (1 << bit)) for i in range(size)])


def swap_rep(value, mask):
    size = lax.axis_size("rep")
    return lax.ppermute(value, "rep", [(i, i ^ mask) for i in range(size)])


def link_bits():
    count = lax.axis_size("dp").bit_length() - 1
    return (list(range(1, count)), list(range(count - 1, 0, -1)))


def path_ids(order):
    ids = [0]
    for bit in order:
        ids = ids + [i | (1 << bit) for i in ids]
    return ids


def call(kernel, ins, outs, scratch=(), specs=None, mib=56, flops=0, moved=0, out_specs=None):
    return list(pl.pallas_call(
        kernel,
        out_shape=tuple(outs),
        in_specs=specs or [VMEM] * len(ins),
        out_specs=tuple(out_specs or [VMEM] * len(outs)),
        scratch_shapes=list(scratch),
        compiler_params=limits(mib),
        cost_estimate=pl.CostEstimate(flops=flops // 64, bytes_accessed=moved // 64, transcendentals=0),
    )(*ins))


def after(value, *others):
    return lax.optimization_barrier((value, others))[0]


def piece_ids(order):
    ids = [0]
    for bit in order[:-1]:
        ids = ids + [i | (1 << bit) for i in ids]
    far = [i | (1 << order[-1]) for i in ids]
    return [ids, far, [i | 1 for i in ids], [i | 1 for i in far]]


def gather_steps(firsts, orders, axis=0):
    nears = firsts
    for step in range(len(orders[0]) - 1):
        arrived = [swap_dp(near, order[step]) for near, order in zip(nears, orders)]
        ties = yield nears
        nears = [
            jnp.concatenate([near, after(value, *ties)], axis)
            for near, value in zip(nears, arrived)
        ]
    arrived = [swap_dp(near, order[-1]) for near, order in zip(nears, orders)]
    others = [swap_dp(near, 0) for near in nears]
    ties = yield nears
    fars = [after(value, *ties) for value in arrived]
    ends = [swap_dp(far, 0) for far in fars]
    yield fars
    yield [list(value) for value in zip(nears, fars, others, ends)]


def natural(pieces, ids):
    me = lax.axis_index("dp")
    flat = [i for group in ids for i in group]
    slot = [0] * len(flat)
    for at, i in enumerate(flat):
        slot[i] = at
    joined = jnp.concatenate(pieces, 0)
    wanted = jnp.asarray(slot, jnp.int32)[jnp.arange(len(flat)) ^ me]
    taken = jnp.take(joined, wanted, axis=0)
    mats, width = taken.shape[1], taken.shape[3]
    return taken.transpose(1, 0, 2, 3).reshape(1, mats, -1, width)


def scatter_steps(parts, orders, join):
    low = lax.axis_index("rep") & 1
    keeps, sends = [parts[0], parts[2]], [parts[1], parts[3]]
    values = keeps
    for step in range(len(orders[0])):
        arrived = [swap_dp(send, order[step]) for send, order in zip(sends, orders)]
        ties = yield values
        values = [add_low(keep, after(value, *ties)) for keep, value in zip(keeps, arrived)]
        half = values[0].shape[0] // 2
        keeps = [value[:half] for value in values]
        sends = [value[half:] for value in values]
    pair = join([value[0] for value in values])
    keep = lax.dynamic_index_in_dim(pair, low, 0, keepdims=False)
    arrived = swap_rep(lax.dynamic_index_in_dim(pair, 1 - low, 0, keepdims=False), 1)
    ties = yield keep
    yield keep.astype(F32) + after(arrived, *ties).astype(F32)


def sum_steps(rows):
    core = lax.axis_index("dp") & 1
    high = lax.axis_index("rep") >> 1
    half = rows.shape[0] // 2
    total = lax.dynamic_slice_in_dim(rows, core * half, half, 0)
    swaps = [functools.partial(swap_dp, bit=bit) for bit in link_bits()[0]]
    swaps.append(functools.partial(swap_rep, mask=1))
    arrived = swap_dp(lax.dynamic_slice_in_dim(rows, (1 - core) * half, half, 0), 0)
    for swap in swaps:
        ties = yield total
        total = total + after(arrived, *ties)
        arrived = swap(total)
    ties = yield total
    total = total + after(arrived, *ties)
    arrived = swap_rep(total, 2)
    ties = yield total
    other = after(arrived, *ties)
    both = jnp.where(high == 0, jnp.stack([total, other]), jnp.stack([other, total]))
    arrived = swap_dp(both, 0)
    ties = yield both
    other = after(arrived, *ties)
    first = jnp.where(core == 0, both, other)
    second = jnp.where(core == 0, other, both)
    yield jnp.concatenate([first, second], 1)


class Steps:
    def __init__(self, steps):
        self.steps = steps
        self.last = next(steps)

    def go(self, *ties):
        self.last = self.steps.send(ties)
        return self.last

    def finish(self, *ties):
        try:
            while True:
                self.go(*ties)
        except StopIteration:
            return self.last


def local(
    features,
    tile_records,
    patch_counts,
    lead_counts,
    attn_master,
    attn_momentum,
    mlp_master,
    mlp_momentum,
    vectors,
    vec_momentum,
    head_master,
    head_momentum,
):
    rep_size = lax.axis_size("rep")
    dp_size = lax.axis_size("dp")
    me = lax.axis_index("dp")
    core = me & 1
    rep = lax.axis_index("rep")
    rep_low = rep & 1
    rep_high = rep >> 1
    quarter_rows = features.shape[0]
    count = 2 * quarter_rows
    attn_rows = attn_master.shape[1]
    mlp_rows = mlp_master.shape[1]
    half_rows = mlp_rows // 2
    links = dp_size // 2
    width = links.bit_length() - 1
    paths = link_bits()
    path_a, path_b = paths
    back_orders = (path_b, path_a)
    direct = attn_rows % 16 == 0 and mlp_rows == CHUNK
    assert LAYERS == 2 and rep_size == 2 * LAYERS

    def frame_moves(upper):
        moves = ([], [])
        for d in range(dp_size):
            for r in range(rep_size):
                to = (d - d % 2 + r // 2) * rep_size + 2 * upper + d % 2
                moves[r % 2].append((d * rep_size + r, to))
        return moves

    def bring(value, upper):
        both = [lax.ppermute(value, ("dp", "rep"), pairs) for pairs in frame_moves(upper)]
        return jnp.concatenate(both, 0)

    def take_back(value, upper):
        parts = [
            lax.ppermute(
                value[at * quarter_rows : (at + 1) * quarter_rows],
                ("dp", "rep"),
                [(to, came) for came, to in pairs],
            )
            for at, pairs in enumerate(frame_moves(upper))
        ]
        return jnp.where(rep_low == 0, parts[0], parts[1])

    def up_layer(value):
        return lax.ppermute(value, "rep", [(0, 2), (1, 3)])

    def down_layer(value):
        return lax.ppermute(value, "rep", [(2, 0), (3, 1)])

    def both_owners(own, near):
        pair = jnp.stack([own, near])
        return [lax.dynamic_index_in_dim(pair, rep_low ^ i, 0, keepdims=False) for i in (0, 1)]

    attn_low = attn_master.astype(BF16)
    attn_near = swap_rep(attn_low, 1)
    features = bring(after(features, attn_near), 0)
    mlp_low = mlp_master[0].astype(BF16)
    mlp_near = swap_rep(after(mlp_low, attn_near), 1)

    counts = jnp.concatenate([patch_counts, lead_counts]).reshape(1, 2)
    counts = jnp.concatenate([counts, swap_dp(counts, 0)], 0)
    tile_records = bring(after(tile_records, attn_near), 1)
    frame_count, lead_value = lax.dynamic_index_in_dim(counts, core ^ rep_low, 0, keepdims=False)
    info = jnp.stack(
        [me if direct else 0 * me, frame_count, lead_value, core, rep_high]
    ).astype(jnp.int32)

    position = jnp.arange(D) // attn_rows
    distance = ((position % links) << 1) | (position // links)
    source = ((distance ^ me) * attn_rows + jnp.arange(D) % attn_rows).astype(jnp.int32)[None]
    order = [(at % links) << 1 | at // links for at in range(dp_size)]

    vec_rows = VEC_ROWS * LAYERS + 2
    vec_all = vectors[: vec_rows * D].reshape(vec_rows, D)
    vec = lax.dynamic_slice_in_dim(vec_all, VEC_ROWS * rep_high, VEC_ROWS, 0)
    vec_tail = vec_all[VEC_ROWS * LAYERS :]
    head_bias = vectors[vec_rows * D :].reshape(1, -1)
    chunks = FF // CHUNK
    up_bias = vec[8:12].reshape(chunks, 1, CHUNK)

    ids_a, ids_b = piece_ids(path_a), piece_ids(path_b)
    if direct:
        chunk_ids = order
        found = [
            {i: (piece, at) for piece, group in enumerate(ids) for at, i in enumerate(group)}
            for ids in (ids_a, ids_b)
        ]
        plan = [
            [(path, *found[path][i], 0, half_rows) for i in order[at : at + 2] for path in range(2)]
            for at in range(0, dp_size, 2)
        ]
        attn_ids = (ids_a, ids_b)
        mlp_sizes = (4, 4)
        place_rows = attn_rows
    else:
        chunk_ids = list(range(chunks))
        plan = [[(0, 0, 0, at, WIDE)] for at in range(0, FF, WIDE)]
        attn_ids = ([[0]], [[0]])
        mlp_sizes = (1, 0)
        place_rows = D
    n_attn = sum(len(group) for group in attn_ids)
    n_mlp = sum(mlp_sizes)
    copies_each = sum(len(group) for group in attn_ids[0])
    mlp_copies_all = 2 * sum(len(parts) for parts in plan)
    dma = pltpu.SemaphoreType.DMA
    unit_scratch = [pltpu.VMEM((count, FF), F32), pltpu.VMEM((count, FF), BF16)]
    unit_scratch += [dma((len(plan),)), dma((len(plan),))]
    matrix = D * D
    layer_flops = 2 * count * matrix

    def mlp_rel(first, second):
        if direct:
            return first, second
        whole = jnp.concatenate([first, second], 1).reshape(count, dp_size, mlp_rows)
        whole = jnp.take(whole, jnp.asarray(order, jnp.int32) ^ me, axis=1).reshape(count, FF)
        return whole[:, : FF // 2], whole[:, FF // 2 :]

    def qkv(hidden, *ties):
        own, other, queries, pair = call(
            functools.partial(qkv_kernel, attn_ids, place_rows),
            [after(info, *ties), hidden, vec, source] + attn_pieces,
            [
                shape_of(count, D // 2, dtype=BF16),
                shape_of(count, D // 2, dtype=BF16),
                shape_of(count, D, dtype=BF16),
                shape_of(count, 2 * D, dtype=BF16),
            ],
            [pltpu.VMEM((3, D, D), BF16), dma((3 * copies_each,))],
            [SMEM, VMEM, VMEM, VMEM] + [IN_HBM] * n_attn,
            flops=4 * layer_flops,
            moved=6 * matrix + 4 * count * D * 4,
        )
        return [hidden, own, swap_dp(other, 0), queries, [pair, swap_dp(pair, 0)]]

    def attend(saved):
        outs = call(
            functools.partial(attend_kernel, attn_ids, place_rows),
            [after(info, saved[2]), saved[0], vec, source, saved[3]] + saved[4] + attn_pieces,
            [
                shape_of(count, D // 2, dtype=BF16),
                shape_of(count, D // 2, dtype=BF16),
                shape_of(count, 128),
                shape_of(count, D),
                shape_of(count, D, dtype=BF16),
            ],
            [pltpu.VMEM((1, D, D), BF16), pltpu.VMEM((count, D), BF16), dma((copies_each,))],
            [SMEM, VMEM, VMEM, VMEM] + [VMEM] * 3 + [IN_HBM] * n_attn,
            flops=8 * layer_flops,
            moved=2 * matrix + count * D * 8,
        )
        outs[1] = swap_dp(outs[1], 0)
        return saved + outs

    def feed(saved):
        outs = call(
            functools.partial(mlp_kernel, mlp_sizes, plan, chunk_ids),
            [info, saved[8], saved[9], vec, up_bias] + mlp_pieces,
            [
                shape_of(count, D),
                shape_of(count, D, dtype=BF16),
                shape_of(count, FF),
                shape_of(count, FF // 2, dtype=BF16),
                shape_of(count, FF // 2, dtype=BF16),
            ],
            [pltpu.VMEM((2, FF, D), BF16), dma((mlp_copies_all,))] + unit_scratch,
            [SMEM] + [VMEM] * 4 + [IN_HBM] * n_mlp,
            out_specs=[VMEM] * 2 + [IN_HBM] * 3,
            flops=8 * layer_flops,
            moved=4 * FF * D + count * FF * 6,
        )
        near_act, other_act = mlp_rel(outs[3], outs[4])
        far = [swap_dp(other_act, 0), swap_dp(saved[9], 0)]
        return outs[0], outs[1], saved + [outs[2], near_act] + far

    def mlp_back(saved, grad, *ties):
        outs = call(
            functools.partial(mlp_back_kernel, attn_ids, place_rows, mlp_sizes, plan, chunk_ids),
            [after(info, *ties), grad, saved[8], saved[10], vec] + mlp_pieces + attn_pieces,
            [
                shape_of(count, D, dtype=BF16),
                shape_of(count, FF // 2, dtype=BF16),
                shape_of(count, FF // 2, dtype=BF16),
                shape_of(count, D),
                shape_of(count, D, dtype=BF16),
                shape_of(count, D, dtype=BF16),
                shape_of(8, D),
                shape_of(8, D),
            ],
            [
                pltpu.VMEM((2, FF, D), BF16),
                pltpu.VMEM((1, D, D), BF16),
                dma((mlp_copies_all,)),
                dma((copies_each,)),
            ]
            + unit_scratch,
            [SMEM, VMEM, VMEM, IN_HBM, VMEM] + [IN_HBM] * (n_mlp + n_attn),
            out_specs=[VMEM, IN_HBM, IN_HBM] + [VMEM] * 5,
            flops=9 * layer_flops,
            moved=4 * FF * D + 2 * matrix + count * FF * 6,
        )
        near_pre, other_pre = mlp_rel(outs[1], outs[2])
        outs[1], outs[2] = near_pre, swap_dp(other_pre, 0)
        return outs + [swap_dp(outs[0], 0)]

    def attend_back(saved, grad_attended, *ties):
        grad_queries, keep, send_keys, send_values = call(
            attend_back_kernel,
            [after(info, *ties), saved[3], grad_attended, saved[7]] + saved[4],
            [
                shape_of(count, D, dtype=BF16),
                shape_of(count, 2 * D, dtype=BF16),
                shape_of(count, D, dtype=BF16),
                shape_of(count, D, dtype=BF16),
            ],
            (),
            [SMEM] + [VMEM] * 5,
            flops=20 * layer_flops,
            moved=count * D * 16,
        )
        return grad_queries, [keep, swap_dp(send_keys, 0), swap_dp(send_values, 0)]

    def qkv_back(saved, grad_queries, parts, grad_mid):
        return call(
            functools.partial(qkv_back_kernel, attn_ids, place_rows),
            [info, grad_queries] + parts + [saved[0], grad_mid, vec] + attn_pieces,
            [
                shape_of(count, D),
                shape_of(count, D, dtype=BF16),
                shape_of(count, 2 * D, dtype=BF16),
                shape_of(8 + NLEAD, D),
            ],
            [pltpu.VMEM((3, D, D), BF16), dma((3 * copies_each,))],
            [SMEM] + [VMEM] * 7 + [IN_HBM] * n_attn,
            flops=3 * layer_flops,
            moved=6 * matrix + count * D * 20,
        )

    flipped = jnp.asarray([reversed_bits(at, width) for at in range(links)], jnp.int32)

    def mlp_weights(saved, back, earlier, *ties):
        ins = [after(saved[11], *ties), saved[12], back[1], back[2]]
        ins += [back[0], back[8], saved[9], saved[13]]
        if direct:
            part = shape_of(links // 2, 2, half_rows, D, dtype=BF16)
            return call(
                functools.partial(mlp_weight_kernel, width, half_rows, len(earlier)),
                [info] + ins + earlier,
                [part] * 4,
                specs=[SMEM] + [VMEM] * (8 + len(earlier)),
                flops=8 * layer_flops,
                moved=4 * FF * D + count * FF * 8,
            )
        lefts = [jnp.concatenate(ins[2:4], 0), jnp.concatenate(ins[:2], 0)]
        rights = [jnp.concatenate(ins[6:], 0), jnp.concatenate(ins[4:6], 0)]
        both = jnp.stack([dot_tn(l, r).astype(BF16) for l, r in zip(lefts, rights)])
        both = both.reshape(2, links, 2, half_rows, D).transpose(2, 1, 0, 3, 4)
        return choose([both[0], jnp.take(both[1], flipped, axis=0)], earlier)

    def choose(paths_of, earlier):
        half = links // 2
        parts = [part for path in paths_of for part in (path[:half], path[half:])]
        if earlier:
            parts = [jnp.where(rep_high == 1, old, new) for old, new in zip(earlier, parts)]
        return parts

    def attn_weights(saved, grad_queries, grad_pair, branch, earlier, *ties):
        ins = [after(saved[1], *ties), saved[2], saved[5], saved[6]]
        for value in (grad_queries, grad_pair, branch):
            ins += [value, swap_dp(value, 0)]
        if direct:
            part = shape_of(links // 2, 2, attn_rows, D, dtype=BF16)
            return call(
                functools.partial(attn_weight_kernel, width, attn_rows, len(earlier)),
                [info] + ins + earlier,
                [part] * 4,
                specs=[SMEM] + [VMEM] * (10 + len(earlier)),
                flops=4 * layer_flops,
                moved=4 * matrix + count * D * 16,
            )
        mixed_two, att_two, q_two, pair_two, branch_two = (
            jnp.concatenate(ins[at : at + 2], 0) for at in (0, 2, 4, 6, 8)
        )
        jobs = [(mixed_two, q_two), (mixed_two, pair_two[:, :D])]
        jobs += [(mixed_two, pair_two[:, D:]), (att_two, branch_two)]
        grads = [dot_tn(l, r).astype(BF16).reshape(links, attn_rows, D) for l, r in jobs]
        second = jnp.take(jnp.stack(grads[2:], 1), flipped, axis=0)
        return choose([jnp.stack(grads[:2], 1), second], earlier)

    def rows_of(qkv_sums, back):
        return jnp.concatenate(
            [qkv_sums, back[7], back[6]], 0
        )

    attn_all = Steps(
        gather_steps([value[None] for value in both_owners(attn_low, attn_near)], paths)
    )
    for bit in path_a:
        counts = jnp.concatenate([counts, swap_dp(counts, bit)], 0)
    pixel_total = (TILE_CELLS * jnp.sum(counts[:, 0] * counts[:, 1])).astype(F32)
    tie = attn_all.go(pixel_total, vec, info, source, up_bias, vec_tail, head_bias)
    both = jnp.stack(both_owners(mlp_low, after(mlp_near, tie)))
    mlp_all = Steps(
        gather_steps([both[None, :, :half_rows], both[None, :, half_rows:]], paths)
    )
    tie = attn_all.go(mlp_all.last, features)
    ends = attn_all.finish(tie)
    if direct:
        attn_pieces = ends[0] + ends[1]
    else:
        attn_pieces = [natural(ends[0], ids_a), natural(ends[1], ids_b)]

    saved_0 = qkv(features, tie)
    tie = mlp_all.go(saved_0[3])
    saved_0 = attend(saved_0)
    tie = mlp_all.go(saved_0[8])
    ends = mlp_all.finish(tie)
    if direct:
        mlp_pieces = ends[0] + ends[1]
    else:
        shape = (1, 2, dp_size, half_rows, D)
        parts = [natural(end, ids).reshape(shape) for end, ids in zip(ends, (ids_a, ids_b))]
        mlp_pieces = [jnp.concatenate(parts, 3).reshape(1, 2, FF, D)]
    _, hidden_low, saved_0 = feed(saved_0)

    hidden_low = up_layer(hidden_low)
    saved_1 = attend(qkv(hidden_low, saved_0[6], saved_0[12], saved_0[13], tile_records))
    hidden, _, saved_1 = feed(saved_1)
    scale = (1.0 / pixel_total).reshape(1)
    prediction, head_grad, grad_hidden, head_sums = call(
        head_kernel,
        [info, scale, hidden, tile_records, vec_tail, head_bias, head_master],
        [shape_of(count, TILE_CELLS), shape_of(128, D), shape_of(count, D), shape_of(8, D)],
        (),
        [SMEM, SMEM] + [VMEM] * 5,
        flops=layer_flops,
        moved=D * 128 * 8 + count * D * 8,
    )
    back_1 = mlp_back(saved_1, grad_hidden, saved_1[6], saved_1[12], saved_1[13])
    grad_q_1, parts = attend_back(saved_1, back_1[5])
    _, grad_low, grad_pair_1, sums_1 = qkv_back(saved_1, grad_q_1, parts, back_1[3])
    grad_low = down_layer(grad_low)
    mlp_grads = mlp_weights(saved_1, back_1, [], grad_pair_1)
    attn_grads = attn_weights(saved_1, grad_q_1, grad_pair_1, back_1[4], [], mlp_grads[0])
    prediction = take_back(after(prediction, attn_grads[0]), 1)

    back_0 = mlp_back(saved_0, after(grad_low, attn_grads[0]))
    mlp_grads = mlp_weights(saved_0, back_0, mlp_grads)
    tie = mlp_grads[0]
    mlp_steps = Steps(scatter_steps(mlp_grads, back_orders, lambda parts: jnp.concatenate(parts, 1)))
    grad_q_0, parts = attend_back(saved_0, back_0[5], tie)
    grad_hidden, _, grad_pair_0, sums_0 = qkv_back(saved_0, grad_q_0, parts, back_0[3])
    tie = mlp_steps.go(grad_hidden)
    attn_grads = attn_weights(
        saved_0, grad_q_0, grad_pair_0, back_0[4], attn_grads, tie
    )
    tie = attn_grads[0]
    attn_steps = Steps(scatter_steps(attn_grads, back_orders, jnp.stack))
    layer_rows = jnp.where(rep_high == 0, rows_of(sums_0, back_0), rows_of(sums_1, back_1))
    sums = Steps(sum_steps(jnp.concatenate([head_grad, head_sums, layer_rows], 0)))
    tie = mlp_steps.go(tie)
    tie = sums.go(tie)
    tie = attn_steps.go(tie)
    mlp_share = mlp_steps.finish(tie)[None]
    mlp_moment = MOMENTUM * mlp_momentum + mlp_share
    mlp_state = mlp_share + MOMENTUM * mlp_moment
    low = mlp_state[0].astype(BF16)
    mlp_all = Steps(gather_steps([low[:half_rows], low[half_rows:]], paths))
    features_grad = take_back(after(grad_hidden, mlp_share), 0)
    tie = attn_steps.go(mlp_share)
    tie = sums.go(tie)
    tie = mlp_all.go(tie)
    attn_share = attn_steps.finish(tie)
    attn_moment = MOMENTUM * attn_momentum + attn_share
    attn_state = attn_share + MOMENTUM * attn_moment
    low = attn_state.astype(BF16)
    attn_all = Steps(gather_steps([low[0], low[1]], paths))
    tie = sums.go(attn_share)
    tie = mlp_all.go(tie)
    mlp_all = mlp_all.finish(tie)
    tie = attn_all.go(tie)
    tie = sums.go(tie)

    def polynomial(groups, master, state, rate):
        pieces = [piece for group in groups for piece in group]
        sizes = [len(group) for group in groups]
        square = pltpu.VMEM((D, D), F32)
        low = pltpu.VMEM((D, D), BF16)
        rows = sum(piece.shape[0] for piece in pieces)
        return call(
            functools.partial(polynomial_kernel, sizes),
            [rate] + pieces + [master, state],
            [shape_of(*master.shape)],
            [square, low, low, low, square],
            [SMEM] + [VMEM] * (len(pieces) + 2),
            flops=2 * matrix * (rows + 4 * D * len(groups)),
            moved=rows * D * 2,
        )[0]

    attn_rate = jnp.asarray(ATTN_RATES, F32).reshape(2, 2)[rep_low]
    mlp_rate = jnp.asarray(MLP_RATES, F32)[rep_low].reshape(1)
    mlp_new = polynomial([mlp_all[0] + mlp_all[1]], mlp_master, mlp_state, after(mlp_rate, tie))
    tie = attn_all.go(mlp_new)
    tie = sums.go(tie)
    attn_new = polynomial(attn_all.finish(tie), attn_master, attn_state, attn_rate)
    sums = sums.finish(attn_new)

    def layer_of(rows):
        return [rows[:4], rows[16:20], rows[24:28], rows[8:16]]

    head_sum = jnp.concatenate(
        [sums[1, :128, at : at + 128] for at in range(0, D, 128)], 0
    )
    head_sums = sums[1, 128:136]
    vec_sum = layer_of(sums[0, 136:]) + layer_of(sums[1, 136:]) + [head_sums[:2]]
    vec_sum = jnp.concatenate(
        [jnp.concatenate(vec_sum, 0).reshape(-1), head_sums[2, :128]]
    )
    penalty = jnp.sum(head_sums[3, :128]) / pixel_total

    vec_moment = MOMENTUM * vec_momentum + vec_sum
    vec_new = vectors - VEC_RATE * vec_moment
    head_moment = MOMENTUM * head_momentum + head_sum
    head_new = head_master - HEAD_RATE * head_moment
    return (
        prediction,
        features_grad,
        penalty,
        attn_moment,
        attn_new,
        mlp_moment,
        mlp_new,
        vec_moment,
        vec_new,
        head_moment,
        head_new,
    )


def solution(mesh):
    return jax.shard_map(
        local,
        mesh=mesh,
        in_specs=(
            P(("dp", "rep"), None),
            P(("dp", "rep"), None),
            P("dp"),
            P("dp"),
            P("rep", "dp", None),
            P("rep", "dp", None),
            P("rep", "dp", None),
            P("rep", "dp", None),
            P(),
            P(),
            P(),
            P(),
        ),
        out_specs=(
            P(("dp", "rep"), None),
            P(("dp", "rep"), None),
            P(),
            P("rep", "dp", None),
            P("rep", "dp", None),
            P("rep", "dp", None),
            P("rep", "dp", None),
            P(),
            P(),
            P(),
            P(),
        ),
        check_vma=False,
    )
```

```python
import functools

import jax
import jax.numpy as jnp
from jax import lax
from jax.experimental import pallas as pl
from jax.experimental.pallas import tpu as pltpu
from jax.sharding import PartitionSpec as P

D = 768
HEADS = 12
HDIM = 64
FF = 3072
LAYERS = 2
MODEL_NUMBER = 3
TILE_CELLS = 32
NLEAD = 8
NS_STEPS = 2


EPS = 1e-05
NEG = -1e30
MOMENTUM = 0.95
COEF_A = 3.4445
COEF_B = -4.775
COEF_C = 2.0315
PENALTY = 0.5
VEC_RATE = 1000.0
HEAD_RATE = 300.0
DECAY = 0.01
ATTN_RATES = (1.0, 1.0, 1.0, 4.0)
MLP_RATES = (2.0, 1.0)


def norm_parts(hidden):
    centred = hidden - jnp.mean(hidden, -1, keepdims=True)
    variance = jnp.mean(centred * centred, -1, keepdims=True)
    inverse = lax.rsqrt(variance + EPS)
    return (centred * inverse, inverse)


def norm_back(grad_out, normed, inverse, gain):
    scaled = grad_out * gain
    mean_one = jnp.mean(scaled, -1, keepdims=True)
    mean_two = jnp.mean(scaled * normed, -1, keepdims=True)
    grad_in = inverse * (scaled - mean_one - normed * mean_two)
    return (grad_in, jnp.sum(grad_out * normed, 0), jnp.sum(grad_out, 0))


ROOT_TWO_OVER_PI = 0.7978845608028654
CUBE = 0.044715
VEC_ROWS = 20
VMEM = pl.BlockSpec(memory_space=pltpu.VMEM)
SMEM = pl.BlockSpec(memory_space=pltpu.SMEM)
IN_HBM = pl.BlockSpec(memory_space=pltpu.HBM)
BF16 = jnp.bfloat16
F32 = jnp.float32


def shape_of(*dims, dtype=F32):
    return jax.ShapeDtypeStruct(dims, dtype)


def limits(mib):
    return pltpu.CompilerParams(vmem_limit_bytes=mib * 1024 * 1024)


def dot_nn(left, right):
    return jnp.dot(left, right, preferred_element_type=F32)


def dot_nt(left, right):
    return lax.dot_general(left, right, (((1,), (1,)), ((), ())), preferred_element_type=F32)


def dot_tn(left, right):
    return lax.dot_general(left, right, (((0,), (0,)), ((), ())), preferred_element_type=F32)


def column_sum(value):
    return jnp.sum(value, 0, keepdims=True)


def add_low(keep, arrived):
    return (keep.astype(F32) + arrived.astype(F32)).astype(BF16)


def start_all(copies):
    for copy in copies:
        copy.start()


def wait_all(copies):
    for copy in copies:
        copy.wait()


def attn_copies(refs, ids, rows, me, wanted, store, sems):
    result = []
    count = 0
    for place_at, (path, mat) in enumerate(wanted):
        copies = []
        for ref, ref_ids in zip(refs[path], ids[path]):
            for at, i in enumerate(ref_ids):
                first = pl.multiple_of((me ^ i) * rows, rows)
                copies.append(
                    pltpu.make_async_copy(
                        ref.at[at, mat], store.at[place_at, pl.ds(first, rows)], sems.at[count]
                    )
                )
                count += 1
        result.append(copies)
    return result


def mlp_copies(refs, plan, store, sems):
    result = []
    count = 0
    for chunk, parts in enumerate(plan):
        pair = []
        for mat in range(2):
            copies = []
            first = chunk * WIDE
            for path, piece, at, start, rows in parts:
                copies.append(
                    pltpu.make_async_copy(
                        refs[path][piece].at[at, mat, pl.ds(start, rows)],
                        store.at[mat, pl.ds(first, rows)],
                        sems.at[count],
                    )
                )
                first += rows
                count += 1
            pair.append(copies)
        result.append(pair)
    return result


CHUNK = 384
AHEAD = 2
WIDE = 2 * CHUNK


def split_refs(refs, sizes):
    out = []
    at = 0
    for size in sizes:
        out.append(refs[at : at + size])
        at += size
    assert at == len(refs)
    return out


def select_matrix(source):
    rows = lax.broadcasted_iota(jnp.int32, (D, D), 0)
    return (rows == source).astype(F32).astype(BF16)


def qkv_kernel(ids, rows, info, hidden, vec, source, *refs):
    sizes = [len(ids[0]), len(ids[1]), 4, 2]
    path_a, path_b, (own, other, queries, pair), (store, sems) = split_refs(refs, sizes)
    copies = attn_copies((path_a, path_b), ids, rows, info[0], ((0, 0), (0, 1), (1, 0)), store, sems)
    for group in copies:
        start_all(group)
    lead_row = 12 + info[2] - 1
    normed, _ = norm_parts(hidden[...].astype(F32))
    mixed = (normed * vec[0:1] + vec[1:2] + vec[pl.ds(lead_row, 1)]).astype(BF16)
    moved = dot_nn(mixed, select_matrix(source[...])).astype(BF16)
    own[...] = moved[:, : D // 2]
    other[...] = moved[:, D // 2 :]
    wait_all(copies[0])
    queries[...] = (dot_nn(mixed, store[0]) + vec[2:3]).astype(BF16)
    wait_all(copies[1])
    pair[:, :D] = dot_nn(mixed, store[1]).astype(BF16)
    wait_all(copies[2])
    pair[:, D:] = (dot_nn(mixed, store[2]) + vec[3:4]).astype(BF16)


def valid_row(quarter, count, rows, total):
    at = lax.broadcasted_iota(jnp.int32, (1, total), 1)
    block = jnp.zeros((1, total), jnp.int32)
    for step in range(1, total // rows):
        block = block + (at >= step * rows).astype(jnp.int32)
    return ((quarter ^ block) - block) * rows + at < count


def head_mask(sub, rows):
    lanes = lax.broadcasted_iota(jnp.int32, (rows, 2 * HDIM), 1)
    return (lanes < HDIM) if sub == 0 else (lanes >= HDIM)


def attend_kernel(ids, rows, info, hidden, vec, source, queries, *refs):
    sizes = [2, len(ids[0]), len(ids[1]), 5, 3]
    pairs, path_a, path_b, (own, other, log_total, mid, mlp_in), (store, joined, sems) = split_refs(refs, sizes)
    copies = attn_copies((path_a, path_b), ids, rows, info[0], ((1, 1),), store, sems)
    start_all(copies[0])
    count = queries.shape[0]
    total = count * len(pairs)
    valid = valid_row(info[3], info[1], count, total)
    log_total[...] = jnp.zeros_like(log_total)
    for pair in range(HEADS // 2):
        lanes = slice(2 * HDIM * pair, 2 * HDIM * (pair + 1))
        shifted = slice(D + 2 * HDIM * pair, D + 2 * HDIM * (pair + 1))
        query = queries[:, lanes] * jnp.asarray(HDIM ** (-0.5), BF16)
        keys = jnp.concatenate([ref[:, lanes] for ref in pairs], 0)
        values = jnp.concatenate([ref[:, shifted] for ref in pairs], 0)
        outs = []
        for sub in range(2):
            mask = head_mask(sub, count)
            scores = dot_nt(jnp.where(mask, query, jnp.zeros_like(query)), keys)
            scores = jnp.where(valid, scores, NEG)
            top = jnp.max(scores, -1, keepdims=True)
            expo = jnp.exp(scores - top)
            sums = jnp.sum(expo, -1, keepdims=True)
            probs = (expo * (1.0 / sums)).astype(BF16)
            outs.append(dot_nn(probs, values))
            head = 2 * pair + sub
            log_total[:, head : head + 1] = top + jnp.log(sums)
        joined[:, lanes] = jnp.where(head_mask(0, count), outs[0], outs[1]).astype(BF16)
    attended = joined[...]
    moved = dot_nn(attended, select_matrix(source[...])).astype(BF16)
    own[...] = moved[:, : D // 2]
    other[...] = moved[:, D // 2 :]
    wait_all(copies[0])
    hidden_mid = hidden[...].astype(F32) + dot_nn(attended, store[0]) + vec[4:5]
    mid[...] = hidden_mid
    normed, _ = norm_parts(hidden_mid)
    mlp_in[...] = (normed * vec[5:6] + vec[6:7]).astype(BF16)


def gelu_and_slope(value):
    square = value * value
    tanh = jnp.tanh(value * (ROOT_TWO_OVER_PI + (ROOT_TWO_OVER_PI * CUBE) * square))
    half = 0.5 + 0.5 * tanh
    rise = value * (ROOT_TWO_OVER_PI + (3.0 * ROOT_TWO_OVER_PI * CUBE) * square)
    return value * half, half * (1.0 + (1.0 - tanh) * rise)


def row_sum(value):
    return dot_nn(jnp.ones((8, value.shape[0]), BF16), value)[:1]


def split_copies(store, first, second, chunk, chunks, sem):
    at = chunk * WIDE
    half = chunks // 2 * WIDE
    target, spot = (first, at) if at < half else (second, at - half)
    return pltpu.make_async_copy(store.at[:, pl.ds(at, WIDE)], target.at[:, pl.ds(spot, WIDE)], sem)


def mlp_kernel(sizes, plan, chunk_ids, info, mid, mlp_in, vec, up_bias, *refs):
    count_a, count_b = sizes
    path_a, path_b, outs, scratch = split_refs(refs, [count_a, count_b, 5, 6])
    hidden, hidden_low, slopes, act_own, act_other = outs
    store, sems, slope_store, act_store, slope_sems, act_sems = scratch
    copies = mlp_copies((path_a, path_b), plan, store, sems)
    for pair in copies[:AHEAD]:
        start_all(pair[0])
        start_all(pair[1])
    total = mid[...] + vec[7:8]
    given = mlp_in[...]
    chunks = len(plan)
    sent = []
    for chunk in range(chunks):
        at = slice(chunk * WIDE, (chunk + 1) * WIDE)
        bias = [
            up_bias[pl.ds(info[0] ^ i, 1)].reshape(1, CHUNK)
            for i in chunk_ids[2 * chunk : 2 * chunk + 2]
        ]
        wait_all(copies[chunk][0])
        for pair in copies[chunk + AHEAD : chunk + AHEAD + 1]:
            start_all(pair[0])
            start_all(pair[1])
        value, slope = gelu_and_slope(dot_nt(given, store[0, at]) + jnp.concatenate(bias, 1))
        active = value.astype(BF16)
        slope_store[:, at] = slope
        act_store[:, at] = active
        span = pl.ds(chunk * WIDE, WIDE)
        out = [
            pltpu.make_async_copy(slope_store.at[:, span], slopes.at[:, span], slope_sems.at[chunk]),
            split_copies(act_store, act_own, act_other, chunk, chunks, act_sems.at[chunk]),
        ]
        start_all(out)
        sent += out
        wait_all(copies[chunk][1])
        total = total + dot_nn(active, store[1, at])
    hidden[...] = total
    hidden_low[...] = total.astype(BF16)
    wait_all(sent)


def head_kernel(info, scale, hidden, tiles, vec, head_bias, head, *outs):
    prediction, head_grad, grad_hidden, sums = outs
    gain = vec[0:1]
    count = hidden.shape[0]
    normed, inverse = norm_parts(hidden[...])
    final_in = (normed * gain + vec[1:2]).astype(BF16)
    low = head[...].astype(BF16)
    out = dot_nn(final_in, low) + head_bias[...]
    lanes = lax.broadcasted_iota(jnp.int32, out.shape, 1)
    last = lanes >= MODEL_NUMBER * TILE_CELLS

    def over(value, join):
        result = value
        for step in range(1, MODEL_NUMBER + 1):
            result = join(result, pltpu.roll(value, step * TILE_CELLS, 1))
        return result

    def add(left, right):
        return left + right

    record = tiles[...]
    logits = jnp.where(last, NEG, out)
    shifted = logits - over(logits, jnp.maximum)
    log_gate = shifted - jnp.log(over(jnp.exp(shifted), add))
    gate = jnp.where(last, 0.0, jnp.exp(log_gate))
    blend = over(gate * record, add)
    estimate = blend + over(jnp.where(last, out, 0.0), add)
    error = estimate - over(jnp.where(last, record, 0.0), add)
    entropy = over(gate * log_gate, add)
    row_ids = info[3] * count + lax.broadcasted_iota(jnp.int32, (count, 1), 0)
    valid = (row_ids < info[1]).astype(F32)
    weight = valid * info[2].astype(F32)
    share = weight * scale[0]
    factor = share * error
    grads = gate * (factor * (record - blend) + PENALTY * share * (log_gate - entropy))
    grads = jnp.where(last, factor, grads).astype(BF16)
    prediction[...] = (estimate * valid)[:, :TILE_CELLS]
    head_rows = dot_tn(final_in, grads)
    for at in range(0, D, 128):
        head_grad[:, at : at + 128] = head_rows[at : at + 128]
    grad_final = dot_nt(grads, low)
    grad_in, gain_grad, bias_grad = norm_back(grad_final, normed, inverse, gain)
    grad_hidden[...] = grad_in
    sums[...] = jnp.zeros_like(sums)
    sums[0:1] = gain_grad[None]
    sums[1:2] = bias_grad[None]
    sums[2:3, :128] = column_sum(grads.astype(F32))
    sums[3:4, :128] = column_sum(jnp.where(lanes < TILE_CELLS, weight * entropy, 0.0))


def mlp_back_kernel(ids, rows, sizes, plan, chunk_ids, info, grad, mid, slopes, vec, *refs):
    groups = [sizes[0], sizes[1], len(ids[0]), len(ids[1]), 8, 8]
    mlp_a, mlp_b, path_a, path_b, outs, scratch = split_refs(refs, groups)
    grad_low, pre_own, pre_other, grad_mid, grad_branch, grad_attended, up_bias_grad, sums = outs
    store, out_store, sems, out_sems, slope_store, pre_store, slope_sems, pre_sems = scratch
    copies = mlp_copies((mlp_a, mlp_b), plan, store, sems)
    chunks = len(plan)
    slope_copies = []
    for chunk, pair in enumerate(copies):
        span = pl.ds(chunk * WIDE, WIDE)
        slope_copies.append(
            pltpu.make_async_copy(slopes.at[:, span], slope_store.at[:, span], slope_sems.at[chunk])
        )
    out_copies = attn_copies((path_a, path_b), ids, rows, info[0], ((1, 1),), out_store, out_sems)
    order = [[*pair[1], slope_copies[chunk], *pair[0]] for chunk, pair in enumerate(copies)]
    order[-1] += out_copies[0]
    for group in order[:AHEAD]:
        start_all(group)
    upper = grad[...].astype(F32)
    low = upper.astype(BF16)
    grad_low[...] = low
    up_bias_grad[...] = jnp.zeros_like(up_bias_grad)
    total = jnp.zeros(upper.shape, F32)
    sent = []
    for chunk in range(chunks):
        at = slice(chunk * WIDE, (chunk + 1) * WIDE)
        wait_all(copies[chunk][1])
        for group in order[chunk + AHEAD : chunk + AHEAD + 1]:
            start_all(group)
        grad_active = dot_nt(low, store[1, at])
        slope_copies[chunk].wait()
        grad_pre = (grad_active * slope_store[:, at]).astype(BF16)
        pre_store[:, at] = grad_pre
        out = split_copies(pre_store, pre_own, pre_other, chunk, chunks, pre_sems.at[chunk])
        out.start()
        sent.append(out)
        bias_grad = row_sum(grad_pre)
        for which in range(2):
            i = info[0] ^ chunk_ids[2 * chunk + which]
            lanes = pl.ds(pl.multiple_of((i & 1) * CHUNK, CHUNK), CHUNK)
            up_bias_grad[pl.ds(i >> 1, 1), lanes] = bias_grad[:, which * CHUNK : (which + 1) * CHUNK]
        wait_all(copies[chunk][0])
        total = total + dot_nn(grad_pre, store[0, at])
    normed, inverse = norm_parts(mid[...])
    grad_norm, gain_grad, bias_grad = norm_back(total, normed, inverse, vec[5:6])
    grad_sum = upper + grad_norm
    grad_mid[...] = grad_sum
    branch = grad_sum.astype(BF16)
    grad_branch[...] = branch
    sums[...] = jnp.zeros_like(sums)
    sums[0:1] = row_sum(branch)
    sums[1:2] = gain_grad[None]
    sums[2:3] = bias_grad[None]
    sums[3:4] = row_sum(low)
    wait_all(out_copies[0])
    grad_attended[...] = dot_nt(branch, out_store[0]).astype(BF16)
    wait_all(sent)


def attend_back_kernel(info, queries, grad_attended, log_total, *refs):
    pairs, outs = split_refs(refs, [2, 4])
    grad_queries, keep, send_keys, send_values = outs
    count = queries.shape[0]
    total = count * len(pairs)
    valid = valid_row(info[3], info[1], count, total)
    scale = HDIM ** (-0.5)
    for pair in range(HEADS // 2):
        lanes = slice(2 * HDIM * pair, 2 * HDIM * (pair + 1))
        shifted = slice(D + 2 * HDIM * pair, D + 2 * HDIM * (pair + 1))
        query = queries[:, lanes] * jnp.asarray(scale, BF16)
        grad = grad_attended[:, lanes]
        query_t = query.astype(F32).T.astype(BF16)
        grad_t = grad.astype(F32).T.astype(BF16)
        keys = jnp.concatenate([ref[:, lanes] for ref in pairs], 0)
        values = jnp.concatenate([ref[:, shifted] for ref in pairs], 0)
        outs_q, outs_k, outs_v = [], [], []
        for sub in range(2):
            mask = head_mask(sub, count)
            head = 2 * pair + sub
            rows = slice(HDIM * sub, HDIM * (sub + 1))
            zero = jnp.zeros_like(query)
            scores = dot_nt(jnp.where(mask, query, zero), keys)
            scores = jnp.where(valid, scores, NEG)
            probs = jnp.exp(scores - log_total[:, head : head + 1])
            grad_probs = dot_nt(jnp.where(mask, grad, zero), values)
            row_dot = jnp.sum(probs * grad_probs, -1, keepdims=True)
            grad_scores = (probs * (grad_probs - row_dot)).astype(BF16)
            outs_q.append(dot_nn(grad_scores, keys))
            outs_k.append(dot_nn(query_t[rows], grad_scores))
            outs_v.append(dot_nn(grad_t[rows], probs.astype(BF16)))
        grad_queries[:, lanes] = (jnp.where(head_mask(0, count), outs_q[0], outs_q[1]) * scale).astype(BF16)
        for where, outs_t, send in ((lanes, outs_k, send_keys), (shifted, outs_v, send_values)):
            part = jnp.concatenate(outs_t, 0).T.astype(BF16)
            keep[:, where] = part[:count]
            send[:, lanes] = part[count:]


def qkv_back_kernel(ids, rows, info, grad_queries, keep, came_keys, came_values, hidden, grad_mid, vec, *refs):
    groups = [len(ids[0]), len(ids[1]), 4, 2]
    path_a, path_b, outs, (store, sems) = split_refs(refs, groups)
    grad_hidden, hidden_low, grad_pair, sums = outs
    copies = attn_copies((path_a, path_b), ids, rows, info[0], ((0, 0), (0, 1), (1, 0)), store, sems)
    for group in copies:
        start_all(group)
    came = jnp.concatenate([came_keys[...], came_values[...]], 1)
    pair = add_low(keep[...], came)
    grad_pair[...] = pair
    grad_q = grad_queries[...]
    wait_all(copies[0])
    total = dot_nt(grad_q, store[0])
    wait_all(copies[1])
    total = total + dot_nt(pair[:, :D], store[1])
    wait_all(copies[2])
    total = total + dot_nt(pair[:, D:], store[2])
    normed, inverse = norm_parts(hidden[...].astype(F32))
    grad_norm, gain_grad, bias_grad = norm_back(total, normed, inverse, vec[0:1])
    result = grad_mid[...] + grad_norm
    grad_hidden[...] = result
    hidden_low[...] = result.astype(BF16)
    sums[...] = jnp.zeros_like(sums)
    sums[0:1] = gain_grad[None]
    sums[1:2] = bias_grad[None]
    sums[2:3] = row_sum(grad_q)
    sums[3:4] = row_sum(pair[:, D:])
    lead = lax.broadcasted_iota(jnp.int32, (NLEAD, D), 0) == info[2] - 1
    sums[8:] = jnp.where(lead, bias_grad[None], 0.0)


def reversed_bits(value, width):
    return sum(((value >> bit) & 1) << (width - 1 - bit) for bit in range(width))


def place_parts(value, blocks, width, mat, path, start, outs):
    at, rows = blocks
    at = at if path == 0 else reversed_bits(at, width)
    half = 1 << (width - 1)
    keep, send = outs[path]
    ref = keep if at < half else send
    ref[at % half, mat, start : start + rows] = value


def keep_earlier(info, earlier, outs, compute):
    if not earlier:
        compute()
        return
    later = info[4] == 1

    @pl.when(later)
    def _():
        for value, out in zip(earlier, outs):
            out[...] = value[...]

    @pl.when(jnp.logical_not(later))
    def _():
        compute()


def mlp_weight_kernel(width, half_rows, count, info, *refs):
    ins, earlier, outs = split_refs(refs, [8, count, 4])
    keep_earlier(info, earlier, outs, lambda: mlp_weight_body(width, half_rows, ins, outs))


def mlp_weight_body(width, half_rows, ins, outs):
    act, act_far, pre, pre_far, grad, grad_far, given, given_far = ins
    paths = (outs[:2], outs[2:])
    grad_two = jnp.concatenate([grad[...], grad_far[...]], 0)
    given_two = jnp.concatenate([given[...], given_far[...]], 0)
    rows = 2 * half_rows
    for first in range(0, 1 << width, 2):
        lanes = slice(first * rows, (first + 2) * rows)
        for mat, near, far, right in ((0, pre, pre_far, given_two), (1, act, act_far, grad_two)):
            left = jnp.concatenate([near[:, lanes], far[:, lanes]], 0)
            value = dot_tn(left, right).astype(BF16)
            for at in (first, first + 1):
                for path in range(2):
                    start = (at - first) * rows + path * half_rows
                    part = value[start : start + half_rows]
                    place_parts(part, (at, half_rows), width, mat, path, 0, paths)


def attn_weight_kernel(width, rows, count, info, *refs):
    ins, earlier, outs = split_refs(refs, [10, count, 4])
    keep_earlier(info, earlier, outs, lambda: attn_weight_body(width, rows, ins, outs))


def attn_weight_body(width, rows, ins, outs):
    mixed, mixed_far, att, att_far, grad_q, grad_q_far, pair, pair_far, branch, branch_far = ins
    paths = (outs[:2], outs[2:])
    mixed_two = jnp.concatenate([mixed[...], mixed_far[...]], 0)
    att_two = jnp.concatenate([att[...], att_far[...]], 0)
    jobs = (
        (0, 0, mixed_two, jnp.concatenate([grad_q[...], grad_q_far[...]], 0)),
        (0, 1, mixed_two, jnp.concatenate([pair[:, :D], pair_far[:, :D]], 0)),
        (1, 0, mixed_two, jnp.concatenate([pair[:, D:], pair_far[:, D:]], 0)),
        (1, 1, att_two, jnp.concatenate([branch[...], branch_far[...]], 0)),
    )
    for path, mat, left, right in jobs:
        value = dot_tn(left, right).astype(BF16)
        for at in range(1 << width):
            place_parts(value[at * rows : (at + 1) * rows], (at, rows), width, mat, path, 0, paths)


def polynomial_kernel(pieces, rate, *refs):
    mats = len(pieces)
    ins, (master, state, new), scratch = split_refs(refs, [sum(pieces), 3, 5])
    gram, low, mix, cross, moved = scratch
    block = D // 3
    spots = range(0, D, block)

    def square(store, left_of, right_of, finish):
        for spot in spots:
            at, rest = slice(spot, spot + block), slice(spot, D)
            value = finish(at, rest, left_of(at), right_of(rest))
            store[at, rest] = value.astype(store.dtype)
            for other in range(spot + block, D, block):
                part = value[:, other - spot : other - spot + block]
                store[other : other + block, at] = part.T.astype(store.dtype)

    at_piece = 0
    for mat in range(mats):
        mine = ins[at_piece : at_piece + pieces[mat]]
        at_piece += pieces[mat]

        def gram_block(at, rest, left, right):
            total = dot_tn(mine[0][:, at], mine[0][:, rest])
            for ref in mine[1:]:
                total = total + dot_tn(ref[:, at], ref[:, rest])
            return total

        square(gram, lambda at: None, lambda rest: None, gram_block)
        trace = jnp.zeros((), F32)
        for spot in spots:
            at = slice(spot, spot + block)
            hot = lax.broadcasted_iota(jnp.int32, (block, block), 0) == lax.broadcasted_iota(
                jnp.int32, (block, block), 1
            )
            trace = trace + jnp.sum(jnp.where(hot, gram[at, at], 0.0))
        factor = 1.0 / (jnp.sqrt(trace) + 1e-07)
        scaled = factor * factor
        for spot in spots:
            at = slice(spot, spot + block)
            value = gram[at] * scaled
            gram[at] = value
            low[at] = value.astype(BF16)

        def mixed(at, rest, left, right):
            return COEF_B * gram[at, rest] + COEF_C * dot_nn(left, right)

        def crossed(at, rest, left, right):
            return dot_nn(left, right)

        def moved_gram(at, rest, left, right):
            result = (COEF_A * COEF_A) * gram[at, rest] + (2.0 * COEF_A) * moved[at, rest]
            return result + dot_nn(left, right)

        value = state[mat] * factor
        square(mix, lambda at: low[at], lambda rest: low[:, rest], mixed)
        value = COEF_A * value + dot_nn(value.astype(BF16), mix[...])
        square(moved, lambda at: mix[at], lambda rest: low[:, rest], crossed)
        cross[...] = moved[...].astype(BF16)
        square(low, lambda at: mix[at], lambda rest: cross[:, rest], moved_gram)
        once = dot_nn(value.astype(BF16), low[...])
        twice = dot_nn(once.astype(BF16), low[...])
        value = COEF_A * value + COEF_B * once + COEF_C * twice
        new[mat] = master[mat] * (1.0 - rate[mat] * DECAY) - rate[mat] * value


def swap_dp(value, bit):
    size = lax.axis_size("dp")
    return lax.ppermute(value, "dp", [(i, i ^ (1 << bit)) for i in range(size)])


def swap_rep(value, mask):
    size = lax.axis_size("rep")
    return lax.ppermute(value, "rep", [(i, i ^ mask) for i in range(size)])


def link_bits():
    count = lax.axis_size("dp").bit_length() - 1
    return (list(range(1, count)), list(range(count - 1, 0, -1)))


def path_ids(order):
    ids = [0]
    for bit in order:
        ids = ids + [i | (1 << bit) for i in ids]
    return ids


def call(kernel, ins, outs, scratch=(), specs=None, mib=56, flops=0, moved=0, out_specs=None):
    return list(pl.pallas_call(
        kernel,
        out_shape=tuple(outs),
        in_specs=specs or [VMEM] * len(ins),
        out_specs=tuple(out_specs or [VMEM] * len(outs)),
        scratch_shapes=list(scratch),
        compiler_params=limits(mib),
        cost_estimate=pl.CostEstimate(flops=flops // 64, bytes_accessed=moved // 64, transcendentals=0),
    )(*ins))


def after(value, *others):
    return lax.optimization_barrier((value, others))[0]


def piece_ids(order):
    ids = [0]
    for bit in order[:-1]:
        ids = ids + [i | (1 << bit) for i in ids]
    far = [i | (1 << order[-1]) for i in ids]
    return [ids, far, [i | 1 for i in ids], [i | 1 for i in far]]


def gather_steps(firsts, orders, axis=0):
    nears = firsts
    for step in range(len(orders[0]) - 1):
        arrived = [swap_dp(near, order[step]) for near, order in zip(nears, orders)]
        ties = yield nears
        nears = [
            jnp.concatenate([near, after(value, *ties)], axis)
            for near, value in zip(nears, arrived)
        ]
    arrived = [swap_dp(near, order[-1]) for near, order in zip(nears, orders)]
    others = [swap_dp(near, 0) for near in nears]
    ties = yield nears
    fars = [after(value, *ties) for value in arrived]
    ends = [swap_dp(far, 0) for far in fars]
    yield fars
    yield [list(value) for value in zip(nears, fars, others, ends)]


def natural(pieces, ids):
    me = lax.axis_index("dp")
    flat = [i for group in ids for i in group]
    slot = [0] * len(flat)
    for at, i in enumerate(flat):
        slot[i] = at
    joined = jnp.concatenate(pieces, 0)
    wanted = jnp.asarray(slot, jnp.int32)[jnp.arange(len(flat)) ^ me]
    taken = jnp.take(joined, wanted, axis=0)
    mats, width = taken.shape[1], taken.shape[3]
    return taken.transpose(1, 0, 2, 3).reshape(1, mats, -1, width)


def scatter_steps(parts, orders, join):
    low = lax.axis_index("rep") & 1
    keeps, sends = [parts[0], parts[2]], [parts[1], parts[3]]
    values = keeps
    for step in range(len(orders[0])):
        arrived = [swap_dp(send, order[step]) for send, order in zip(sends, orders)]
        ties = yield values
        values = [add_low(keep, after(value, *ties)) for keep, value in zip(keeps, arrived)]
        half = values[0].shape[0] // 2
        keeps = [value[:half] for value in values]
        sends = [value[half:] for value in values]
    pair = join([value[0] for value in values])
    keep = lax.dynamic_index_in_dim(pair, low, 0, keepdims=False)
    arrived = swap_rep(lax.dynamic_index_in_dim(pair, 1 - low, 0, keepdims=False), 1)
    ties = yield keep
    yield keep.astype(F32) + after(arrived, *ties).astype(F32)


def sum_steps(rows):
    core = lax.axis_index("dp") & 1
    half = rows.shape[0] // 2
    total = lax.dynamic_slice_in_dim(rows, core * half, half, 0)
    arrived = swap_dp(lax.dynamic_slice_in_dim(rows, (1 - core) * half, half, 0), 0)
    for bit in link_bits()[0]:
        ties = yield total
        total = total + after(arrived, *ties)
        arrived = swap_dp(total, bit)
    ties = yield total
    yield total + after(arrived, *ties)


def share_steps(total):
    core = lax.axis_index("dp") & 1
    high = lax.axis_index("rep") >> 1
    arrived = swap_rep(total, 1)
    ties = yield total
    total = total + after(arrived, *ties)
    arrived = swap_rep(total, 2)
    ties = yield total
    other = after(arrived, *ties)
    both = jnp.where(high == 0, jnp.stack([total, other]), jnp.stack([other, total]))
    arrived = swap_dp(both, 0)
    ties = yield both
    other = after(arrived, *ties)
    first = jnp.where(core == 0, both, other)
    second = jnp.where(core == 0, other, both)
    yield first, second


class Steps:
    def __init__(self, steps):
        self.steps = steps
        self.last = next(steps)

    def go(self, *ties):
        self.last = self.steps.send(ties)
        return self.last

    def finish(self, *ties):
        try:
            while True:
                self.go(*ties)
        except StopIteration:
            return self.last


def local(
    features,
    tile_records,
    patch_counts,
    lead_counts,
    attn_master,
    attn_momentum,
    mlp_master,
    mlp_momentum,
    vectors,
    vec_momentum,
    head_master,
    head_momentum,
):
    rep_size = lax.axis_size("rep")
    dp_size = lax.axis_size("dp")
    me = lax.axis_index("dp")
    core = me & 1
    rep = lax.axis_index("rep")
    rep_low = rep & 1
    rep_high = rep >> 1
    quarter_rows = features.shape[0]
    count = 2 * quarter_rows
    attn_rows = attn_master.shape[1]
    mlp_rows = mlp_master.shape[1]
    half_rows = mlp_rows // 2
    links = dp_size // 2
    width = links.bit_length() - 1
    paths = link_bits()
    path_a, path_b = paths
    back_orders = (path_b, path_a)
    direct = attn_rows % 16 == 0 and mlp_rows == CHUNK
    assert LAYERS == 2 and rep_size == 2 * LAYERS

    def frame_moves(upper):
        moves = ([], [])
        for d in range(dp_size):
            for r in range(rep_size):
                to = (d - d % 2 + r // 2) * rep_size + 2 * upper + d % 2
                moves[r % 2].append((d * rep_size + r, to))
        return moves

    def bring(value, upper):
        both = [lax.ppermute(value, ("dp", "rep"), pairs) for pairs in frame_moves(upper)]
        return jnp.concatenate(both, 0)

    def take_back(value, upper):
        parts = [
            lax.ppermute(
                value[at * quarter_rows : (at + 1) * quarter_rows],
                ("dp", "rep"),
                [(to, came) for came, to in pairs],
            )
            for at, pairs in enumerate(frame_moves(upper))
        ]
        return jnp.where(rep_low == 0, parts[0], parts[1])

    def up_layer(value):
        return lax.ppermute(value, "rep", [(0, 2), (1, 3)])

    def down_layer(value):
        return lax.ppermute(value, "rep", [(2, 0), (3, 1)])

    def both_owners(own, near):
        pair = jnp.stack([own, near])
        return [lax.dynamic_index_in_dim(pair, rep_low ^ i, 0, keepdims=False) for i in (0, 1)]

    attn_low = attn_master.astype(BF16)
    attn_near = swap_rep(attn_low, 1)
    features = bring(after(features, attn_near), 0)
    mlp_low = mlp_master[0].astype(BF16)
    mlp_near = swap_rep(mlp_low, 1)

    counts = jnp.concatenate([patch_counts, lead_counts]).reshape(1, 2)
    counts = jnp.concatenate([counts, swap_dp(counts, 0)], 0)
    tile_records = bring(after(tile_records, attn_near), 1)
    frame_count, lead_value = lax.dynamic_index_in_dim(counts, core ^ rep_low, 0, keepdims=False)
    info = jnp.stack(
        [me if direct else 0 * me, frame_count, lead_value, core, rep_high]
    ).astype(jnp.int32)

    position = jnp.arange(D) // attn_rows
    distance = ((position % links) << 1) | (position // links)
    source = ((distance ^ me) * attn_rows + jnp.arange(D) % attn_rows).astype(jnp.int32)[None]
    order = [(at % links) << 1 | at // links for at in range(dp_size)]

    vec_rows = VEC_ROWS * LAYERS + 2
    vec_all = vectors[: vec_rows * D].reshape(vec_rows, D)
    vec = lax.dynamic_slice_in_dim(vec_all, VEC_ROWS * rep_high, VEC_ROWS, 0)
    vec_tail = vec_all[VEC_ROWS * LAYERS :]
    head_bias = vectors[vec_rows * D :].reshape(1, -1)
    chunks = FF // CHUNK
    up_bias = vec[8:12].reshape(chunks, 1, CHUNK)

    ids_a, ids_b = piece_ids(path_a), piece_ids(path_b)
    if direct:
        chunk_ids = order
        found = [
            {i: (piece, at) for piece, group in enumerate(ids) for at, i in enumerate(group)}
            for ids in (ids_a, ids_b)
        ]
        plan = [
            [(path, *found[path][i], 0, half_rows) for i in order[at : at + 2] for path in range(2)]
            for at in range(0, dp_size, 2)
        ]
        attn_ids = (ids_a, ids_b)
        mlp_sizes = (4, 4)
        place_rows = attn_rows
    else:
        chunk_ids = list(range(chunks))
        plan = [[(0, 0, 0, at, WIDE)] for at in range(0, FF, WIDE)]
        attn_ids = ([[0]], [[0]])
        mlp_sizes = (1, 0)
        place_rows = D
    n_attn = sum(len(group) for group in attn_ids)
    n_mlp = sum(mlp_sizes)
    copies_each = sum(len(group) for group in attn_ids[0])
    mlp_copies_all = 2 * sum(len(parts) for parts in plan)
    dma = pltpu.SemaphoreType.DMA
    unit_scratch = [pltpu.VMEM((count, FF), F32), pltpu.VMEM((count, FF), BF16)]
    unit_scratch += [dma((len(plan),)), dma((len(plan),))]
    matrix = D * D
    layer_flops = 2 * count * matrix

    def mlp_rel(first, second):
        if direct:
            return first, second
        whole = jnp.concatenate([first, second], 1).reshape(count, dp_size, mlp_rows)
        whole = jnp.take(whole, jnp.asarray(order, jnp.int32) ^ me, axis=1).reshape(count, FF)
        return whole[:, : FF // 2], whole[:, FF // 2 :]

    def qkv(hidden, *ties):
        own, other, queries, pair = call(
            functools.partial(qkv_kernel, attn_ids, place_rows),
            [after(info, *ties), hidden, vec, source] + attn_pieces,
            [
                shape_of(count, D // 2, dtype=BF16),
                shape_of(count, D // 2, dtype=BF16),
                shape_of(count, D, dtype=BF16),
                shape_of(count, 2 * D, dtype=BF16),
            ],
            [pltpu.VMEM((3, D, D), BF16), dma((3 * copies_each,))],
            [SMEM, VMEM, VMEM, VMEM] + [IN_HBM] * n_attn,
            flops=4 * layer_flops,
            moved=6 * matrix + 4 * count * D * 4,
        )
        return [hidden, own, swap_dp(other, 0), queries, [pair, swap_dp(pair, 0)]]

    def attend(saved):
        outs = call(
            functools.partial(attend_kernel, attn_ids, place_rows),
            [after(info, saved[2]), saved[0], vec, source, saved[3]] + saved[4] + attn_pieces,
            [
                shape_of(count, D // 2, dtype=BF16),
                shape_of(count, D // 2, dtype=BF16),
                shape_of(count, 128),
                shape_of(count, D),
                shape_of(count, D, dtype=BF16),
            ],
            [pltpu.VMEM((1, D, D), BF16), pltpu.VMEM((count, D), BF16), dma((copies_each,))],
            [SMEM, VMEM, VMEM, VMEM] + [VMEM] * 3 + [IN_HBM] * n_attn,
            flops=8 * layer_flops,
            moved=2 * matrix + count * D * 8,
        )
        outs[1] = swap_dp(outs[1], 0)
        return saved + outs

    def feed(saved):
        outs = call(
            functools.partial(mlp_kernel, mlp_sizes, plan, chunk_ids),
            [info, saved[8], saved[9], vec, up_bias] + mlp_pieces,
            [
                shape_of(count, D),
                shape_of(count, D, dtype=BF16),
                shape_of(count, FF),
                shape_of(count, FF // 2, dtype=BF16),
                shape_of(count, FF // 2, dtype=BF16),
            ],
            [pltpu.VMEM((2, FF, D), BF16), dma((mlp_copies_all,))] + unit_scratch,
            [SMEM] + [VMEM] * 4 + [IN_HBM] * n_mlp,
            out_specs=[VMEM] * 2 + [IN_HBM] * 3,
            flops=8 * layer_flops,
            moved=4 * FF * D + count * FF * 6,
        )
        near_act, other_act = mlp_rel(outs[3], outs[4])
        far = [swap_dp(other_act, 0), swap_dp(saved[9], 0)]
        return outs[0], outs[1], saved + [outs[2], near_act] + far

    def mlp_back(saved, grad, *ties):
        outs = call(
            functools.partial(mlp_back_kernel, attn_ids, place_rows, mlp_sizes, plan, chunk_ids),
            [after(info, *ties), grad, saved[8], saved[10], vec] + mlp_pieces + attn_pieces,
            [
                shape_of(count, D, dtype=BF16),
                shape_of(count, FF // 2, dtype=BF16),
                shape_of(count, FF // 2, dtype=BF16),
                shape_of(count, D),
                shape_of(count, D, dtype=BF16),
                shape_of(count, D, dtype=BF16),
                shape_of(8, D),
                shape_of(8, D),
            ],
            [
                pltpu.VMEM((2, FF, D), BF16),
                pltpu.VMEM((1, D, D), BF16),
                dma((mlp_copies_all,)),
                dma((copies_each,)),
            ]
            + unit_scratch,
            [SMEM, VMEM, VMEM, IN_HBM, VMEM] + [IN_HBM] * (n_mlp + n_attn),
            out_specs=[VMEM, IN_HBM, IN_HBM] + [VMEM] * 5,
            flops=9 * layer_flops,
            moved=4 * FF * D + 2 * matrix + count * FF * 6,
        )
        near_pre, other_pre = mlp_rel(outs[1], outs[2])
        outs[1], outs[2] = near_pre, swap_dp(other_pre, 0)
        return outs + [swap_dp(outs[0], 0)]

    def attend_back(saved, grad_attended, *ties):
        grad_queries, keep, send_keys, send_values = call(
            attend_back_kernel,
            [after(info, *ties), saved[3], grad_attended, saved[7]] + saved[4],
            [
                shape_of(count, D, dtype=BF16),
                shape_of(count, 2 * D, dtype=BF16),
                shape_of(count, D, dtype=BF16),
                shape_of(count, D, dtype=BF16),
            ],
            (),
            [SMEM] + [VMEM] * 5,
            flops=20 * layer_flops,
            moved=count * D * 16,
        )
        return grad_queries, [keep, swap_dp(send_keys, 0), swap_dp(send_values, 0)]

    def qkv_back(saved, grad_queries, parts, grad_mid, *ties):
        return call(
            functools.partial(qkv_back_kernel, attn_ids, place_rows),
            [after(info, *ties), grad_queries] + parts + [saved[0], grad_mid, vec] + attn_pieces,
            [
                shape_of(count, D),
                shape_of(count, D, dtype=BF16),
                shape_of(count, 2 * D, dtype=BF16),
                shape_of(8 + NLEAD, D),
            ],
            [pltpu.VMEM((3, D, D), BF16), dma((3 * copies_each,))],
            [SMEM] + [VMEM] * 7 + [IN_HBM] * n_attn,
            flops=3 * layer_flops,
            moved=6 * matrix + count * D * 20,
        )

    flipped = jnp.asarray([reversed_bits(at, width) for at in range(links)], jnp.int32)

    def mlp_weights(saved, back, earlier, *ties):
        ins = [after(saved[11], *ties), saved[12], back[1], back[2]]
        ins += [back[0], back[8], saved[9], saved[13]]
        if direct:
            part = shape_of(links // 2, 2, half_rows, D, dtype=BF16)
            return call(
                functools.partial(mlp_weight_kernel, width, half_rows, len(earlier)),
                [info] + ins + earlier,
                [part] * 4,
                specs=[SMEM] + [VMEM] * (8 + len(earlier)),
                flops=8 * layer_flops,
                moved=4 * FF * D + count * FF * 8,
            )
        lefts = [jnp.concatenate(ins[2:4], 0), jnp.concatenate(ins[:2], 0)]
        rights = [jnp.concatenate(ins[6:], 0), jnp.concatenate(ins[4:6], 0)]
        both = jnp.stack([dot_tn(l, r).astype(BF16) for l, r in zip(lefts, rights)])
        both = both.reshape(2, links, 2, half_rows, D).transpose(2, 1, 0, 3, 4)
        return choose([both[0], jnp.take(both[1], flipped, axis=0)], earlier)

    def choose(paths_of, earlier):
        half = links // 2
        parts = [part for path in paths_of for part in (path[:half], path[half:])]
        if earlier:
            parts = [jnp.where(rep_high == 1, old, new) for old, new in zip(earlier, parts)]
        return parts

    def attn_weights(saved, grad_queries, grad_pair, branch, earlier, *ties):
        ins = [after(saved[1], *ties), saved[2], saved[5], saved[6]]
        for value in (grad_queries, grad_pair, branch):
            ins += [value, swap_dp(value, 0)]
        if direct:
            part = shape_of(links // 2, 2, attn_rows, D, dtype=BF16)
            return call(
                functools.partial(attn_weight_kernel, width, attn_rows, len(earlier)),
                [info] + ins + earlier,
                [part] * 4,
                specs=[SMEM] + [VMEM] * (10 + len(earlier)),
                flops=4 * layer_flops,
                moved=4 * matrix + count * D * 16,
            )
        mixed_two, att_two, q_two, pair_two, branch_two = (
            jnp.concatenate(ins[at : at + 2], 0) for at in (0, 2, 4, 6, 8)
        )
        jobs = [(mixed_two, q_two), (mixed_two, pair_two[:, :D])]
        jobs += [(mixed_two, pair_two[:, D:]), (att_two, branch_two)]
        grads = [dot_tn(l, r).astype(BF16).reshape(links, attn_rows, D) for l, r in jobs]
        second = jnp.take(jnp.stack(grads[2:], 1), flipped, axis=0)
        return choose([jnp.stack(grads[:2], 1), second], earlier)

    def rows_of(qkv_sums, back):
        return jnp.concatenate(
            [qkv_sums, back[7], back[6]], 0
        )

    attn_all = Steps(
        gather_steps([value[None] for value in both_owners(attn_low, attn_near)], paths)
    )
    for bit in path_a:
        counts = jnp.concatenate([counts, swap_dp(counts, bit)], 0)
    pixel_total = (TILE_CELLS * jnp.sum(counts[:, 0] * counts[:, 1])).astype(F32)
    tie = attn_all.go(pixel_total, vec, info, source, up_bias, vec_tail, head_bias, mlp_near)
    both = jnp.stack(both_owners(mlp_low, after(mlp_near, tie)))
    mlp_all = Steps(
        gather_steps([both[None, :, :half_rows], both[None, :, half_rows:]], paths)
    )
    tie = attn_all.go(mlp_all.last, features)
    ends = attn_all.finish(tie)
    if direct:
        attn_pieces = ends[0] + ends[1]
    else:
        attn_pieces = [natural(ends[0], ids_a), natural(ends[1], ids_b)]

    saved_0 = qkv(features, tie)
    tie = mlp_all.go(saved_0[3])
    saved_0 = attend(saved_0)
    tie = mlp_all.go(saved_0[8])
    ends = mlp_all.finish(tie)
    if direct:
        mlp_pieces = ends[0] + ends[1]
    else:
        shape = (1, 2, dp_size, half_rows, D)
        parts = [natural(end, ids).reshape(shape) for end, ids in zip(ends, (ids_a, ids_b))]
        mlp_pieces = [jnp.concatenate(parts, 3).reshape(1, 2, FF, D)]
    _, hidden_low, saved_0 = feed(saved_0)

    hidden_low = up_layer(hidden_low)
    saved_1 = attend(qkv(hidden_low, saved_0[6], saved_0[12], saved_0[13], tile_records))
    hidden, _, saved_1 = feed(saved_1)
    scale = (1.0 / pixel_total).reshape(1)
    prediction, head_grad, grad_hidden, head_sums = call(
        head_kernel,
        [info, scale, hidden, tile_records, vec_tail, head_bias, head_master],
        [shape_of(count, TILE_CELLS), shape_of(128, D), shape_of(count, D), shape_of(8, D)],
        (),
        [SMEM, SMEM] + [VMEM] * 5,
        flops=layer_flops,
        moved=D * 128 * 8 + count * D * 8,
    )
    back_1 = mlp_back(saved_1, grad_hidden, saved_1[6], saved_1[12], saved_1[13])
    head_steps = Steps(sum_steps(jnp.concatenate([head_grad, head_sums], 0)))
    grad_q_1, parts = attend_back(saved_1, back_1[5])
    _, grad_low, grad_pair_1, sums_1 = qkv_back(
        saved_1, grad_q_1, parts, back_1[3], back_1[2], back_1[8]
    )
    grad_low = down_layer(grad_low)
    mlp_grads = mlp_weights(saved_1, back_1, [], grad_pair_1)
    attn_grads = attn_weights(saved_1, grad_q_1, grad_pair_1, back_1[4], [], mlp_grads[0])
    prediction = take_back(prediction, 1)

    tie = head_steps.go(attn_grads[0])
    for _ in path_a:
        tie = head_steps.go(tie)
    back_0 = mlp_back(saved_0, after(grad_low, tie, prediction))
    mlp_grads = mlp_weights(saved_0, back_0, mlp_grads)
    tie = mlp_grads[0]
    mlp_steps = Steps(scatter_steps(mlp_grads, back_orders, lambda parts: jnp.concatenate(parts, 1)))
    grad_q_0, parts = attend_back(saved_0, back_0[5], tie)
    grad_hidden, grad_low, grad_pair_0, sums_0 = qkv_back(saved_0, grad_q_0, parts, back_0[3])
    tie = mlp_steps.go(grad_hidden)
    attn_grads = attn_weights(
        saved_0, grad_q_0, grad_pair_0, back_0[4], attn_grads, tie
    )
    layer_rows = jnp.where(rep_high == 0, rows_of(sums_0, back_0), rows_of(sums_1, back_1))
    sums = Steps(sum_steps(layer_rows))
    tie = attn_grads[0]
    attn_steps = Steps(scatter_steps(attn_grads, back_orders, jnp.stack))
    tie = mlp_steps.go(tie)
    tie = sums.go(tie)
    tie = attn_steps.go(tie)
    mlp_share = mlp_steps.finish(tie)[None]
    mlp_moment = MOMENTUM * mlp_momentum + mlp_share
    mlp_state = mlp_share + MOMENTUM * mlp_moment
    low = mlp_state[0].astype(BF16)
    mlp_all = Steps(gather_steps([low[:half_rows], low[half_rows:]], paths))
    tie = mlp_all.go(mlp_share)
    tie = sums.go(tie)
    tie = attn_steps.go(tie)
    layer_rows = sums.finish(tie)
    sums = Steps(share_steps(jnp.concatenate([head_steps.finish(tie), layer_rows], 0)))
    attn_share = attn_steps.finish(layer_rows)
    attn_moment = MOMENTUM * attn_momentum + attn_share
    attn_state = attn_share + MOMENTUM * attn_moment
    low = attn_state.astype(BF16)
    attn_all = Steps(gather_steps([low[0], low[1]], paths))
    tie = attn_all.go(attn_share)
    tie = mlp_all.go(tie)
    mlp_all = mlp_all.finish(tie)
    tie = sums.go(tie)

    def polynomial(groups, master, state, rate):
        pieces = [piece for group in groups for piece in group]
        sizes = [len(group) for group in groups]
        square = pltpu.VMEM((D, D), F32)
        low = pltpu.VMEM((D, D), BF16)
        rows = sum(piece.shape[0] for piece in pieces)
        return call(
            functools.partial(polynomial_kernel, sizes),
            [rate] + pieces + [master, state],
            [shape_of(*master.shape)],
            [square, low, low, low, square],
            [SMEM] + [VMEM] * (len(pieces) + 2),
            flops=2 * matrix * (rows + 4 * D * len(groups)),
            moved=rows * D * 2,
        )[0]

    attn_rate = jnp.asarray(ATTN_RATES, F32).reshape(2, 2)[rep_low]
    mlp_rate = jnp.asarray(MLP_RATES, F32)[rep_low].reshape(1)
    mlp_new = polynomial([mlp_all[0] + mlp_all[1]], mlp_master, mlp_state, after(mlp_rate, tie))
    features_grad = take_back(after(grad_low, mlp_new), 0).astype(F32)
    tie = attn_all.go(mlp_new)
    attn_all = attn_all.finish(tie)
    tie = sums.go(tie)
    sums = sums.finish(tie)
    attn_new = polynomial(attn_all, attn_master, attn_state, attn_rate)

    head_half = head_grad.shape[0] // 2 + head_sums.shape[0] // 2
    halves = [half[:, head_half:] for half in sums]
    layers = [jnp.concatenate([half[layer] for half in halves], 0) for layer in range(LAYERS)]
    head_rows = jnp.concatenate([half[1, :head_half] for half in sums], 0)

    def layer_of(rows):
        return [rows[:4], rows[16:20], rows[24:28], rows[8:16]]

    head_sum = jnp.concatenate(
        [head_rows[:128, at : at + 128] for at in range(0, D, 128)], 0
    )
    head_sums = head_rows[128:136]
    vec_sum = layer_of(layers[0]) + layer_of(layers[1]) + [head_sums[:2]]
    vec_sum = jnp.concatenate(
        [jnp.concatenate(vec_sum, 0).reshape(-1), head_sums[2, :128]]
    )
    penalty = jnp.sum(head_sums[3, :128]) / pixel_total

    vec_moment = MOMENTUM * vec_momentum + vec_sum
    vec_new = vectors - VEC_RATE * vec_moment
    head_moment = MOMENTUM * head_momentum + head_sum
    head_new = head_master - HEAD_RATE * head_moment
    return (
        prediction,
        features_grad,
        penalty,
        attn_moment,
        attn_new,
        mlp_moment,
        mlp_new,
        vec_moment,
        vec_new,
        head_moment,
        head_new,
    )


def solution(mesh):
    return jax.shard_map(
        local,
        mesh=mesh,
        in_specs=(
            P(("dp", "rep"), None),
            P(("dp", "rep"), None),
            P("dp"),
            P("dp"),
            P("rep", "dp", None),
            P("rep", "dp", None),
            P("rep", "dp", None),
            P("rep", "dp", None),
            P(),
            P(),
            P(),
            P(),
        ),
        out_specs=(
            P(("dp", "rep"), None),
            P(("dp", "rep"), None),
            P(),
            P("rep", "dp", None),
            P("rep", "dp", None),
            P("rep", "dp", None),
            P("rep", "dp", None),
            P(),
            P(),
            P(),
            P(),
        ),
        check_vma=False,
    )
```

```python
import functools

import jax
import jax.numpy as jnp
from jax import lax
from jax.experimental import pallas as pl
from jax.experimental.pallas import tpu as pltpu
from jax.sharding import PartitionSpec as P

D = 768
HEADS = 12
HDIM = 64
FF = 3072
LAYERS = 2
MODEL_NUMBER = 3
TILE_CELLS = 32
NLEAD = 8
NS_STEPS = 2


EPS = 1e-05
NEG = -1e30
MOMENTUM = 0.95
COEF_A = 3.4445
COEF_B = -4.775
COEF_C = 2.0315
PENALTY = 0.5
VEC_RATE = 1000.0
HEAD_RATE = 300.0
DECAY = 0.01
ATTN_RATES = (1.0, 1.0, 1.0, 4.0)
MLP_RATES = (2.0, 1.0)


def norm_parts(hidden):
    centred = hidden - jnp.mean(hidden, -1, keepdims=True)
    variance = jnp.mean(centred * centred, -1, keepdims=True)
    inverse = lax.rsqrt(variance + EPS)
    return (centred * inverse, inverse)


def norm_back(grad_out, normed, inverse, gain):
    scaled = grad_out * gain
    mean_one = jnp.mean(scaled, -1, keepdims=True)
    mean_two = jnp.mean(scaled * normed, -1, keepdims=True)
    grad_in = inverse * (scaled - mean_one - normed * mean_two)
    return (grad_in, jnp.sum(grad_out * normed, 0), jnp.sum(grad_out, 0))


ROOT_TWO_OVER_PI = 0.7978845608028654
CUBE = 0.044715
VEC_ROWS = 20
VMEM = pl.BlockSpec(memory_space=pltpu.VMEM)
SMEM = pl.BlockSpec(memory_space=pltpu.SMEM)
IN_HBM = pl.BlockSpec(memory_space=pltpu.HBM)
BF16 = jnp.bfloat16
F32 = jnp.float32


def shape_of(*dims, dtype=F32):
    return jax.ShapeDtypeStruct(dims, dtype)


def limits(mib):
    return pltpu.CompilerParams(vmem_limit_bytes=mib * 1024 * 1024)


def dot_nn(left, right):
    return jnp.dot(left, right, preferred_element_type=F32)


def dot_nt(left, right):
    return lax.dot_general(left, right, (((1,), (1,)), ((), ())), preferred_element_type=F32)


def dot_tn(left, right):
    return lax.dot_general(left, right, (((0,), (0,)), ((), ())), preferred_element_type=F32)


def column_sum(value):
    return jnp.sum(value, 0, keepdims=True)


def add_low(keep, arrived):
    return (keep.astype(F32) + arrived.astype(F32)).astype(BF16)


def start_all(copies):
    for copy in copies:
        copy.start()


def wait_all(copies):
    for copy in copies:
        copy.wait()


def attn_copies(refs, ids, rows, me, wanted, store, sems):
    result = []
    count = 0
    for place_at, (path, mat) in enumerate(wanted):
        copies = []
        for ref, ref_ids in zip(refs[path], ids[path]):
            for at, i in enumerate(ref_ids):
                first = pl.multiple_of((me ^ i) * rows, rows)
                copies.append(
                    pltpu.make_async_copy(
                        ref.at[at, mat], store.at[place_at, pl.ds(first, rows)], sems.at[count]
                    )
                )
                count += 1
        result.append(copies)
    return result


def mlp_copies(refs, plan, store, sems):
    result = []
    count = 0
    for chunk, parts in enumerate(plan):
        pair = []
        for mat in range(2):
            copies = []
            first = chunk * WIDE
            for path, piece, at, start, rows in parts:
                copies.append(
                    pltpu.make_async_copy(
                        refs[path][piece].at[at, mat, pl.ds(start, rows)],
                        store.at[mat, pl.ds(first, rows)],
                        sems.at[count],
                    )
                )
                first += rows
                count += 1
            pair.append(copies)
        result.append(pair)
    return result


CHUNK = 384
AHEAD = 2
WIDE = 2 * CHUNK


def split_refs(refs, sizes):
    out = []
    at = 0
    for size in sizes:
        out.append(refs[at : at + size])
        at += size
    assert at == len(refs)
    return out


def select_matrix(source):
    rows = lax.broadcasted_iota(jnp.int32, (D, D), 0)
    return (rows == source).astype(F32).astype(BF16)


def qkv_kernel(ids, rows, info, hidden, vec, source, *refs):
    sizes = [len(ids[0]), len(ids[1]), 4, 2]
    path_a, path_b, (own, other, queries, pair), (store, sems) = split_refs(refs, sizes)
    copies = attn_copies((path_a, path_b), ids, rows, info[0], ((0, 0), (0, 1), (1, 0)), store, sems)
    for group in copies:
        start_all(group)
    lead_row = 12 + info[2] - 1
    normed, _ = norm_parts(hidden[...].astype(F32))
    mixed = (normed * vec[0:1] + vec[1:2] + vec[pl.ds(lead_row, 1)]).astype(BF16)
    moved = dot_nn(mixed, select_matrix(source[...])).astype(BF16)
    own[...] = moved[:, : D // 2]
    other[...] = moved[:, D // 2 :]
    wait_all(copies[0])
    queries[...] = (dot_nn(mixed, store[0]) + vec[2:3]).astype(BF16)
    wait_all(copies[1])
    pair[:, :D] = dot_nn(mixed, store[1]).astype(BF16)
    wait_all(copies[2])
    pair[:, D:] = (dot_nn(mixed, store[2]) + vec[3:4]).astype(BF16)


def valid_row(quarter, count, rows, total):
    at = lax.broadcasted_iota(jnp.int32, (1, total), 1)
    block = jnp.zeros((1, total), jnp.int32)
    for step in range(1, total // rows):
        block = block + (at >= step * rows).astype(jnp.int32)
    return ((quarter ^ block) - block) * rows + at < count


def head_mask(sub, rows):
    lanes = lax.broadcasted_iota(jnp.int32, (rows, 2 * HDIM), 1)
    return (lanes < HDIM) if sub == 0 else (lanes >= HDIM)


def attend_kernel(ids, rows, info, hidden, vec, source, queries, *refs):
    sizes = [2, len(ids[0]), len(ids[1]), 5, 3]
    pairs, path_a, path_b, (own, other, log_total, mid, mlp_in), (store, joined, sems) = split_refs(refs, sizes)
    copies = attn_copies((path_a, path_b), ids, rows, info[0], ((1, 1),), store, sems)
    start_all(copies[0])
    count = queries.shape[0]
    total = count * len(pairs)
    valid = valid_row(info[3], info[1], count, total)
    log_total[...] = jnp.zeros_like(log_total)
    for pair in range(HEADS // 2):
        lanes = slice(2 * HDIM * pair, 2 * HDIM * (pair + 1))
        shifted = slice(D + 2 * HDIM * pair, D + 2 * HDIM * (pair + 1))
        query = queries[:, lanes] * jnp.asarray(HDIM ** (-0.5), BF16)
        keys = jnp.concatenate([ref[:, lanes] for ref in pairs], 0)
        values = jnp.concatenate([ref[:, shifted] for ref in pairs], 0)
        outs = []
        for sub in range(2):
            mask = head_mask(sub, count)
            scores = dot_nt(jnp.where(mask, query, jnp.zeros_like(query)), keys)
            scores = jnp.where(valid, scores, NEG)
            top = jnp.max(scores, -1, keepdims=True)
            expo = jnp.exp(scores - top)
            sums = jnp.sum(expo, -1, keepdims=True)
            probs = (expo * (1.0 / sums)).astype(BF16)
            outs.append(dot_nn(probs, values))
            head = 2 * pair + sub
            log_total[:, head : head + 1] = top + jnp.log(sums)
        joined[:, lanes] = jnp.where(head_mask(0, count), outs[0], outs[1]).astype(BF16)
    attended = joined[...]
    moved = dot_nn(attended, select_matrix(source[...])).astype(BF16)
    own[...] = moved[:, : D // 2]
    other[...] = moved[:, D // 2 :]
    wait_all(copies[0])
    hidden_mid = hidden[...].astype(F32) + dot_nn(attended, store[0]) + vec[4:5]
    mid[...] = hidden_mid
    normed, _ = norm_parts(hidden_mid)
    mlp_in[...] = (normed * vec[5:6] + vec[6:7]).astype(BF16)


def gelu_and_slope(value):
    square = value * value
    tanh = jnp.tanh(value * (ROOT_TWO_OVER_PI + (ROOT_TWO_OVER_PI * CUBE) * square))
    half = 0.5 + 0.5 * tanh
    rise = value * (ROOT_TWO_OVER_PI + (3.0 * ROOT_TWO_OVER_PI * CUBE) * square)
    return value * half, half * (1.0 + (1.0 - tanh) * rise)


def row_sum(value):
    return dot_nn(jnp.ones((8, value.shape[0]), BF16), value)[:1]


def split_copies(store, first, second, chunk, chunks, sem):
    at = chunk * WIDE
    half = chunks // 2 * WIDE
    target, spot = (first, at) if at < half else (second, at - half)
    return pltpu.make_async_copy(store.at[:, pl.ds(at, WIDE)], target.at[:, pl.ds(spot, WIDE)], sem)


def mlp_kernel(sizes, plan, chunk_ids, info, mid, mlp_in, vec, up_bias, *refs):
    count_a, count_b = sizes
    path_a, path_b, outs, scratch = split_refs(refs, [count_a, count_b, 5, 6])
    hidden, hidden_low, slopes, act_own, act_other = outs
    store, sems, slope_store, act_store, slope_sems, act_sems = scratch
    copies = mlp_copies((path_a, path_b), plan, store, sems)
    for pair in copies[:AHEAD]:
        start_all(pair[0])
        start_all(pair[1])
    total = mid[...] + vec[7:8]
    given = mlp_in[...]
    chunks = len(plan)
    sent = []
    for chunk in range(chunks):
        at = slice(chunk * WIDE, (chunk + 1) * WIDE)
        bias = [
            up_bias[pl.ds(info[0] ^ i, 1)].reshape(1, CHUNK)
            for i in chunk_ids[2 * chunk : 2 * chunk + 2]
        ]
        wait_all(copies[chunk][0])
        for pair in copies[chunk + AHEAD : chunk + AHEAD + 1]:
            start_all(pair[0])
            start_all(pair[1])
        value, slope = gelu_and_slope(dot_nt(given, store[0, at]) + jnp.concatenate(bias, 1))
        active = value.astype(BF16)
        slope_store[:, at] = slope
        act_store[:, at] = active
        span = pl.ds(chunk * WIDE, WIDE)
        out = [
            pltpu.make_async_copy(slope_store.at[:, span], slopes.at[:, span], slope_sems.at[chunk]),
            split_copies(act_store, act_own, act_other, chunk, chunks, act_sems.at[chunk]),
        ]
        start_all(out)
        sent += out
        wait_all(copies[chunk][1])
        total = total + dot_nn(active, store[1, at])
    hidden[...] = total
    hidden_low[...] = total.astype(BF16)
    wait_all(sent)


def head_kernel(info, scale, hidden, tiles, vec, head_bias, head, *outs):
    prediction, head_grad, grad_hidden, sums = outs
    gain = vec[0:1]
    count = hidden.shape[0]
    normed, inverse = norm_parts(hidden[...])
    final_in = (normed * gain + vec[1:2]).astype(BF16)
    low = head[...].astype(BF16)
    out = dot_nn(final_in, low) + head_bias[...]
    lanes = lax.broadcasted_iota(jnp.int32, out.shape, 1)
    last = lanes >= MODEL_NUMBER * TILE_CELLS

    def over(value, join):
        result = value
        for step in range(1, MODEL_NUMBER + 1):
            result = join(result, pltpu.roll(value, step * TILE_CELLS, 1))
        return result

    def add(left, right):
        return left + right

    record = tiles[...]
    logits = jnp.where(last, NEG, out)
    shifted = logits - over(logits, jnp.maximum)
    log_gate = shifted - jnp.log(over(jnp.exp(shifted), add))
    gate = jnp.where(last, 0.0, jnp.exp(log_gate))
    blend = over(gate * record, add)
    estimate = blend + over(jnp.where(last, out, 0.0), add)
    error = estimate - over(jnp.where(last, record, 0.0), add)
    entropy = over(gate * log_gate, add)
    row_ids = info[3] * count + lax.broadcasted_iota(jnp.int32, (count, 1), 0)
    valid = (row_ids < info[1]).astype(F32)
    weight = valid * info[2].astype(F32)
    share = weight * scale[0]
    factor = share * error
    grads = gate * (factor * (record - blend) + PENALTY * share * (log_gate - entropy))
    grads = jnp.where(last, factor, grads).astype(BF16)
    prediction[...] = (estimate * valid)[:, :TILE_CELLS]
    head_rows = dot_tn(final_in, grads)
    for at in range(0, D, 128):
        head_grad[:, at : at + 128] = head_rows[at : at + 128]
    grad_final = dot_nt(grads, low)
    grad_in, gain_grad, bias_grad = norm_back(grad_final, normed, inverse, gain)
    grad_hidden[...] = grad_in
    sums[...] = jnp.zeros_like(sums)
    sums[0:1] = gain_grad[None]
    sums[1:2] = bias_grad[None]
    sums[2:3, :128] = column_sum(grads.astype(F32))
    sums[3:4, :128] = column_sum(jnp.where(lanes < TILE_CELLS, weight * entropy, 0.0))


def mlp_back_kernel(ids, rows, sizes, plan, chunk_ids, info, grad, mid, slopes, vec, *refs):
    groups = [sizes[0], sizes[1], len(ids[0]), len(ids[1]), 8, 8]
    mlp_a, mlp_b, path_a, path_b, outs, scratch = split_refs(refs, groups)
    grad_low, pre_own, pre_other, grad_mid, grad_branch, grad_attended, up_bias_grad, sums = outs
    store, out_store, sems, out_sems, slope_store, pre_store, slope_sems, pre_sems = scratch
    copies = mlp_copies((mlp_a, mlp_b), plan, store, sems)
    chunks = len(plan)
    slope_copies = []
    for chunk, pair in enumerate(copies):
        span = pl.ds(chunk * WIDE, WIDE)
        slope_copies.append(
            pltpu.make_async_copy(slopes.at[:, span], slope_store.at[:, span], slope_sems.at[chunk])
        )
    out_copies = attn_copies((path_a, path_b), ids, rows, info[0], ((1, 1),), out_store, out_sems)
    order = [[*pair[1], slope_copies[chunk], *pair[0]] for chunk, pair in enumerate(copies)]
    order[-1] += out_copies[0]
    for group in order[:AHEAD]:
        start_all(group)
    upper = grad[...].astype(F32)
    low = upper.astype(BF16)
    grad_low[...] = low
    up_bias_grad[...] = jnp.zeros_like(up_bias_grad)
    total = jnp.zeros(upper.shape, F32)
    sent = []
    for chunk in range(chunks):
        at = slice(chunk * WIDE, (chunk + 1) * WIDE)
        wait_all(copies[chunk][1])
        for group in order[chunk + AHEAD : chunk + AHEAD + 1]:
            start_all(group)
        grad_active = dot_nt(low, store[1, at])
        slope_copies[chunk].wait()
        grad_pre = (grad_active * slope_store[:, at]).astype(BF16)
        pre_store[:, at] = grad_pre
        out = split_copies(pre_store, pre_own, pre_other, chunk, chunks, pre_sems.at[chunk])
        out.start()
        sent.append(out)
        bias_grad = row_sum(grad_pre)
        for which in range(2):
            i = info[0] ^ chunk_ids[2 * chunk + which]
            lanes = pl.ds(pl.multiple_of((i & 1) * CHUNK, CHUNK), CHUNK)
            up_bias_grad[pl.ds(i >> 1, 1), lanes] = bias_grad[:, which * CHUNK : (which + 1) * CHUNK]
        wait_all(copies[chunk][0])
        total = total + dot_nn(grad_pre, store[0, at])
    normed, inverse = norm_parts(mid[...])
    grad_norm, gain_grad, bias_grad = norm_back(total, normed, inverse, vec[5:6])
    grad_sum = upper + grad_norm
    grad_mid[...] = grad_sum
    branch = grad_sum.astype(BF16)
    grad_branch[...] = branch
    sums[...] = jnp.zeros_like(sums)
    sums[0:1] = row_sum(branch)
    sums[1:2] = gain_grad[None]
    sums[2:3] = bias_grad[None]
    sums[3:4] = row_sum(low)
    wait_all(out_copies[0])
    grad_attended[...] = dot_nt(branch, out_store[0]).astype(BF16)
    wait_all(sent)


def attend_back_kernel(info, queries, grad_attended, log_total, *refs):
    pairs, outs = split_refs(refs, [2, 4])
    grad_queries, keep, send_keys, send_values = outs
    count = queries.shape[0]
    total = count * len(pairs)
    valid = valid_row(info[3], info[1], count, total)
    scale = HDIM ** (-0.5)
    for pair in range(HEADS // 2):
        lanes = slice(2 * HDIM * pair, 2 * HDIM * (pair + 1))
        shifted = slice(D + 2 * HDIM * pair, D + 2 * HDIM * (pair + 1))
        query = queries[:, lanes] * jnp.asarray(scale, BF16)
        grad = grad_attended[:, lanes]
        query_t = query.astype(F32).T.astype(BF16)
        grad_t = grad.astype(F32).T.astype(BF16)
        keys = jnp.concatenate([ref[:, lanes] for ref in pairs], 0)
        values = jnp.concatenate([ref[:, shifted] for ref in pairs], 0)
        outs_q, outs_k, outs_v = [], [], []
        for sub in range(2):
            mask = head_mask(sub, count)
            head = 2 * pair + sub
            rows = slice(HDIM * sub, HDIM * (sub + 1))
            zero = jnp.zeros_like(query)
            scores = dot_nt(jnp.where(mask, query, zero), keys)
            scores = jnp.where(valid, scores, NEG)
            probs = jnp.exp(scores - log_total[:, head : head + 1])
            grad_probs = dot_nt(jnp.where(mask, grad, zero), values)
            row_dot = jnp.sum(probs * grad_probs, -1, keepdims=True)
            grad_scores = (probs * (grad_probs - row_dot)).astype(BF16)
            outs_q.append(dot_nn(grad_scores, keys))
            outs_k.append(dot_nn(query_t[rows], grad_scores))
            outs_v.append(dot_nn(grad_t[rows], probs.astype(BF16)))
        grad_queries[:, lanes] = (jnp.where(head_mask(0, count), outs_q[0], outs_q[1]) * scale).astype(BF16)
        for where, outs_t, send in ((lanes, outs_k, send_keys), (shifted, outs_v, send_values)):
            part = jnp.concatenate(outs_t, 0).T.astype(BF16)
            keep[:, where] = part[:count]
            send[:, lanes] = part[count:]


def qkv_back_kernel(ids, rows, info, grad_queries, keep, came_keys, came_values, hidden, grad_mid, vec, *refs):
    groups = [len(ids[0]), len(ids[1]), 4, 2]
    path_a, path_b, outs, (store, sems) = split_refs(refs, groups)
    grad_hidden, hidden_low, grad_pair, sums = outs
    copies = attn_copies((path_a, path_b), ids, rows, info[0], ((0, 0), (0, 1), (1, 0)), store, sems)
    for group in copies:
        start_all(group)
    came = jnp.concatenate([came_keys[...], came_values[...]], 1)
    pair = add_low(keep[...], came)
    grad_pair[...] = pair
    grad_q = grad_queries[...]
    wait_all(copies[0])
    total = dot_nt(grad_q, store[0])
    wait_all(copies[1])
    total = total + dot_nt(pair[:, :D], store[1])
    wait_all(copies[2])
    total = total + dot_nt(pair[:, D:], store[2])
    normed, inverse = norm_parts(hidden[...].astype(F32))
    grad_norm, gain_grad, bias_grad = norm_back(total, normed, inverse, vec[0:1])
    result = grad_mid[...] + grad_norm
    grad_hidden[...] = result
    hidden_low[...] = result.astype(BF16)
    sums[...] = jnp.zeros_like(sums)
    sums[0:1] = gain_grad[None]
    sums[1:2] = bias_grad[None]
    sums[2:3] = row_sum(grad_q)
    sums[3:4] = row_sum(pair[:, D:])
    lead = lax.broadcasted_iota(jnp.int32, (NLEAD, D), 0) == info[2] - 1
    sums[8:] = jnp.where(lead, bias_grad[None], 0.0)


def reversed_bits(value, width):
    return sum(((value >> bit) & 1) << (width - 1 - bit) for bit in range(width))


def place_parts(value, blocks, width, mat, path, start, outs):
    at, rows = blocks
    at = at if path == 0 else reversed_bits(at, width)
    half = 1 << (width - 1)
    keep, send = outs[path]
    ref = keep if at < half else send
    ref[at % half, mat, start : start + rows] = value


def keep_earlier(info, earlier, outs, compute):
    if not earlier:
        compute()
        return
    later = info[4] == 1

    @pl.when(later)
    def _():
        for value, out in zip(earlier, outs):
            out[...] = value[...]

    @pl.when(jnp.logical_not(later))
    def _():
        compute()


def mlp_weight_kernel(width, half_rows, count, info, *refs):
    ins, earlier, outs = split_refs(refs, [8, count, 4])
    keep_earlier(info, earlier, outs, lambda: mlp_weight_body(width, half_rows, ins, outs))


def mlp_weight_body(width, half_rows, ins, outs):
    act, act_far, pre, pre_far, grad, grad_far, given, given_far = ins
    paths = (outs[:2], outs[2:])
    grad_two = jnp.concatenate([grad[...], grad_far[...]], 0)
    given_two = jnp.concatenate([given[...], given_far[...]], 0)
    rows = 2 * half_rows
    for first in range(0, 1 << width, 2):
        lanes = slice(first * rows, (first + 2) * rows)
        for mat, near, far, right in ((0, pre, pre_far, given_two), (1, act, act_far, grad_two)):
            left = jnp.concatenate([near[:, lanes], far[:, lanes]], 0)
            value = dot_tn(left, right).astype(BF16)
            for at in (first, first + 1):
                for path in range(2):
                    start = (at - first) * rows + path * half_rows
                    part = value[start : start + half_rows]
                    place_parts(part, (at, half_rows), width, mat, path, 0, paths)


def attn_weight_kernel(width, rows, count, info, *refs):
    ins, earlier, outs = split_refs(refs, [10, count, 4])
    keep_earlier(info, earlier, outs, lambda: attn_weight_body(width, rows, ins, outs))


def attn_weight_body(width, rows, ins, outs):
    mixed, mixed_far, att, att_far, grad_q, grad_q_far, pair, pair_far, branch, branch_far = ins
    paths = (outs[:2], outs[2:])
    mixed_two = jnp.concatenate([mixed[...], mixed_far[...]], 0)
    att_two = jnp.concatenate([att[...], att_far[...]], 0)
    jobs = (
        (0, 0, mixed_two, jnp.concatenate([grad_q[...], grad_q_far[...]], 0)),
        (0, 1, mixed_two, jnp.concatenate([pair[:, :D], pair_far[:, :D]], 0)),
        (1, 0, mixed_two, jnp.concatenate([pair[:, D:], pair_far[:, D:]], 0)),
        (1, 1, att_two, jnp.concatenate([branch[...], branch_far[...]], 0)),
    )
    for path, mat, left, right in jobs:
        value = dot_tn(left, right).astype(BF16)
        for at in range(1 << width):
            place_parts(value[at * rows : (at + 1) * rows], (at, rows), width, mat, path, 0, paths)


def polynomial_kernel(pieces, rate, *refs):
    mats = len(pieces)
    ins, (master, state, new), scratch = split_refs(refs, [sum(pieces), 3, 5])
    gram, low, mix, cross, moved = scratch
    block = D // 3
    spots = range(0, D, block)

    def square(store, left_of, right_of, finish):
        for spot in spots:
            at, rest = slice(spot, spot + block), slice(spot, D)
            value = finish(at, rest, left_of(at), right_of(rest))
            store[at, rest] = value.astype(store.dtype)
            for other in range(spot + block, D, block):
                part = value[:, other - spot : other - spot + block]
                store[other : other + block, at] = part.T.astype(store.dtype)

    at_piece = 0
    for mat in range(mats):
        mine = ins[at_piece : at_piece + pieces[mat]]
        at_piece += pieces[mat]

        def gram_block(at, rest, left, right):
            total = dot_tn(mine[0][:, at], mine[0][:, rest])
            for ref in mine[1:]:
                total = total + dot_tn(ref[:, at], ref[:, rest])
            return total

        square(gram, lambda at: None, lambda rest: None, gram_block)
        trace = jnp.zeros((), F32)
        for spot in spots:
            at = slice(spot, spot + block)
            hot = lax.broadcasted_iota(jnp.int32, (block, block), 0) == lax.broadcasted_iota(
                jnp.int32, (block, block), 1
            )
            trace = trace + jnp.sum(jnp.where(hot, gram[at, at], 0.0))
        factor = 1.0 / (jnp.sqrt(trace) + 1e-07)
        scaled = factor * factor
        for spot in spots:
            at = slice(spot, spot + block)
            value = gram[at] * scaled
            gram[at] = value
            low[at] = value.astype(BF16)

        def mixed(at, rest, left, right):
            return COEF_B * gram[at, rest] + COEF_C * dot_nn(left, right)

        def crossed(at, rest, left, right):
            return dot_nn(left, right)

        def moved_gram(at, rest, left, right):
            result = (COEF_A * COEF_A) * gram[at, rest] + (2.0 * COEF_A) * moved[at, rest]
            return result + dot_nn(left, right)

        value = state[mat] * factor
        square(mix, lambda at: low[at], lambda rest: low[:, rest], mixed)
        value = COEF_A * value + dot_nn(value.astype(BF16), mix[...])
        square(moved, lambda at: mix[at], lambda rest: low[:, rest], crossed)
        cross[...] = moved[...].astype(BF16)
        square(low, lambda at: mix[at], lambda rest: cross[:, rest], moved_gram)
        once = dot_nn(value.astype(BF16), low[...])
        twice = dot_nn(once.astype(BF16), low[...])
        value = COEF_A * value + COEF_B * once + COEF_C * twice
        new[mat] = master[mat] * (1.0 - rate[mat] * DECAY) - rate[mat] * value


def swap_dp(value, bit):
    size = lax.axis_size("dp")
    return lax.ppermute(value, "dp", [(i, i ^ (1 << bit)) for i in range(size)])


def swap_rep(value, mask):
    size = lax.axis_size("rep")
    return lax.ppermute(value, "rep", [(i, i ^ mask) for i in range(size)])


def link_bits():
    count = lax.axis_size("dp").bit_length() - 1
    return (list(range(1, count)), list(range(count - 1, 0, -1)))


def path_ids(order):
    ids = [0]
    for bit in order:
        ids = ids + [i | (1 << bit) for i in ids]
    return ids


def call(kernel, ins, outs, scratch=(), specs=None, mib=56, flops=0, moved=0, out_specs=None):
    return list(pl.pallas_call(
        kernel,
        out_shape=tuple(outs),
        in_specs=specs or [VMEM] * len(ins),
        out_specs=tuple(out_specs or [VMEM] * len(outs)),
        scratch_shapes=list(scratch),
        compiler_params=limits(mib),
        cost_estimate=pl.CostEstimate(flops=flops // 64, bytes_accessed=moved // 64, transcendentals=0),
    )(*ins))


def after(value, *others):
    return lax.optimization_barrier((value, others))[0]


def piece_ids(order):
    ids = [0]
    for bit in order[:-1]:
        ids = ids + [i | (1 << bit) for i in ids]
    far = [i | (1 << order[-1]) for i in ids]
    return [ids, far, [i | 1 for i in ids], [i | 1 for i in far]]


def gather_steps(firsts, orders, axis=0):
    nears = firsts
    for step in range(len(orders[0]) - 1):
        arrived = [swap_dp(near, order[step]) for near, order in zip(nears, orders)]
        ties = yield nears
        nears = [
            jnp.concatenate([near, after(value, *ties)], axis)
            for near, value in zip(nears, arrived)
        ]
    arrived = [swap_dp(near, order[-1]) for near, order in zip(nears, orders)]
    others = [swap_dp(near, 0) for near in nears]
    ties = yield nears
    fars = [after(value, *ties) for value in arrived]
    ends = [swap_dp(far, 0) for far in fars]
    yield fars
    yield [list(value) for value in zip(nears, fars, others, ends)]


def natural(pieces, ids):
    me = lax.axis_index("dp")
    flat = [i for group in ids for i in group]
    slot = [0] * len(flat)
    for at, i in enumerate(flat):
        slot[i] = at
    joined = jnp.concatenate(pieces, 0)
    wanted = jnp.asarray(slot, jnp.int32)[jnp.arange(len(flat)) ^ me]
    taken = jnp.take(joined, wanted, axis=0)
    mats, width = taken.shape[1], taken.shape[3]
    return taken.transpose(1, 0, 2, 3).reshape(1, mats, -1, width)


def scatter_steps(parts, orders, join):
    low = lax.axis_index("rep") & 1
    keeps, sends = [parts[0], parts[2]], [parts[1], parts[3]]
    values = keeps
    for step in range(len(orders[0])):
        arrived = [swap_dp(send, order[step]) for send, order in zip(sends, orders)]
        ties = yield values
        values = [add_low(keep, after(value, *ties)) for keep, value in zip(keeps, arrived)]
        half = values[0].shape[0] // 2
        keeps = [value[:half] for value in values]
        sends = [value[half:] for value in values]
    pair = join([value[0] for value in values])
    keep = lax.dynamic_index_in_dim(pair, low, 0, keepdims=False)
    arrived = swap_rep(lax.dynamic_index_in_dim(pair, 1 - low, 0, keepdims=False), 1)
    ties = yield keep
    yield keep.astype(F32) + after(arrived, *ties).astype(F32)


def sum_steps(rows):
    core = lax.axis_index("dp") & 1
    half = rows.shape[0] // 2
    total = lax.dynamic_slice_in_dim(rows, core * half, half, 0)
    arrived = swap_dp(lax.dynamic_slice_in_dim(rows, (1 - core) * half, half, 0), 0)
    for bit in link_bits()[0]:
        ties = yield total
        total = total + after(arrived, *ties)
        arrived = swap_dp(total, bit)
    ties = yield total
    yield total + after(arrived, *ties)


def share_steps(total):
    core = lax.axis_index("dp") & 1
    high = lax.axis_index("rep") >> 1
    arrived = swap_rep(total, 1)
    ties = yield total
    total = total + after(arrived, *ties)
    arrived = swap_rep(total, 2)
    ties = yield total
    other = after(arrived, *ties)
    both = jnp.where(high == 0, jnp.stack([total, other]), jnp.stack([other, total]))
    arrived = swap_dp(both, 0)
    ties = yield both
    other = after(arrived, *ties)
    first = jnp.where(core == 0, both, other)
    second = jnp.where(core == 0, other, both)
    yield first, second


class Steps:
    def __init__(self, steps):
        self.steps = steps
        self.last = next(steps)

    def go(self, *ties):
        self.last = self.steps.send(ties)
        return self.last

    def finish(self, *ties):
        try:
            while True:
                self.go(*ties)
        except StopIteration:
            return self.last


def local(
    features,
    tile_records,
    patch_counts,
    lead_counts,
    attn_master,
    attn_momentum,
    mlp_master,
    mlp_momentum,
    vectors,
    vec_momentum,
    head_master,
    head_momentum,
):
    rep_size = lax.axis_size("rep")
    dp_size = lax.axis_size("dp")
    me = lax.axis_index("dp")
    core = me & 1
    rep = lax.axis_index("rep")
    rep_low = rep & 1
    rep_high = rep >> 1
    quarter_rows = features.shape[0]
    count = 2 * quarter_rows
    attn_rows = attn_master.shape[1]
    mlp_rows = mlp_master.shape[1]
    half_rows = mlp_rows // 2
    links = dp_size // 2
    width = links.bit_length() - 1
    paths = link_bits()
    path_a, path_b = paths
    back_orders = (path_b, path_a)
    direct = attn_rows % 16 == 0 and mlp_rows == CHUNK
    assert LAYERS == 2 and rep_size == 2 * LAYERS

    def frame_moves(upper):
        moves = ([], [])
        for d in range(dp_size):
            for r in range(rep_size):
                to = (d - d % 2 + r // 2) * rep_size + 2 * upper + d % 2
                moves[r % 2].append((d * rep_size + r, to))
        return moves

    def bring(value, upper):
        both = [lax.ppermute(value, ("dp", "rep"), pairs) for pairs in frame_moves(upper)]
        return jnp.concatenate(both, 0)

    def take_back(value, upper):
        parts = [
            lax.ppermute(
                value[at * quarter_rows : (at + 1) * quarter_rows],
                ("dp", "rep"),
                [(to, came) for came, to in pairs],
            )
            for at, pairs in enumerate(frame_moves(upper))
        ]
        return jnp.where(rep_low == 0, parts[0], parts[1])

    def up_layer(value):
        return lax.ppermute(value, "rep", [(0, 2), (1, 3)])

    def down_layer(value):
        return lax.ppermute(value, "rep", [(2, 0), (3, 1)])

    def both_owners(own, near):
        pair = jnp.stack([own, near])
        return [lax.dynamic_index_in_dim(pair, rep_low ^ i, 0, keepdims=False) for i in (0, 1)]

    attn_low = attn_master.astype(BF16)
    attn_near = swap_rep(attn_low, 1)
    features = bring(after(features, attn_near), 0)
    mlp_low = mlp_master[0].astype(BF16)
    mlp_near = swap_rep(mlp_low, 1)

    counts = jnp.concatenate([patch_counts, lead_counts]).reshape(1, 2)
    counts = jnp.concatenate([counts, swap_dp(counts, 0)], 0)
    tile_records = bring(after(tile_records, attn_near), 1)
    frame_count, lead_value = lax.dynamic_index_in_dim(counts, core ^ rep_low, 0, keepdims=False)
    info = jnp.stack(
        [me if direct else 0 * me, frame_count, lead_value, core, rep_high]
    ).astype(jnp.int32)

    position = jnp.arange(D) // attn_rows
    distance = ((position % links) << 1) | (position // links)
    source = ((distance ^ me) * attn_rows + jnp.arange(D) % attn_rows).astype(jnp.int32)[None]
    order = [(at % links) << 1 | at // links for at in range(dp_size)]

    vec_rows = VEC_ROWS * LAYERS + 2
    vec_all = vectors[: vec_rows * D].reshape(vec_rows, D)
    vec = lax.dynamic_slice_in_dim(vec_all, VEC_ROWS * rep_high, VEC_ROWS, 0)
    vec_tail = vec_all[VEC_ROWS * LAYERS :]
    head_bias = vectors[vec_rows * D :].reshape(1, -1)
    chunks = FF // CHUNK
    up_bias = vec[8:12].reshape(chunks, 1, CHUNK)

    ids_a, ids_b = piece_ids(path_a), piece_ids(path_b)
    if direct:
        chunk_ids = order
        found = [
            {i: (piece, at) for piece, group in enumerate(ids) for at, i in enumerate(group)}
            for ids in (ids_a, ids_b)
        ]
        plan = [
            [(path, *found[path][i], 0, half_rows) for i in order[at : at + 2] for path in range(2)]
            for at in range(0, dp_size, 2)
        ]
        attn_ids = (ids_a, ids_b)
        mlp_sizes = (4, 4)
        place_rows = attn_rows
    else:
        chunk_ids = list(range(chunks))
        plan = [[(0, 0, 0, at, WIDE)] for at in range(0, FF, WIDE)]
        attn_ids = ([[0]], [[0]])
        mlp_sizes = (1, 0)
        place_rows = D
    n_attn = sum(len(group) for group in attn_ids)
    n_mlp = sum(mlp_sizes)
    copies_each = sum(len(group) for group in attn_ids[0])
    mlp_copies_all = 2 * sum(len(parts) for parts in plan)
    dma = pltpu.SemaphoreType.DMA
    unit_scratch = [pltpu.VMEM((count, FF), F32), pltpu.VMEM((count, FF), BF16)]
    unit_scratch += [dma((len(plan),)), dma((len(plan),))]
    matrix = D * D
    layer_flops = 2 * count * matrix

    def mlp_rel(first, second):
        if direct:
            return first, second
        whole = jnp.concatenate([first, second], 1).reshape(count, dp_size, mlp_rows)
        whole = jnp.take(whole, jnp.asarray(order, jnp.int32) ^ me, axis=1).reshape(count, FF)
        return whole[:, : FF // 2], whole[:, FF // 2 :]

    def qkv(hidden, *ties):
        own, other, queries, pair = call(
            functools.partial(qkv_kernel, attn_ids, place_rows),
            [after(info, *ties), hidden, vec, source] + attn_pieces,
            [
                shape_of(count, D // 2, dtype=BF16),
                shape_of(count, D // 2, dtype=BF16),
                shape_of(count, D, dtype=BF16),
                shape_of(count, 2 * D, dtype=BF16),
            ],
            [pltpu.VMEM((3, D, D), BF16), dma((3 * copies_each,))],
            [SMEM, VMEM, VMEM, VMEM] + [IN_HBM] * n_attn,
            flops=4 * layer_flops,
            moved=6 * matrix + 4 * count * D * 4,
        )
        return [hidden, own, swap_dp(other, 0), queries, [pair, swap_dp(pair, 0)]]

    def attend(saved):
        outs = call(
            functools.partial(attend_kernel, attn_ids, place_rows),
            [after(info, saved[2]), saved[0], vec, source, saved[3]] + saved[4] + attn_pieces,
            [
                shape_of(count, D // 2, dtype=BF16),
                shape_of(count, D // 2, dtype=BF16),
                shape_of(count, 128),
                shape_of(count, D),
                shape_of(count, D, dtype=BF16),
            ],
            [pltpu.VMEM((1, D, D), BF16), pltpu.VMEM((count, D), BF16), dma((copies_each,))],
            [SMEM, VMEM, VMEM, VMEM] + [VMEM] * 3 + [IN_HBM] * n_attn,
            flops=8 * layer_flops,
            moved=2 * matrix + count * D * 8,
        )
        outs[1] = swap_dp(outs[1], 0)
        return saved + outs

    def feed(saved):
        outs = call(
            functools.partial(mlp_kernel, mlp_sizes, plan, chunk_ids),
            [info, saved[8], saved[9], vec, up_bias] + mlp_pieces,
            [
                shape_of(count, D),
                shape_of(count, D, dtype=BF16),
                shape_of(count, FF),
                shape_of(count, FF // 2, dtype=BF16),
                shape_of(count, FF // 2, dtype=BF16),
            ],
            [pltpu.VMEM((2, FF, D), BF16), dma((mlp_copies_all,))] + unit_scratch,
            [SMEM] + [VMEM] * 4 + [IN_HBM] * n_mlp,
            out_specs=[VMEM] * 2 + [IN_HBM] * 3,
            flops=8 * layer_flops,
            moved=4 * FF * D + count * FF * 6,
        )
        near_act, other_act = mlp_rel(outs[3], outs[4])
        far = [swap_dp(other_act, 0), swap_dp(saved[9], 0)]
        return outs[0], outs[1], saved + [outs[2], near_act] + far

    def mlp_back(saved, grad, *ties):
        outs = call(
            functools.partial(mlp_back_kernel, attn_ids, place_rows, mlp_sizes, plan, chunk_ids),
            [after(info, *ties), grad, saved[8], saved[10], vec] + mlp_pieces + attn_pieces,
            [
                shape_of(count, D, dtype=BF16),
                shape_of(count, FF // 2, dtype=BF16),
                shape_of(count, FF // 2, dtype=BF16),
                shape_of(count, D),
                shape_of(count, D, dtype=BF16),
                shape_of(count, D, dtype=BF16),
                shape_of(8, D),
                shape_of(8, D),
            ],
            [
                pltpu.VMEM((2, FF, D), BF16),
                pltpu.VMEM((1, D, D), BF16),
                dma((mlp_copies_all,)),
                dma((copies_each,)),
            ]
            + unit_scratch,
            [SMEM, VMEM, VMEM, IN_HBM, VMEM] + [IN_HBM] * (n_mlp + n_attn),
            out_specs=[VMEM, IN_HBM, IN_HBM] + [VMEM] * 5,
            flops=9 * layer_flops,
            moved=4 * FF * D + 2 * matrix + count * FF * 6,
        )
        near_pre, other_pre = mlp_rel(outs[1], outs[2])
        outs[1], outs[2] = near_pre, swap_dp(other_pre, 0)
        return outs + [swap_dp(outs[0], 0)]

    def attend_back(saved, grad_attended, *ties):
        grad_queries, keep, send_keys, send_values = call(
            attend_back_kernel,
            [after(info, *ties), saved[3], grad_attended, saved[7]] + saved[4],
            [
                shape_of(count, D, dtype=BF16),
                shape_of(count, 2 * D, dtype=BF16),
                shape_of(count, D, dtype=BF16),
                shape_of(count, D, dtype=BF16),
            ],
            (),
            [SMEM] + [VMEM] * 5,
            flops=20 * layer_flops,
            moved=count * D * 16,
        )
        return grad_queries, [keep, swap_dp(send_keys, 0), swap_dp(send_values, 0)]

    def qkv_back(saved, grad_queries, parts, grad_mid, *ties):
        return call(
            functools.partial(qkv_back_kernel, attn_ids, place_rows),
            [after(info, *ties), grad_queries] + parts + [saved[0], grad_mid, vec] + attn_pieces,
            [
                shape_of(count, D),
                shape_of(count, D, dtype=BF16),
                shape_of(count, 2 * D, dtype=BF16),
                shape_of(8 + NLEAD, D),
            ],
            [pltpu.VMEM((3, D, D), BF16), dma((3 * copies_each,))],
            [SMEM] + [VMEM] * 7 + [IN_HBM] * n_attn,
            flops=3 * layer_flops,
            moved=6 * matrix + count * D * 20,
        )

    flipped = jnp.asarray([reversed_bits(at, width) for at in range(links)], jnp.int32)

    def mlp_weights(saved, back, earlier, *ties):
        ins = [after(saved[11], *ties), saved[12], back[1], back[2]]
        ins += [back[0], back[8], saved[9], saved[13]]
        if direct:
            part = shape_of(links // 2, 2, half_rows, D, dtype=BF16)
            return call(
                functools.partial(mlp_weight_kernel, width, half_rows, len(earlier)),
                [info] + ins + earlier,
                [part] * 4,
                specs=[SMEM] + [VMEM] * (8 + len(earlier)),
                flops=8 * layer_flops,
                moved=4 * FF * D + count * FF * 8,
            )
        lefts = [jnp.concatenate(ins[2:4], 0), jnp.concatenate(ins[:2], 0)]
        rights = [jnp.concatenate(ins[6:], 0), jnp.concatenate(ins[4:6], 0)]
        both = jnp.stack([dot_tn(l, r).astype(BF16) for l, r in zip(lefts, rights)])
        both = both.reshape(2, links, 2, half_rows, D).transpose(2, 1, 0, 3, 4)
        return choose([both[0], jnp.take(both[1], flipped, axis=0)], earlier)

    def choose(paths_of, earlier):
        half = links // 2
        parts = [part for path in paths_of for part in (path[:half], path[half:])]
        if earlier:
            parts = [jnp.where(rep_high == 1, old, new) for old, new in zip(earlier, parts)]
        return parts

    def attn_weights(saved, grad_queries, grad_pair, branch, earlier, *ties):
        ins = [after(saved[1], *ties), saved[2], saved[5], saved[6]]
        for value in (grad_queries, grad_pair, branch):
            ins += [value, swap_dp(value, 0)]
        if direct:
            part = shape_of(links // 2, 2, attn_rows, D, dtype=BF16)
            return call(
                functools.partial(attn_weight_kernel, width, attn_rows, len(earlier)),
                [info] + ins + earlier,
                [part] * 4,
                specs=[SMEM] + [VMEM] * (10 + len(earlier)),
                flops=4 * layer_flops,
                moved=4 * matrix + count * D * 16,
            )
        mixed_two, att_two, q_two, pair_two, branch_two = (
            jnp.concatenate(ins[at : at + 2], 0) for at in (0, 2, 4, 6, 8)
        )
        jobs = [(mixed_two, q_two), (mixed_two, pair_two[:, :D])]
        jobs += [(mixed_two, pair_two[:, D:]), (att_two, branch_two)]
        grads = [dot_tn(l, r).astype(BF16).reshape(links, attn_rows, D) for l, r in jobs]
        second = jnp.take(jnp.stack(grads[2:], 1), flipped, axis=0)
        return choose([jnp.stack(grads[:2], 1), second], earlier)

    def rows_of(qkv_sums, back):
        return jnp.concatenate(
            [qkv_sums, back[7], back[6]], 0
        )

    attn_all = Steps(
        gather_steps([value[None] for value in both_owners(attn_low, attn_near)], paths)
    )
    for bit in path_a:
        counts = jnp.concatenate([counts, swap_dp(counts, bit)], 0)
    pixel_total = (TILE_CELLS * jnp.sum(counts[:, 0] * counts[:, 1])).astype(F32)
    tie = attn_all.go(pixel_total, vec, info, source, up_bias, vec_tail, head_bias, mlp_near)
    both = jnp.stack(both_owners(mlp_low, after(mlp_near, tie)))
    mlp_all = Steps(
        gather_steps([both[None, :, :half_rows], both[None, :, half_rows:]], paths)
    )
    tie = attn_all.go(mlp_all.last, features)
    ends = attn_all.finish(tie)
    if direct:
        attn_pieces = ends[0] + ends[1]
    else:
        attn_pieces = [natural(ends[0], ids_a), natural(ends[1], ids_b)]

    saved_0 = qkv(features, tie)
    tie = mlp_all.go(saved_0[3])
    saved_0 = attend(saved_0)
    tie = mlp_all.go(saved_0[8])
    ends = mlp_all.finish(tie)
    if direct:
        mlp_pieces = ends[0] + ends[1]
    else:
        shape = (1, 2, dp_size, half_rows, D)
        parts = [natural(end, ids).reshape(shape) for end, ids in zip(ends, (ids_a, ids_b))]
        mlp_pieces = [jnp.concatenate(parts, 3).reshape(1, 2, FF, D)]
    _, hidden_low, saved_0 = feed(saved_0)

    hidden_low = up_layer(hidden_low)
    saved_1 = attend(qkv(hidden_low, saved_0[6], saved_0[12], saved_0[13], tile_records))
    hidden, _, saved_1 = feed(saved_1)
    scale = (1.0 / pixel_total).reshape(1)
    prediction, head_grad, grad_hidden, head_sums = call(
        head_kernel,
        [info, scale, hidden, tile_records, vec_tail, head_bias, head_master],
        [shape_of(count, TILE_CELLS), shape_of(128, D), shape_of(count, D), shape_of(8, D)],
        (),
        [SMEM, SMEM] + [VMEM] * 5,
        flops=layer_flops,
        moved=D * 128 * 8 + count * D * 8,
    )
    back_1 = mlp_back(saved_1, grad_hidden, saved_1[6], saved_1[12], saved_1[13])
    head_steps = Steps(sum_steps(jnp.concatenate([head_grad, head_sums], 0)))
    grad_q_1, parts = attend_back(saved_1, back_1[5])
    _, grad_low, grad_pair_1, sums_1 = qkv_back(
        saved_1, grad_q_1, parts, back_1[3], back_1[2], back_1[8]
    )
    grad_low = down_layer(grad_low)
    mlp_grads = mlp_weights(saved_1, back_1, [], grad_pair_1)
    attn_grads = attn_weights(saved_1, grad_q_1, grad_pair_1, back_1[4], [], mlp_grads[0])
    prediction = take_back(prediction, 1)

    tie = head_steps.go(attn_grads[0])
    for _ in path_a:
        tie = head_steps.go(tie)
    back_0 = mlp_back(saved_0, after(grad_low, tie, prediction))
    mlp_grads = mlp_weights(saved_0, back_0, mlp_grads)
    tie = mlp_grads[0]
    mlp_steps = Steps(scatter_steps(mlp_grads, back_orders, lambda parts: jnp.concatenate(parts, 1)))
    grad_q_0, parts = attend_back(saved_0, back_0[5], tie)
    grad_hidden, grad_low, grad_pair_0, sums_0 = qkv_back(saved_0, grad_q_0, parts, back_0[3])
    tie = mlp_steps.go(grad_hidden)
    attn_grads = attn_weights(
        saved_0, grad_q_0, grad_pair_0, back_0[4], attn_grads, tie
    )
    layer_rows = jnp.where(rep_high == 0, rows_of(sums_0, back_0), rows_of(sums_1, back_1))
    sums = Steps(sum_steps(layer_rows))
    tie = attn_grads[0]
    attn_steps = Steps(scatter_steps(attn_grads, back_orders, jnp.stack))
    tie = mlp_steps.go(tie)
    tie = sums.go(tie)
    tie = attn_steps.go(tie)
    mlp_share = mlp_steps.finish(tie)[None]
    mlp_moment = MOMENTUM * mlp_momentum + mlp_share
    mlp_state = mlp_share + MOMENTUM * mlp_moment
    low = mlp_state[0].astype(BF16)
    mlp_all = Steps(gather_steps([low[:half_rows], low[half_rows:]], paths))
    tie = mlp_all.go(mlp_share)
    tie = sums.go(tie)
    tie = attn_steps.go(tie)
    layer_rows = sums.finish(tie)
    sums = Steps(share_steps(jnp.concatenate([head_steps.finish(tie), layer_rows], 0)))
    attn_share = attn_steps.finish(layer_rows)
    attn_moment = MOMENTUM * attn_momentum + attn_share
    attn_state = attn_share + MOMENTUM * attn_moment
    low = attn_state.astype(BF16)
    attn_all = Steps(gather_steps([low[0], low[1]], paths))
    tie = attn_all.go(attn_share)
    tie = mlp_all.go(tie)
    mlp_all = mlp_all.finish(tie)

    def polynomial(groups, master, state, rate):
        pieces = [piece for group in groups for piece in group]
        sizes = [len(group) for group in groups]
        square = pltpu.VMEM((D, D), F32)
        low = pltpu.VMEM((D, D), BF16)
        rows = sum(piece.shape[0] for piece in pieces)
        return call(
            functools.partial(polynomial_kernel, sizes),
            [rate] + pieces + [master, state],
            [shape_of(*master.shape)],
            [square, low, low, low, square],
            [SMEM] + [VMEM] * (len(pieces) + 2),
            flops=2 * matrix * (rows + 4 * D * len(groups)),
            moved=rows * D * 2,
        )[0]

    attn_rate = jnp.asarray(ATTN_RATES, F32).reshape(2, 2)[rep_low]
    mlp_rate = jnp.asarray(MLP_RATES, F32)[rep_low].reshape(1)
    mlp_new = polynomial([mlp_all[0] + mlp_all[1]], mlp_master, mlp_state, after(mlp_rate, tie))
    features_grad = take_back(after(grad_low, mlp_new), 0).astype(F32)
    tie = sums.go(mlp_new)
    tie = attn_all.go(tie)
    attn_all = attn_all.finish(tie)
    attn_new = polynomial(attn_all, attn_master, attn_state, attn_rate)
    tie = sums.go(attn_new)
    sums = sums.finish(tie)

    head_half = head_grad.shape[0] // 2 + head_sums.shape[0] // 2
    halves = [half[:, head_half:] for half in sums]
    layers = [jnp.concatenate([half[layer] for half in halves], 0) for layer in range(LAYERS)]
    head_rows = jnp.concatenate([half[1, :head_half] for half in sums], 0)

    def layer_of(rows):
        return [rows[:4], rows[16:20], rows[24:28], rows[8:16]]

    head_sum = jnp.concatenate(
        [head_rows[:128, at : at + 128] for at in range(0, D, 128)], 0
    )
    head_sums = head_rows[128:136]
    vec_sum = layer_of(layers[0]) + layer_of(layers[1]) + [head_sums[:2]]
    vec_sum = jnp.concatenate(
        [jnp.concatenate(vec_sum, 0).reshape(-1), head_sums[2, :128]]
    )
    penalty = jnp.sum(head_sums[3, :128]) / pixel_total

    vec_moment = MOMENTUM * vec_momentum + vec_sum
    vec_new = vectors - VEC_RATE * vec_moment
    head_moment = MOMENTUM * head_momentum + head_sum
    head_new = head_master - HEAD_RATE * head_moment
    return (
        prediction,
        features_grad,
        penalty,
        attn_moment,
        attn_new,
        mlp_moment,
        mlp_new,
        vec_moment,
        vec_new,
        head_moment,
        head_new,
    )


def solution(mesh):
    return jax.shard_map(
        local,
        mesh=mesh,
        in_specs=(
            P(("dp", "rep"), None),
            P(("dp", "rep"), None),
            P("dp"),
            P("dp"),
            P("rep", "dp", None),
            P("rep", "dp", None),
            P("rep", "dp", None),
            P("rep", "dp", None),
            P(),
            P(),
            P(),
            P(),
        ),
        out_specs=(
            P(("dp", "rep"), None),
            P(("dp", "rep"), None),
            P(),
            P("rep", "dp", None),
            P("rep", "dp", None),
            P("rep", "dp", None),
            P("rep", "dp", None),
            P(),
            P(),
            P(),
            P(),
        ),
        check_vma=False,
    )
```
